128 devices in a mesh: shard: 4 (over x), context: 4 (over z), tensor: 8 (over y, core).
Axes of the slice: x: 4, y: 4, z: 4, core: 2. Of those that a mesh axis runs over, the one named last changes fastest.
Arguments:
- hidden: bfloat16 [32768, 768], P(('shard', 'context')), may hold values from -6 to 6
- cotangent: bfloat16 [32768, 768], P(('shard', 'context')), may hold values from -6 to 6
- lengths: int32 [4, 4], P('shard'), may hold values from 1 to 8189, as said below
- norm_gain: float32 [768], replicated, may hold values from 0.5 to 1.5
- gate_proj: bfloat16 [768, 1536], P(('shard', 'context'), 'tensor'), may hold values from -0.21875 to 0.21875
- value_proj: bfloat16 [768, 1536], P(('shard', 'context'), 'tensor'), may hold values from -0.21875 to 0.21875
- state_proj: bfloat16 [768, 256], P(('shard', 'context'), 'tensor'), may hold values from -0.21875 to 0.21875
- step_proj: bfloat16 [768, 24], P(('shard', 'context'), 'tensor'), may hold values from -0.21875 to 0.21875
- conv_value: float32 [4, 1536], P(None, 'tensor'), may hold values from -0.5 to 0.5
- conv_state: float32 [4, 256], P(None, 'tensor'), may hold values from -0.5 to 0.5
- value_bias: float32 [1536], P('tensor'), may hold values from -0.5 to 0.5
- state_bias: float32 [256], P('tensor'), may hold values from -0.5 to 0.5
- step_bias: float32 [24], P('tensor'), may hold values from -3 to -1
- decay_log: float32 [24], P('tensor'), may hold values from -10 to -1
- skip_gain: float32 [24], P('tensor'), may hold values from 0.5 to 3
- mixer_gain: float32 [1536], P('tensor'), may hold values from 0.5 to 1.5
- out_proj: bfloat16 [1536, 768], P('tensor', ('shard', 'context')), may hold values from -0.15625 to 0.15625
Outputs:
- output: bfloat16 [32768, 768], P(('shard', 'context'))
- grad_hidden: bfloat16 [32768, 768], P(('shard', 'context'))
- grad_norm_gain: float32 [768], replicated
- grad_gate_proj: float32 [768, 1536], P(('shard', 'context'), 'tensor')
- grad_value_proj: float32 [768, 1536], P(('shard', 'context'), 'tensor')
- grad_state_proj: float32 [768, 256], P(('shard', 'context'), 'tensor')
- grad_step_proj: float32 [768, 24], P(('shard', 'context'), 'tensor')
- grad_conv_value: float32 [4, 1536], P(None, 'tensor')
- grad_conv_state: float32 [4, 256], P(None, 'tensor')
- grad_value_bias: float32 [1536], P('tensor')
- grad_state_bias: float32 [256], P('tensor')
- grad_step_bias: float32 [24], P('tensor')
- grad_decay_log: float32 [24], P('tensor')
- grad_skip_gain: float32 [24], P('tensor')
- grad_mixer_gain: float32 [1536], P('tensor')
- grad_out_proj: float32 [1536, 768], P('tensor', ('shard', 'context'))
The draws below stay inside these ranges and needn't reach their ends.
Inputs may be any that keep to these rules, and one draw needn't show every extreme that they name: Row g lists the lengths of the 4 sequences of group g in order; each row sums to 8192, and one sequence of each row starts among its first 2048 tokens and ends among its last 2048.
All inputs are finite; a program needn't handle non-finite values.
Results may differ from the reference program's by a relative error of at most 0.017.
Values may be sent and summed in bfloat16 or wider, within the bound.
No kernel may reach another device: no remote copies, remote signals or barrier semaphores. Data moves between devices by JAX's collectives and lax.ppermute only.
A program may use at most 128 MiB of HBM per device.

```python
import jax
import jax.numpy as jnp
from jax import lax

MODEL = 768
INNER = 1536
HEADS = 24
HEADDIM = 64
STATE = 128
CONV = 4
BLOCK = 256
TOK_DEV = 2048
SEQS = 4
GROUP = 8192
TOKENS = 32768
N_SHARD = 4


def draw_lengths(key, part):
    key = jax.random.fold_in(key, 7)
    keys = jax.random.split(key, 3)
    shorts = jax.random.randint(keys[0], (N_SHARD, SEQS - 1), 1, TOK_DEV // SEQS + 1)
    forced = jax.random.randint(keys[1], (), 0, N_SHARD)
    group_rows = jnp.arange(N_SHARD, dtype=jnp.int32)
    shorts = jnp.where((group_rows == forced)[:, None], 1, shorts)
    longest = GROUP - jnp.sum(shorts, axis=1)
    where_long = jax.random.randint(keys[2], (N_SHARD,), 0, SEQS)
    slots = jnp.arange(SEQS, dtype=jnp.int32)[None, :]
    zero_column = jnp.zeros((N_SHARD, 1), jnp.int32)
    left_side = jnp.concatenate([shorts, zero_column], axis=1)
    right_side = jnp.concatenate([zero_column, shorts], axis=1)
    result = jnp.where(slots < where_long[:, None], left_side, jnp.where(slots == where_long[:, None], longest[:, None], right_side))
    return result.astype(jnp.int32)


def draw_decay_log(key, part):
    key = jax.random.fold_in(key, 11)
    keys = jax.random.split(key, 1)
    values = jax.random.uniform(keys[0], (HEADS,), jnp.float32, -10.0, -1.0)
    return values.astype(jnp.float32)


def level_of(key, dims, cuts, least, high):
    level, own = 1.0, jax.random.fold_in(key, 6)
    for axis_at, shards_of in cuts:
        heights = jnp.exp(jax.random.uniform(jax.random.fold_in(own, axis_at), (shards_of,), jnp.float32, least / len(cuts), high / len(cuts)))
        level = level * jnp.repeat(heights, dims[axis_at] // shards_of).reshape([-1 if axis == axis_at else 1 for axis in range(len(dims))])
    return level


def normal_values(key, shape, scale, most, cuts=(), held_as=jnp.bfloat16):
    factor_of = level_of(key, shape, cuts, -0.22, 0.18) if cuts else 1.0
    drawn = jax.random.normal(key, shape, jnp.float32) * scale * factor_of
    return jnp.minimum(jnp.maximum(drawn, -most), most).astype(held_as)


def setup_inputs(seed: int = 0) -> dict:
    arg_keys = jax.random.split(jax.random.key(seed), 18)
    hidden = normal_values(arg_keys[0], (TOKENS, MODEL), 1.0, 6.0, ((0, 16),))
    cotangent = normal_values(arg_keys[1], (TOKENS, MODEL), 1.0, 6.0, ((0, 16),))
    lengths = draw_lengths(jax.random.fold_in(arg_keys[17], 71), 0)
    norm_gain = jnp.clip(1.0 + 0.1 * jax.random.normal(arg_keys[3], (MODEL,), jnp.float32), 0.5, 1.5)
    gate_proj = normal_values(arg_keys[4], (MODEL, INNER), MODEL ** -0.5, 0.21875, ((0, 16), (1, 8)))
    value_proj = normal_values(arg_keys[5], (MODEL, INNER), MODEL ** -0.5, 0.21875, ((0, 16), (1, 8)))
    state_proj = normal_values(arg_keys[6], (MODEL, 2 * STATE), MODEL ** -0.5, 0.21875, ((0, 16), (1, 8)))
    step_proj = normal_values(arg_keys[7], (MODEL, HEADS), MODEL ** -0.5, 0.21875, ((0, 16), (1, 8)))
    conv_value = jnp.clip(jax.random.uniform(arg_keys[8], (CONV, INNER), jnp.float32, -0.5, 0.5) * level_of(arg_keys[8], (CONV, INNER), ((1, 8),), -0.4, 0.0), -0.5, 0.5)
    conv_state = jnp.clip(jax.random.uniform(arg_keys[9], (CONV, 2 * STATE), jnp.float32, -0.5, 0.5) * level_of(arg_keys[9], (CONV, 2 * STATE), ((1, 8),), -0.4, 0.0), -0.5, 0.5)
    value_bias = jnp.clip(jax.random.uniform(arg_keys[10], (INNER,), jnp.float32, -0.5, 0.5) * level_of(arg_keys[10], (INNER,), ((0, 8),), -0.4, 0.0), -0.5, 0.5)
    state_bias = jnp.clip(jax.random.uniform(arg_keys[11], (2 * STATE,), jnp.float32, -0.5, 0.5) * level_of(arg_keys[11], (2 * STATE,), ((0, 8),), -0.4, 0.0), -0.5, 0.5)
    step_bias = jnp.clip(-3.0 + 2.0 * jax.random.uniform(arg_keys[12], (HEADS,), jnp.float32) ** level_of(arg_keys[12], (HEADS,), ((0, 8),), -0.2, 0.2), -3.0, -1.0)
    decay_log = draw_decay_log(jax.random.fold_in(arg_keys[17], 71), 0)
    skip_gain = jnp.clip(0.5 + 2.5 * jax.random.uniform(arg_keys[14], (HEADS,), jnp.float32) ** level_of(arg_keys[14], (HEADS,), ((0, 8),), -0.2, 0.2), 0.5, 3.0)
    mixer_gain = jnp.clip(1.0 + 0.1 * jax.random.normal(arg_keys[15], (INNER,), jnp.float32), 0.5, 1.5)
    out_proj = normal_values(arg_keys[16], (INNER, MODEL), INNER ** -0.5, 0.15625, ((0, 8), (1, 16)))
    return dict(hidden=hidden, cotangent=cotangent, lengths=lengths, norm_gain=norm_gain, gate_proj=gate_proj, value_proj=value_proj, state_proj=state_proj, step_proj=step_proj, conv_value=conv_value, conv_state=conv_state, value_bias=value_bias, state_bias=state_bias, step_bias=step_bias, decay_log=decay_log, skip_gain=skip_gain, mixer_gain=mixer_gain, out_proj=out_proj)


@jax.custom_vjp
def low(v):
    return lax.optimization_barrier(v.astype(jnp.bfloat16)).astype(jnp.float32)

@jax.custom_vjp
def low_back(v):
    return v

def low_keep(v):
    return (low(v), None)

def low_pass(kept, grad):
    return (grad,)

def back_keep(v):
    return (v, None)

def back_low(kept, grad):
    return (low(grad),)
low.defvjp(low_keep, low_pass)
low_back.defvjp(back_keep, back_low)
HIGH = lax.Precision.HIGHEST
EPSILON = 1e-05

def segment_marks(lengths):
    finishes = jnp.cumsum(lengths, axis=1)
    starts = finishes - lengths
    places = jnp.arange(GROUP, dtype=jnp.int32)
    local_seg = lax.optimization_barrier(jnp.sum((places[None, :, None] >= finishes[:, None, :]).astype(jnp.int32), axis=2))
    opening = lax.optimization_barrier(jnp.sum((places[None, :, None] == starts[:, None, :]).astype(jnp.int32), axis=2))
    offsets = jnp.arange(N_SHARD, dtype=jnp.int32)[:, None] * SEQS
    return ((local_seg + offsets).reshape(TOKENS), opening.reshape(TOKENS))

def conv_causal(inputs, conv_taps, biases, segment):
    summed = biases[None, :] + conv_taps[CONV - 1][None, :] * inputs
    for lag_steps in range(1, CONV):
        earlier = jnp.concatenate([jnp.zeros((lag_steps, inputs.shape[1]), jnp.float32), inputs[:-lag_steps]], axis=0)
        earlier_seg = jnp.concatenate([jnp.full((lag_steps,), -1, jnp.int32), segment[:-lag_steps]])
        same_seq = (earlier_seg == segment).astype(jnp.float32)[:, None]
        summed = summed + conv_taps[CONV - 1 - lag_steps][None, :] * earlier * same_seq
    return summed

def ssd_block(state, pieces):
    head_x, timestep, log_decay, b_matrix, c_matrix, segment, opening = pieces
    cumulative = jnp.cumsum(log_decay, axis=0)
    positions = jnp.arange(BLOCK, dtype=jnp.int32)
    allowed = (segment[:, None] == segment[None, :]) & (positions[None, :] <= positions[:, None])
    spread = cumulative[:, None, :] - cumulative[None, :, :]
    decays = jnp.where(allowed[:, :, None], jnp.exp(jnp.where(allowed[:, :, None], spread, 0.0)), 0.0)
    scores = jnp.dot(c_matrix, b_matrix.T, precision=HIGH)
    mixing = low(scores[:, :, None] * decays * timestep[None, :, :])
    intra_out = jnp.einsum('ijh,jhp->ihp', mixing, head_x, precision=HIGH)
    carried = (jnp.cumsum(opening) == 0).astype(jnp.float32)
    lead_decay = jnp.exp(cumulative) * carried[:, None]
    held_state = low(state)
    inter_out = lead_decay[:, :, None] * jnp.einsum('in,hpn->ihp', c_matrix, held_state, precision=HIGH)
    last_same = (segment == segment[-1]).astype(jnp.float32)
    tail_decay = jnp.exp(cumulative[-1][None, :] - cumulative) * last_same[:, None] * timestep
    packed = low(head_x * tail_decay[:, :, None])
    fresh_state = jnp.einsum('jhp,jn->hpn', packed, b_matrix, precision=HIGH)
    new_state = lead_decay[-1][:, None, None] * state + fresh_state
    return (new_state, intra_out + inter_out)

def run_group(start_state, pieces):
    return lax.scan(jax.checkpoint(ssd_block), start_state, pieces)

def forward(residual, norm_gain, gate_proj, value_proj, state_proj, step_proj, conv_value, conv_state, value_bias, state_bias, step_bias, decay_log, skip_gain, mixer_gain, out_proj, segment, opening):
    scaling = lax.rsqrt(lax.optimization_barrier(jnp.mean(residual * residual, axis=1, keepdims=True)) + EPSILON)
    normed = low(residual * scaling * norm_gain[None, :])
    gate_pre = low_back(jnp.dot(normed, gate_proj, precision=HIGH))
    value_pre = low_back(jnp.dot(normed, value_proj, precision=HIGH))
    state_pre = low_back(jnp.dot(normed, state_proj, precision=HIGH))
    step_pre = low_back(jnp.dot(normed, step_proj, precision=HIGH))
    value_in = low(value_pre)
    state_in = low(state_pre)
    x_values = low(jax.nn.silu(conv_causal(value_in, conv_value, value_bias, segment)))
    state_values = low(jax.nn.silu(conv_causal(state_in, conv_state, state_bias, segment)))
    b_matrix = state_values[:, :STATE]
    c_matrix = state_values[:, STATE:]
    timestep = jax.nn.softplus(step_pre + step_bias[None, :])
    rates = -jnp.exp(decay_log)
    log_decay = timestep * rates[None, :]
    head_x = x_values.reshape(TOKENS, HEADS, HEADDIM)
    group_blocks = GROUP // BLOCK

    def split_blocks(array):
        return array.reshape((N_SHARD, group_blocks, BLOCK) + array.shape[1:])
    initial = jnp.zeros((N_SHARD, HEADS, HEADDIM, STATE), jnp.float32)
    unused_state, block_out = jax.vmap(run_group)(initial, (split_blocks(head_x), split_blocks(timestep), split_blocks(log_decay), split_blocks(b_matrix), split_blocks(c_matrix), split_blocks(segment), split_blocks(opening)))
    y_heads = block_out.reshape(TOKENS, HEADS, HEADDIM) + skip_gain[None, :, None] * head_x
    y_rows = y_heads.reshape(TOKENS, INNER)
    gated = y_rows * jax.nn.silu(gate_pre)
    root = lax.rsqrt(lax.optimization_barrier(jnp.mean(gated * gated, axis=1, keepdims=True)) + EPSILON)
    mixed = low(gated * mixer_gain[None, :])
    projected = jnp.dot(mixed, out_proj, precision=HIGH)
    return residual + root * projected

def reference(hidden, cotangent, lengths, norm_gain, gate_proj, value_proj, state_proj, step_proj, conv_value, conv_state, value_bias, state_bias, step_bias, decay_log, skip_gain, mixer_gain, out_proj):
    segment, opening = segment_marks(lengths)
    params = (norm_gain.astype(jnp.float32), gate_proj.astype(jnp.float32), value_proj.astype(jnp.float32), state_proj.astype(jnp.float32), step_proj.astype(jnp.float32), conv_value.astype(jnp.float32), conv_state.astype(jnp.float32), value_bias.astype(jnp.float32), state_bias.astype(jnp.float32), step_bias.astype(jnp.float32), decay_log.astype(jnp.float32), skip_gain.astype(jnp.float32), mixer_gain.astype(jnp.float32), out_proj.astype(jnp.float32))

    def run(residual, *weights):
        return forward(residual, *weights, segment, opening)
    result, pullback = jax.vjp(run, hidden.astype(jnp.float32), *params)
    grads = pullback(cotangent.astype(jnp.float32))
    return (result.astype(jnp.bfloat16), grads[0].astype(jnp.bfloat16), grads[1], grads[2], grads[3], grads[4], grads[5], grads[6], grads[7], grads[8], grads[9], grads[10], grads[11], grads[12], grads[13], grads[14])
```

```python
import jax
import jax.numpy as jnp
from jax import lax
from jax.experimental import pallas as pl
from jax.experimental.pallas import tpu as pltpu
from jax.sharding import PartitionSpec as P

MODEL = 768
INNER = 1536
HEADDIM = 64
STATE = 128
CONV = 4
BLOCK = 256
HEADS_DEV = 3
INNER_DEV = 192
WIDE = 256
CHAN = 512
EPSILON = 1e-05
F32 = jnp.float32
BF16 = jnp.bfloat16
CELLS = ("shard", "context")
VMEM_LIMIT = 60 * 1024 * 1024


def nn(a, b):
    return lax.dot_general(a, b, (((1,), (0,)), ((), ())), preferred_element_type=F32)


def nt(a, b):
    return lax.dot_general(a, b, (((1,), (1,)), ((), ())), preferred_element_type=F32)


def tn(a, b):
    return lax.dot_general(a, b, (((0,), (0,)), ((), ())), preferred_element_type=F32)


def iota(shape, dim):
    return lax.broadcasted_iota(jnp.int32, shape, dim)


def start_of(marks, pos):
    start = jnp.zeros_like(pos)
    for k in range(3):
        start = jnp.where(pos >= marks[k], marks[k], start)
    return start


def end_of(marks, pos):
    end = jnp.full_like(pos, marks[3])
    for k in (2, 1, 0):
        end = jnp.where(pos < marks[k], marks[k], end)
    return end


def running_sum(rows, ones):
    top = rows.astype(BF16)
    rest = rows - top.astype(F32)
    mid = rest.astype(BF16)
    low = (rest - mid.astype(F32)).astype(BF16)
    pieces = [top.astype(F32), mid.astype(F32), low.astype(F32), jnp.zeros((8, BLOCK), F32)]
    sums = nn(jnp.concatenate(pieces, axis=0).astype(BF16), ones)
    return sums[0:8] + sums[8:16] + sums[16:24]


def by_head(cols, width=WIDE):
    lane = iota((1, width), 1)
    return jnp.where(
        lane < HEADDIM,
        cols[0],
        jnp.where(lane < 2 * HEADDIM, cols[1], jnp.where(lane < 3 * HEADDIM, cols[2], 0.0)),
    )


def head_masks():
    row = iota((8, WIDE), 0)
    lane = iota((8, WIDE), 1)
    low = row * HEADDIM
    return jnp.where((lane >= low) & (lane < low + HEADDIM) & (row < HEADS_DEV), 1.0, 0.0)


def of_head(values, h):
    lane = iota((1, WIDE), 1)
    return jnp.where((lane >= h * HEADDIM) & (lane < (h + 1) * HEADDIM), values, 0.0)


def to_columns(rows):
    have = 8 * len(rows)
    stacked = jnp.concatenate(list(rows) + [jnp.zeros((128 - have, BLOCK), F32)], axis=0)
    return stacked.T


def column(cols, part, h):
    at = 8 * part + h
    return cols[:, at : at + 1]


def silu_parts(values):
    sig = 1.0 / (1.0 + jnp.exp(-values))
    return values * sig, sig * (1.0 + values * (1.0 - sig))


class Block:
    def __init__(self, marks, b):
        self.marks = marks
        self.start = marks[4] + b * BLOCK
        self.pos_row = self.start + iota((1, BLOCK), 1)
        self.pos_col = self.start + iota((BLOCK, 1), 0)

    def lead(self, cum):
        carried = start_of(self.marks, self.pos_row) < self.start
        return jnp.where(carried, jnp.exp(cum), 0.0)

    def tail_base(self, cum):
        last = cum[:, BLOCK - 1 : BLOCK]
        kept = end_of(self.marks, self.pos_row) > self.start + BLOCK - 1
        return jnp.where(kept, jnp.exp(last - cum), 0.0)

    def allowed(self):
        first = start_of(self.marks, self.pos_col)
        return (self.pos_row >= first) & (self.pos_row <= self.pos_col)

    def since_start(self):
        return self.pos_col - start_of(self.marks, self.pos_col)

    def until_end(self):
        return end_of(self.marks, self.pos_col) - self.pos_col


def decay_of(allowed, cum_col, cum_row):
    return jnp.exp(jnp.where(allowed, cum_col - cum_row, -1e30))


def last_by_lane(rows):
    return by_head([rows[h : h + 1, BLOCK - 1 : BLOCK] for h in range(HEADS_DEV)])


def call(kernel, grid, in_specs, out_specs, out_shape, scratch, flops, moved, *args):
    return pl.pallas_call(
        kernel,
        grid=(grid,),
        in_specs=in_specs,
        out_specs=out_specs,
        out_shape=out_shape,
        scratch_shapes=scratch,
        compiler_params=pltpu.CompilerParams(
            dimension_semantics=("arbitrary",), vmem_limit_bytes=VMEM_LIMIT
        ),
        cost_estimate=pl.CostEstimate(flops=flops, bytes_accessed=moved, transcendentals=0),
    )(*args)


def shape(dims, dtype=F32):
    return jax.ShapeDtypeStruct(dims, dtype)


SMEM = pl.BlockSpec(memory_space=pltpu.SMEM)


def whole(dims):
    return pl.BlockSpec(dims, lambda s: (0,) * len(dims))


def project_kernel(
    marks, hidden, halo, gain, wv, ws, taps, cbias, hcols, upto,
    normed_o, xbc_o, slope_o, cin_o, cin_halo_o, rows_o, state_o, device_o,
    ext, state, decay,
):
    b = pl.program_id(0)
    blk = Block(marks, b)

    def norm(rows):
        rows = rows.astype(F32)
        scale = lax.rsqrt(jnp.mean(rows * rows, axis=1, keepdims=True) + EPSILON)
        return (rows * scale * gain[...]).astype(BF16)

    @pl.when(b == 0)
    def _():
        ahead = norm(halo[...])
        into = jnp.concatenate([nn(ahead, wv[...]), nn(ahead, ws[...])], axis=1)
        into = into.astype(BF16).astype(F32)
        ext[0:8] = into[8:16]
        cin_halo_o[...] = into[8:16]
        state[...] = jnp.zeros_like(state)
        decay[...] = jnp.ones_like(decay)

    normed = norm(hidden[...])
    normed_o[...] = normed
    value_pre = nn(normed, wv[...])
    state_pre = nn(normed, ws[...])
    cin = jnp.concatenate([value_pre, state_pre], axis=1).astype(BF16)
    cin_o[...] = cin
    ext[8 : 8 + BLOCK] = cin.astype(F32)
    pre = cbias[...] + taps[3:4] * ext[8 : 8 + BLOCK]
    since = blk.since_start()
    for lag in range(1, CONV):
        pre = pre + taps[3 - lag : 4 - lag] * (
            jnp.where(since >= lag, ext[8 - lag : 8 - lag + BLOCK], 0.0)
        )
    ext[0:8] = ext[BLOCK : BLOCK + 8]
    act, slope = silu_parts(pre)
    act = act.astype(BF16)
    xbc_o[...] = act
    slope_o[...] = slope.astype(BF16)

    raw = value_pre[:, 128:256].T[64:72] + hcols[0]
    dt = jnp.maximum(raw, 0.0) + jnp.log1p(jnp.exp(-jnp.abs(raw)))
    sig = 1.0 / (1.0 + jnp.exp(-raw))
    cum = running_sum(dt * hcols[1], upto[...])
    rows_o[0:8] = dt
    rows_o[8:16] = sig
    rows_o[16:24] = cum
    lead = blk.lead(cum)
    tail = blk.tail_base(cum) * dt
    cols = to_columns([tail])
    tail_lanes = by_head([column(cols, 0, h) for h in range(HEADS_DEV)])
    packed = (act[:, :WIDE].astype(F32) * tail_lanes).astype(BF16)
    fresh = tn(act[:, WIDE : WIDE + STATE], packed)
    last = last_by_lane(lead)
    state_o[0, 0:STATE] = state[...]
    state_o[0, STATE : STATE + 8] = decay[...]
    state[...] = last * state[...] + fresh
    decay[...] = last * decay[...]

    @pl.when(b == pl.num_programs(0) - 1)
    def _():
        device_o[0:STATE] = state[...]
        device_o[STATE : STATE + 8] = decay[...]


def intra_kernel(marks, normed, cot, wg, wo_t, xbc, rows, skip, z_o, e_o, yi_o):
    b = pl.program_id(0)
    blk = Block(marks, b)
    z_o[...] = nn(normed[...], wg[...])
    e_o[...] = nn(cot[...], wo_t[...])
    dt = rows[0:8]
    cum = rows[16:24]
    x = xbc[:, :WIDE].astype(F32)
    scores = nt(xbc[:, WIDE + STATE :], xbc[:, WIDE : WIDE + STATE])
    allowed = blk.allowed()
    cols = to_columns([cum])
    out = skip[...] * x
    for h in range(HEADS_DEV):
        decays = decay_of(allowed, column(cols, 0, h), cum[h : h + 1])
        mix = (scores * decays * dt[h : h + 1]).astype(BF16)
        out = out + nn(mix, of_head(x, h).astype(BF16))
    yi_o[...] = out


def gated_kernel(
    marks, yi, z, e, xbc, rows, states, prefix, mgain, wo_t, y_o, mixed_o, part_o, sums_o
):
    b = pl.program_id(0)
    blk = Block(marks, b)
    lead = blk.lead(rows[16:24])
    cols = to_columns([lead])
    lead_lanes = by_head([column(cols, 0, h) for h in range(HEADS_DEV)])
    entering = states[0, 0:STATE] + states[0, STATE : STATE + 1] * prefix[...]
    y = yi[...] + lead_lanes * nn(xbc[:, WIDE + STATE :], entering.astype(BF16))
    y_o[...] = y
    gate, _ = silu_parts(z[...])
    v = y * gate
    mixed = (v * mgain[...]).astype(BF16)
    mixed_o[...] = mixed
    part_o[...] = nt(mixed, wo_t[...]).astype(BF16)
    row = iota((8, 2 * WIDE), 0)
    lane = iota((8, 2 * WIDE), 1)
    pick = jnp.where(((row == 0) & (lane < WIDE)) | ((row == 1) & (lane >= WIDE)), 1.0, 0.0)
    both = jnp.concatenate([v * v, e[...] * mixed.astype(F32)], axis=1)
    sums_o[...] = nt(pick.astype(BF16), both.astype(BF16))


def gate_back_kernel(
    marks, y, z, e, xbc, rows, sums, mgain,
    dy_o, dz_o, reach_o, device_o, gains_o,
    carry, decay,
):
    s = pl.program_id(0)
    b = pl.num_programs(0) - 1 - s
    blk = Block(marks, b)

    @pl.when(s == 0)
    def _():
        carry[...] = jnp.zeros_like(carry)
        decay[...] = jnp.ones_like(decay)
        gains_o[...] = jnp.zeros_like(gains_o)

    lead = blk.lead(rows[16:24])
    root = lax.rsqrt(sums[0:1] / INNER + EPSILON)
    coef = sums[1:2] * root * root * root / INNER
    cols = to_columns([lead, jnp.broadcast_to(root, (8, BLOCK)), jnp.broadcast_to(coef, (8, BLOCK))])
    lead_lanes = by_head([column(cols, 0, h) for h in range(HEADS_DEV)])
    gate, slope = silu_parts(z[...])
    y_v = y[...]
    v = y_v * gate
    dm = column(cols, 1, 0) * e[...]
    dv = mgain[...] * dm - column(cols, 2, 0) * v
    dy = dv * gate
    dy_o[...] = dy
    dz_o[...] = (dv * y_v * slope).astype(BF16)
    x = xbc[:, :WIDE].astype(F32)
    gains_o[0:1] += jnp.sum(v * dm, axis=0, keepdims=True)
    gains_o[1:2] += jnp.sum(dy * x, axis=0, keepdims=True)
    reach = tn(xbc[:, WIDE + STATE :], (dy * lead_lanes).astype(BF16))
    last = last_by_lane(lead)
    reach_o[0, 0:STATE] = carry[...]
    reach_o[0, STATE : STATE + 8] = decay[...]
    carry[...] = last * carry[...] + reach
    decay[...] = last * decay[...]

    @pl.when(b == 0)
    def _():
        device_o[0:STATE] = carry[...]
        device_o[STATE : STATE + 8] = decay[...]


def intra_back_kernel(
    marks, dy_r, xbc, rows, states, prefix, sums, mixed, cot, skip,
    dxi_o, dbc_o, stats_o, grad_out_o,
):
    b = pl.program_id(0)
    blk = Block(marks, b)

    @pl.when(b == 0)
    def _():
        grad_out_o[...] = jnp.zeros_like(grad_out_o)

    dt = rows[0:8]
    cum = rows[16:24]
    lead = blk.lead(cum)
    root = lax.rsqrt(sums[0:1] / INNER + EPSILON)
    cols = to_columns([cum, lead, jnp.broadcast_to(root, (8, BLOCK))])
    lead_lanes = by_head([column(cols, 1, h) for h in range(HEADS_DEV)])
    rooted = (mixed[...].astype(F32) * column(cols, 2, 0)).astype(BF16)
    grad_out_o[...] += tn(cot[...], rooted)

    dy = dy_r[...]
    x_low = xbc[:, :WIDE]
    b_low = xbc[:, WIDE : WIDE + STATE]
    c_low = xbc[:, WIDE + STATE :]
    entering = states[0, 0:STATE] + states[0, STATE : STATE + 1] * prefix[...]
    held = entering.astype(BF16)
    masks = head_masks().astype(BF16)
    cross = nn(c_low, held)
    lead_grad = nt(masks, (dy * cross).astype(BF16))
    dc = nt((dy * lead_lanes).astype(BF16), held)
    scores = nt(c_low, b_low)
    allowed = blk.allowed()
    ds = jnp.zeros((BLOCK, BLOCK), F32)
    dx = skip[...] * dy
    lane = iota((1, 128), 1)
    row8 = iota((8, 1), 0)
    row_sums = jnp.zeros((BLOCK, 128), F32)
    time_grad = jnp.zeros((8, BLOCK), F32)
    for h in range(HEADS_DEV):
        dt_h = dt[h : h + 1]
        dy_h = of_head(dy, h).astype(BF16)
        decays = decay_of(allowed, column(cols, 0, h), cum[h : h + 1])
        weighted = nt(dy_h, x_low) * decays
        ds = ds + weighted * dt_h
        scored = weighted * scores
        time_grad = time_grad + jnp.where(
            row8 == h, jnp.sum(scored, axis=0, keepdims=True), 0.0
        )
        row_sums = row_sums + jnp.where(
            lane == h, jnp.sum(scored * dt_h, axis=1, keepdims=True), 0.0
        )
        mix = (scores * decays * dt_h).astype(BF16)
        dx = dx + tn(mix, dy_h)
    ds_low = ds.astype(BF16)
    dxi_o[...] = dx
    dbc_o[:, 0:STATE] = tn(ds_low, c_low)
    dbc_o[:, STATE : 2 * STATE] = dc + nn(ds_low, b_low)
    stats_o[0:8] = time_grad
    stats_o[8:16] = row_sums.T[0:8] - time_grad * dt + lead_grad * lead


def input_back_kernel(
    marks, hidden, normed, halo, dz, dxi, dbc, xbc, slope, cin, cin_before, cin_halo,
    rows, stats, states, prefix, reaches, suffix, gain, wg, wv, ws, taps, hcols, since,
    dn_o, wgrad_o, chan_o, step_o, norm_o, spill_o,
    ext, ahead,
):
    s = pl.program_id(0)
    b = pl.num_programs(0) - 1 - s
    blk = Block(marks, b)

    @pl.when(s == 0)
    def _():
        wgrad_o[...] = jnp.zeros_like(wgrad_o)
        chan_o[...] = jnp.zeros_like(chan_o)
        step_o[...] = jnp.zeros_like(step_o)
        norm_o[...] = jnp.zeros_like(norm_o)
        ahead[BLOCK : BLOCK + 8] = jnp.zeros((8, CHAN), F32)

    dt = rows[0:8]
    sig = rows[8:16]
    cum = rows[16:24]
    rate = hcols[1]
    lead = blk.lead(cum)
    tail_base = blk.tail_base(cum)
    tail = tail_base * dt
    cols = to_columns([tail])
    tail_lanes = by_head([column(cols, 0, h) for h in range(HEADS_DEV)])
    entering = states[0, 0:STATE] + states[0, STATE : STATE + 1] * prefix[...]
    leaving = reaches[0, 0:STATE] + reaches[0, STATE : STATE + 1] * suffix[...]
    leaving_low = leaving.astype(BF16)
    x = xbc[:, :WIDE].astype(F32)
    dpacked = nn(xbc[:, WIDE : WIDE + STATE], leaving_low)
    packed = (x * tail_lanes).astype(BF16)
    masks = head_masks()
    tail_grad = nt(masks.astype(BF16), (dpacked * x).astype(BF16))
    dx = dxi[...] + dpacked * tail_lanes
    db = dbc[:, 0:STATE] + nt(packed, leaving_low)
    dc = dbc[:, STATE : 2 * STATE]

    tail_term = tail_grad * tail
    state_term = jnp.sum(leaving * entering, axis=0, keepdims=True)
    last_term = jnp.sum(tail_term, axis=1, keepdims=True) + (
        jnp.sum(masks * state_term, axis=1, keepdims=True) * lead[:, BLOCK - 1 : BLOCK]
    )
    dcum = stats[8:16] - tail_term + jnp.where(iota((8, BLOCK), 1) == BLOCK - 1, last_term, 0.0)
    dla = running_sum(dcum, since[...])
    ddt = stats[0:8] + tail_grad * tail_base + dla * rate
    dstep = jnp.where(iota((8, 1), 0) < HEADS_DEV, ddt * sig, 0.0)
    step_o[0:8] += dstep
    step_o[8:16] += dla * dt * rate
    placed = jnp.concatenate(
        [jnp.zeros((64, BLOCK), F32), dstep, jnp.zeros((56, BLOCK), F32)], axis=0
    ).T

    dpre = jnp.concatenate([dx, db, dc], axis=1) * slope[...].astype(F32)
    ext[0:8] = jnp.where(b == 0, cin_halo[...], cin_before[8:16].astype(F32))
    ext[8 : 8 + BLOCK] = cin[...].astype(F32)
    ahead[0:BLOCK] = dpre
    chan_o[4:5] += jnp.sum(dpre, axis=0, keepdims=True)
    chan_o[3:4] += jnp.sum(dpre * ext[8 : 8 + BLOCK], axis=0, keepdims=True)
    din = taps[3:4] * dpre
    reach_back = blk.since_start()
    reach_ahead = blk.until_end()
    for lag in range(1, CONV):
        at = 3 - lag
        chan_o[at : at + 1] += jnp.sum(
            jnp.where(reach_back >= lag, dpre * ext[8 - lag : 8 - lag + BLOCK], 0.0),
            axis=0,
            keepdims=True,
        )
        din = din + taps[at : at + 1] * (
            jnp.where(reach_ahead > lag, ahead[lag : lag + BLOCK], 0.0)
        )
    ahead[BLOCK : BLOCK + 8] = dpre[0:8]

    dz_low = dz[...]
    dv_low = jnp.concatenate([din[:, 0:128], din[:, 128:256] + placed], axis=1).astype(BF16)
    ds_low = din[:, WIDE:].astype(BF16)
    dn = nt(dz_low, wg[...]) + nt(dv_low, wv[...]) + nt(ds_low, ws[...])
    dn_o[...] = dn.astype(BF16)
    wgrad_o[...] += tn(normed[...], jnp.concatenate([dz_low, dv_low, ds_low], axis=1))

    def unit_of(rows_in):
        rows_in = rows_in.astype(F32)
        return rows_in * lax.rsqrt(jnp.mean(rows_in * rows_in, axis=1, keepdims=True) + EPSILON)

    norm_o[0:1] += jnp.sum(dn * unit_of(hidden[...]), axis=0, keepdims=True)

    @pl.when(b == 0)
    def _():
        ahead[0:8] = jnp.zeros((8, CHAN), F32)
        ahead[8:16] = dpre[0:8]
        ahead[16:24] = jnp.zeros((8, CHAN), F32)
        pos = blk.start - 8 + iota((8, 1), 0)
        left = end_of(marks, pos) - pos
        back = jnp.zeros((8, CHAN), F32)
        for lag in range(1, CONV):
            same = (left > lag) & (pos >= 0)
            back = back + taps[3 - lag : 4 - lag] * (
                ahead[lag : lag + 8] * jnp.where(same, 1.0, 0.0)
            )
        low = jnp.concatenate([jnp.zeros((8, CHAN), F32), back], axis=0).astype(BF16)
        given = nt(low[:, :WIDE], wv[...]) + nt(low[:, WIDE:], ws[...])
        spill_o[...] = given[8:16]
        unit_halo = unit_of(halo[...])
        norm_o[0:1] += jnp.sum(given[8:16] * unit_halo[8:16], axis=0, keepdims=True)
        wgrad_o[:, WIDE:] += tn((unit_halo * gain[...]).astype(BF16), low)


def passed_along(values, axis, by):
    count = lax.axis_size(axis)
    pairs = [(i, i + by) for i in range(count) if 0 <= i + by < count]
    return lax.ppermute(values, axis, pairs)


def handed_to_all(values, axis):
    count = lax.axis_size(axis)
    return lax.all_to_all(
        jnp.broadcast_to(values[None], (count,) + values.shape), axis, 0, 0, tiled=False
    )


def carried(device, sign):
    one, two, three = (passed_along(device, "context", sign * k) for k in (1, 2, 3))

    def join(near, far):
        return near[:STATE] + near[STATE : STATE + 1] * far

    return join(one, join(two, three[:STATE]))


def padded(values, width):
    extra = width - values.shape[-1]
    return jnp.pad(values, [(0, 0)] * (values.ndim - 1) + [(0, extra)])


def body(
    hidden, cotangent, lengths, norm_gain, gate_proj, value_proj, state_proj, step_proj,
    conv_value, conv_state, value_bias, state_bias, step_bias, decay_log, skip_gain,
    mixer_gain, out_proj,
):
    tok = hidden.shape[0]
    blocks = tok // BLOCK
    ctx = lax.axis_index("context")
    rank = lax.axis_index("tensor")
    finishes = jnp.cumsum(lengths[0])
    marks = jnp.concatenate([finishes, (ctx * tok)[None], jnp.zeros((3,), jnp.int32)])
    marks = marks.astype(jnp.int32)

    own_rows = state_proj.shape[0]
    low = state_proj.astype(BF16)
    conv_own = jnp.concatenate([conv_state, state_bias[None]], axis=0)
    top = lax.reduce_precision(conv_own, 8, 7)
    mid = lax.reduce_precision(conv_own - top, 8, 7)
    bot = conv_own - top - mid
    spread = jnp.concatenate([top, mid, bot, jnp.zeros((1, low.shape[1]), F32)], axis=0)
    first = jnp.concatenate([low, spread.astype(BF16)], axis=0)
    first = handed_to_all(first, "tensor").transpose(1, 0, 2).reshape(own_rows + 16, 2 * STATE)
    parts = first[own_rows : own_rows + 15].astype(F32).reshape(3, 5, 2 * STATE)
    conv_shared = parts[0] + parts[1] + parts[2]
    weights = jnp.concatenate(
        [
            value_proj, step_proj, jnp.zeros((own_rows, 61), BF16), first[:own_rows],
            padded(gate_proj, WIDE), padded(out_proj.T, WIDE),
        ],
        axis=1,
    )
    weights = handed_to_all(weights, CELLS).reshape(MODEL, 4 * WIDE)
    wv, ws, wg, wo_t = (weights[:, k * WIDE : (k + 1) * WIDE] for k in range(4))
    place = jnp.arange(BLOCK, dtype=jnp.int32)
    upto = (place[:, None] <= place[None, :]).astype(BF16)

    taps = jnp.concatenate([padded(conv_value, WIDE), conv_shared[:4]], axis=1)
    cbias = jnp.concatenate([padded(value_bias[None], WIDE), conv_shared[4:5]], axis=1)
    rates = -jnp.exp(decay_log)
    hcols = jnp.stack([padded(step_bias, 8), padded(rates, 8)])[:, :, None]
    skip = padded(jnp.repeat(skip_gain, HEADDIM)[None], WIDE)
    mgain = padded(mixer_gain[None], WIDE)
    gain = norm_gain[None]
    halo = passed_along(hidden[tok - 16 :], "context", 1)

    def up(dims):
        return pl.BlockSpec(dims, lambda s: (s,) + (0,) * (len(dims) - 1))

    def up_rows(count):
        return pl.BlockSpec((count, BLOCK), lambda s: (0, s))

    def down(dims):
        return pl.BlockSpec(dims, lambda s: (blocks - 1 - s,) + (0,) * (len(dims) - 1))

    def down_rows(count):
        return pl.BlockSpec((count, BLOCK), lambda s: (0, blocks - 1 - s))

    state_dims = (STATE + 8, WIDE)
    one_state = (1,) + state_dims
    all_states = (blocks,) + state_dims
    normed, xbc, slope, cin, cin_halo, rows, states, device = call(
        project_kernel,
        blocks,
        [
            SMEM, up((BLOCK, MODEL)), whole((16, MODEL)), whole((1, MODEL)),
            whole((MODEL, WIDE)), whole((MODEL, WIDE)), whole((4, CHAN)), whole((1, CHAN)),
            whole((2, 8, 1)), whole((BLOCK, BLOCK)),
        ],
        [
            up((BLOCK, MODEL)), up((BLOCK, CHAN)), up((BLOCK, CHAN)), up((BLOCK, CHAN)),
            whole((8, CHAN)), up_rows(24), up(one_state), whole(state_dims),
        ],
        [
            shape((tok, MODEL), BF16), shape((tok, CHAN), BF16), shape((tok, CHAN), BF16),
            shape((tok, CHAN), BF16), shape((8, CHAN)),
            shape((24, tok)), shape(all_states), shape(state_dims),
        ],
        [pltpu.VMEM((BLOCK + 8, CHAN), F32), pltpu.VMEM((STATE, WIDE), F32), pltpu.VMEM((8, WIDE), F32)],
        2 * tok * MODEL * CHAN + 2 * tok * STATE * WIDE,
        14 * 1024 * 1024,
        marks, hidden, halo, gain, wv, ws, taps, cbias, hcols, upto,
    )
    prefix = carried(device, 1)
    z, e, yi = call(
        intra_kernel,
        blocks,
        [
            SMEM, up((BLOCK, MODEL)), up((BLOCK, MODEL)), whole((MODEL, WIDE)),
            whole((MODEL, WIDE)), up((BLOCK, CHAN)), up_rows(24), whole((1, WIDE)),
        ],
        [up((BLOCK, WIDE))] * 3,
        [shape((tok, WIDE))] * 3,
        [],
        4 * tok * MODEL * WIDE + 8 * tok * BLOCK * WIDE,
        14 * 1024 * 1024,
        marks, normed, cotangent, wg, wo_t, xbc, rows, skip,
    )
    y, mixed, part, sums = call(
        gated_kernel,
        blocks,
        [
            SMEM, up((BLOCK, WIDE)), up((BLOCK, WIDE)), up((BLOCK, WIDE)), up((BLOCK, CHAN)),
            up_rows(24), up(one_state), whole((STATE, WIDE)), whole((1, WIDE)),
            whole((MODEL, WIDE)),
        ],
        [up((BLOCK, WIDE)), up((BLOCK, WIDE)), up((BLOCK, MODEL)), up_rows(8)],
        [shape((tok, WIDE)), shape((tok, WIDE), BF16), shape((tok, MODEL), BF16), shape((8, tok))],
        [],
        2 * tok * MODEL * WIDE + 2 * tok * STATE * WIDE,
        14 * 1024 * 1024,
        marks, yi, z, e, xbc, rows, states, prefix, mgain, wo_t,
    )
    sums = jnp.sum(handed_to_all(sums[:2].reshape(32, 128), "tensor"), axis=0).reshape(2, tok)

    own = tok // lax.axis_size("tensor")
    place = rank * own
    own_hidden = lax.dynamic_slice_in_dim(hidden, place, own, 0).astype(F32)
    own_cot = lax.dynamic_slice_in_dim(cotangent, place, own, 0).astype(F32)
    own_root = lax.rsqrt(lax.dynamic_slice_in_dim(sums[0], place, own, 0) / INNER + EPSILON)
    projected = lax.psum_scatter(part, "tensor", scatter_dimension=0, tiled=True).astype(F32)
    own_out = (own_hidden + own_root[:, None] * projected).astype(BF16)

    dy, dz, reaches, back_device, gains = call(
        gate_back_kernel,
        blocks,
        [
            SMEM, down((BLOCK, WIDE)), down((BLOCK, WIDE)), down((BLOCK, WIDE)),
            down((BLOCK, CHAN)), down_rows(24), down_rows(2), whole((1, WIDE)),
        ],
        [
            down((BLOCK, WIDE)), down((BLOCK, WIDE)), down(one_state), whole(state_dims),
            whole((8, WIDE)),
        ],
        [
            shape((tok, WIDE)), shape((tok, WIDE), BF16), shape(all_states), shape(state_dims),
            shape((8, WIDE)),
        ],
        [pltpu.VMEM((STATE, WIDE), F32), pltpu.VMEM((8, WIDE), F32)],
        2 * tok * STATE * WIDE,
        14 * 1024 * 1024,
        marks, y, z, e, xbc, rows, sums, mgain,
    )
    suffix = carried(back_device, -1)
    dxi, dbc, stats, grad_out_t = call(
        intra_back_kernel,
        blocks,
        [
            SMEM, up((BLOCK, WIDE)), up((BLOCK, CHAN)), up_rows(24), up(one_state),
            whole((STATE, WIDE)), up_rows(2), up((BLOCK, WIDE)), up((BLOCK, MODEL)),
            whole((1, WIDE)),
        ],
        [up((BLOCK, WIDE)), up((BLOCK, WIDE)), up_rows(16), whole((MODEL, WIDE))],
        [shape((tok, WIDE)), shape((tok, WIDE)), shape((16, tok)), shape((MODEL, WIDE))],
        [],
        2 * tok * MODEL * WIDE + 16 * tok * BLOCK * WIDE,
        14 * 1024 * 1024,
        marks, dy, xbc, rows, states, prefix, sums, mixed, cotangent, skip,
    )
    dxi, own_out = lax.optimization_barrier((dxi, own_out))
    output = lax.all_gather(own_out, "tensor", axis=0, tiled=True)
    before = pl.BlockSpec(
        (16, CHAN), lambda s: (jnp.maximum((blocks - 1 - s) * (BLOCK // 16) - 1, 0), 0)
    )
    dn, wgrad, chan, step_rows, norm_part, spill = call(
        input_back_kernel,
        blocks,
        [
            SMEM, down((BLOCK, MODEL)), down((BLOCK, MODEL)), whole((16, MODEL)),
            down((BLOCK, WIDE)), down((BLOCK, WIDE)), down((BLOCK, WIDE)), down((BLOCK, CHAN)),
            down((BLOCK, CHAN)), down((BLOCK, CHAN)), before, whole((8, CHAN)), down_rows(24),
            down_rows(16), down(one_state), whole((STATE, WIDE)), down(one_state),
            whole((STATE, WIDE)), whole((1, MODEL)), whole((MODEL, WIDE)), whole((MODEL, WIDE)),
            whole((MODEL, WIDE)), whole((4, CHAN)), whole((2, 8, 1)), whole((BLOCK, BLOCK)),
        ],
        [
            down((BLOCK, MODEL)), whole((MODEL, 3 * WIDE)), whole((8, CHAN)), whole((16, BLOCK)),
            whole((8, MODEL)), whole((8, MODEL)),
        ],
        [
            shape((tok, MODEL), BF16), shape((MODEL, 3 * WIDE)), shape((8, CHAN)),
            shape((16, BLOCK)), shape((8, MODEL)), shape((8, MODEL)),
        ],
        [pltpu.VMEM((BLOCK + 8, CHAN), F32), pltpu.VMEM((BLOCK + 8, CHAN), F32)],
        12 * tok * MODEL * WIDE,
        24 * 1024 * 1024,
        marks, hidden, normed, halo, dz, dxi, dbc, xbc, slope, cin, cin, cin_halo,
        rows, stats, states, prefix, reaches, suffix, gain, wg, wv, ws, taps, hcols, upto.T,
    )
    arrived = passed_along(spill, "context", -1)
    end = dn[tok - 8 :].astype(F32) + arrived
    dn = lax.dynamic_update_slice(dn, end.astype(BF16), (tok - 8, 0))
    dn, output = lax.optimization_barrier((dn, output))
    own_dn = lax.psum_scatter(dn, "tensor", scatter_dimension=0, tiled=True)
    big = jnp.concatenate([wgrad, grad_out_t], axis=1).astype(BF16).reshape(-1, own_rows, 4 * WIDE)
    big = jnp.sum(lax.all_to_all(big, CELLS, 0, 0, tiled=False).astype(F32), axis=0)
    head_sums = jnp.sum(step_rows, axis=1)
    skip_sums = jnp.sum(gains[1, :INNER_DEV].reshape(HEADS_DEV, HEADDIM), axis=1)
    small = jnp.concatenate(
        [
            chan[:5].reshape(-1),
            norm_part[0],
            gains[0],
            head_sums,
            padded(skip_sums, 8),
            jnp.zeros((1000,), F32),
        ]
    ).reshape(36, 128)
    small = jnp.sum(handed_to_all(small, CELLS), axis=0).reshape(-1)
    own_dn, big, small = lax.optimization_barrier((own_dn, big, small))

    scaling = lax.rsqrt(jnp.mean(own_hidden * own_hidden, axis=1, keepdims=True) + EPSILON)
    unit = own_hidden * scaling
    own_dn = own_dn.astype(F32)
    scaled = own_dn * norm_gain[None]
    own_grad = own_cot + scaling * (
        scaled - unit * jnp.mean(scaled * unit, axis=1, keepdims=True)
    )
    grad_hidden = lax.all_gather(own_grad.astype(BF16), "tensor", axis=0, tiled=True)

    chan = small[: 5 * CHAN].reshape(5, CHAN)
    at = 5 * CHAN
    norm_cells = small[at : at + MODEL]
    at += MODEL
    grad_mixer = small[at : at + INNER_DEV]
    at += WIDE
    grad_step_bias = small[at : at + HEADS_DEV]
    grad_decay = small[at + 8 : at + 8 + HEADS_DEV]
    grad_skip = small[at + 16 : at + 16 + HEADS_DEV]
    share = 2 * STATE // lax.axis_size("tensor")
    shared = jnp.concatenate([big[:, 2 * WIDE : 3 * WIDE], chan[:, WIDE:]], axis=0)
    shared = shared.reshape(own_rows + 5, -1, share).transpose(1, 0, 2)
    shared = shared.reshape(shared.shape[0], -1)
    count = shared.shape[1]
    final = jnp.concatenate(
        [shared, jnp.broadcast_to(norm_cells[None], (shared.shape[0], MODEL))], axis=1
    )
    final = padded(final, 2560).reshape(-1, 20, 128)
    final = jnp.sum(lax.all_to_all(final, "tensor", 0, 0, tiled=False), axis=0).reshape(-1)
    state_all = final[:count].reshape(own_rows + 5, share)
    return (
        output,
        grad_hidden,
        final[count : count + MODEL],
        big[:, :INNER_DEV],
        big[:, WIDE : WIDE + INNER_DEV],
        state_all[:own_rows],
        big[:, WIDE + INNER_DEV : WIDE + INNER_DEV + HEADS_DEV],
        chan[:4, :INNER_DEV],
        state_all[own_rows : own_rows + 4],
        chan[4, :INNER_DEV],
        state_all[own_rows + 4],
        grad_step_bias,
        grad_decay,
        grad_skip,
        grad_mixer,
        big[:, 3 * WIDE : 3 * WIDE + INNER_DEV].T,
    )


def solution(mesh):
    cells = P(CELLS, None)
    split = P(CELLS, "tensor")
    return jax.shard_map(
        body,
        mesh=mesh,
        in_specs=(
            cells, cells, P("shard", None), P(), split, split, split, split, P(None, "tensor"),
            P(None, "tensor"), P("tensor"), P("tensor"), P("tensor"), P("tensor"), P("tensor"),
            P("tensor"), P("tensor", CELLS),
        ),
        out_specs=(
            cells, cells, P(), split, split, split, split, P(None, "tensor"), P(None, "tensor"),
            P("tensor"), P("tensor"), P("tensor"), P("tensor"), P("tensor"), P("tensor"),
            P("tensor", CELLS),
        ),
        check_vma=False,
    )
```

```python
import jax
import jax.numpy as jnp
from jax import lax
from jax.experimental import pallas as pl
from jax.experimental.pallas import tpu as pltpu
from jax.sharding import PartitionSpec as P

MODEL = 768
INNER = 1536
HEADDIM = 64
STATE = 128
CONV = 4
BLOCK = 256
HEADS_DEV = 3
INNER_DEV = 192
WIDE = 256
CHAN = 512
EPSILON = 1e-05
F32 = jnp.float32
BF16 = jnp.bfloat16
CELLS = ("shard", "context")
VMEM_LIMIT = 60 * 1024 * 1024
PARTS = (2, 2, 2, 2, 1, 2)


def nn(a, b):
    return lax.dot_general(a, b, (((1,), (0,)), ((), ())), preferred_element_type=F32)


def nt(a, b):
    return lax.dot_general(a, b, (((1,), (1,)), ((), ())), preferred_element_type=F32)


def tn(a, b):
    return lax.dot_general(a, b, (((0,), (0,)), ((), ())), preferred_element_type=F32)


def iota(shape, dim):
    return lax.broadcasted_iota(jnp.int32, shape, dim)


def start_of(marks, pos):
    start = jnp.zeros_like(pos)
    for k in range(3):
        start = jnp.where(pos >= marks[k], marks[k], start)
    return start


def end_of(marks, pos):
    end = jnp.full_like(pos, marks[3])
    for k in (2, 1, 0):
        end = jnp.where(pos < marks[k], marks[k], end)
    return end


def running_sum(rows, ones):
    top = rows.astype(BF16)
    rest = rows - top.astype(F32)
    mid = rest.astype(BF16)
    low = (rest - mid.astype(F32)).astype(BF16)
    pieces = [top.astype(F32), mid.astype(F32), low.astype(F32), jnp.zeros((8, BLOCK), F32)]
    sums = nn(jnp.concatenate(pieces, axis=0).astype(BF16), ones)
    return sums[0:8] + sums[8:16] + sums[16:24]


def by_head(cols, width=WIDE):
    lane = iota((1, width), 1)
    return jnp.where(
        lane < HEADDIM,
        cols[0],
        jnp.where(lane < 2 * HEADDIM, cols[1], jnp.where(lane < 3 * HEADDIM, cols[2], 0.0)),
    )


def head_masks():
    row = iota((8, WIDE), 0)
    lane = iota((8, WIDE), 1)
    low = row * HEADDIM
    return jnp.where((lane >= low) & (lane < low + HEADDIM) & (row < HEADS_DEV), 1.0, 0.0)


def of_head(values, h):
    lane = iota((1, WIDE), 1)
    return jnp.where((lane >= h * HEADDIM) & (lane < (h + 1) * HEADDIM), values, 0.0)


def to_columns(rows):
    have = 8 * len(rows)
    stacked = jnp.concatenate(list(rows) + [jnp.zeros((128 - have, BLOCK), F32)], axis=0)
    return stacked.T


def column(cols, part, h):
    at = 8 * part + h
    return cols[:, at : at + 1]


def silu_parts(values):
    sig = 1.0 / (1.0 + jnp.exp(-values))
    return values * sig, sig * (1.0 + values * (1.0 - sig))


class Block:
    def __init__(self, marks, b):
        self.marks = marks
        self.start = marks[4] + b * BLOCK
        self.pos_row = self.start + iota((1, BLOCK), 1)
        self.pos_col = self.start + iota((BLOCK, 1), 0)

    def lead(self, cum):
        carried = start_of(self.marks, self.pos_row) < self.start
        return jnp.where(carried, jnp.exp(cum), 0.0)

    def tail_base(self, cum):
        last = cum[:, BLOCK - 1 : BLOCK]
        kept = end_of(self.marks, self.pos_row) > self.start + BLOCK - 1
        return jnp.where(kept, jnp.exp(last - cum), 0.0)

    def allowed(self):
        first = start_of(self.marks, self.pos_col)
        return (self.pos_row >= first) & (self.pos_row <= self.pos_col)

    def since_start(self):
        return self.pos_col - start_of(self.marks, self.pos_col)

    def until_end(self):
        return end_of(self.marks, self.pos_col) - self.pos_col


def decay_of(allowed, cum_col, cum_row):
    return jnp.exp(jnp.where(allowed, cum_col - cum_row, -1e30))


def message(state, decay):
    return jnp.concatenate([state, decay], axis=0)


def carried(messages):
    one, two, three = (m[...] for m in messages)

    def join(near, far):
        return near[:STATE] + near[STATE : STATE + 1] * far

    return join(one, join(two, three[:STATE]))


def last_by_lane(rows):
    return by_head([rows[h : h + 1, BLOCK - 1 : BLOCK] for h in range(HEADS_DEV)])


class At:
    def __init__(self, index, blocks, part, parts):
        self.index = index
        self.count = blocks
        self.can_be_first = part == 0
        self.can_be_last = part == parts - 1

    def when_first(self, do):
        if self.can_be_first:
            pl.when(self.index == 0)(do)

    def when_last(self, do):
        if self.can_be_last:
            pl.when(self.index == self.count - 1)(do)


def rows_of(width):
    return ("rows", width)


def lanes_of(count):
    return ("lanes", count)


def whole(dims):
    return ("whole", dims)


STATE_DIMS = (STATE + 8, WIDE)
STATES = ("states",)
SMEM = ("smem",)


def call(kernel, blocks, parts, down, ins, outs, scratch, micros, *args):
    steps = blocks // parts
    tile = parts * BLOCK

    def step(s):
        return steps - 1 - s if down else s

    def spec(kind):
        what = kind[0]
        if what == "smem":
            return pl.BlockSpec(memory_space=pltpu.SMEM)
        if what == "rows":
            return pl.BlockSpec((tile, kind[1]), lambda s: (step(s), 0))
        if what == "lanes":
            return pl.BlockSpec((kind[1], tile), lambda s: (0, step(s)))
        if what == "states":
            return pl.BlockSpec((parts,) + STATE_DIMS, lambda s: (step(s), 0, 0))
        if what == "before":
            return pl.BlockSpec(
                (16, kind[1]), lambda s: (jnp.maximum(step(s) * (tile // 16) - 1, 0), 0)
            )
        return pl.BlockSpec(kind[1], lambda s: (0,) * len(kind[1]))

    def view(refs, n, kind, k):
        ref = refs[n]
        if kind[0] == "rows":
            return ref.at[pl.ds(k * BLOCK, BLOCK)]
        if kind[0] == "lanes":
            return ref.at[:, pl.ds(k * BLOCK, BLOCK)]
        if kind[0] == "states":
            return ref.at[pl.ds(k, 1)]
        if kind[0] == "before" and k > 0:
            return refs[n - 1].at[pl.ds(k * BLOCK - 16, 16)]
        return ref

    kinds = list(ins) + [kind for kind, _ in outs]

    def run(*refs):
        order = range(parts - 1, -1, -1) if down else range(parts)
        for k in order:
            at = At(step(pl.program_id(0)) * parts + k, blocks, k, parts)
            views = [view(refs, n, kind, k) for n, kind in enumerate(kinds)]
            kernel(at, *views, *refs[len(kinds) :])

    def dims(kind):
        what = kind[0]
        if what == "rows":
            return (blocks * BLOCK, kind[1])
        if what == "lanes":
            return (kind[1], blocks * BLOCK)
        if what == "states":
            return (blocks,) + STATE_DIMS
        return kind[1]

    return pl.pallas_call(
        run,
        grid=(steps,),
        in_specs=[spec(kind) for kind in ins],
        out_specs=[spec(kind) for kind, _ in outs],
        out_shape=[jax.ShapeDtypeStruct(dims(kind), dtype) for kind, dtype in outs],
        scratch_shapes=scratch,
        compiler_params=pltpu.CompilerParams(
            dimension_semantics=("arbitrary",), vmem_limit_bytes=VMEM_LIMIT
        ),
        cost_estimate=pl.CostEstimate(
            flops=int(micros * 1.15e9), bytes_accessed=int(micros * 1e6), transcendentals=0
        ),
    )(*args)


def project_kernel(
    at, marks, step_bias, decay_log, skip_gain, hidden, halo, norm_gain, weights, conv_value,
    value_bias, mixer_gain, conv_shared,
    normed_o, xbc_o, slope_o, cin_o, cin_halo_o, rows_o, state_o, device_o,
    gain, taps, lanes, hcols,
    ext, state, decay, upto,
):
    blk = Block(marks, at.index)
    wv = weights.at[:, 0:WIDE]
    ws = weights.at[:, WIDE : 2 * WIDE]

    @at.when_first
    def _():
        gain[...] = jnp.broadcast_to(norm_gain[...].reshape(1, MODEL), (8, MODEL))
        taps[...] = jnp.zeros_like(taps)
        taps[0:4, 0:INNER_DEV] = conv_value[...]
        taps[4:5, 0:INNER_DEV] = value_bias[...].reshape(1, INNER_DEV)
        taps[0:5, WIDE:] = conv_shared[...]
        lanes[...] = jnp.zeros_like(lanes)
        lanes[0:1, 0:INNER_DEV] = mixer_gain[...].reshape(1, INNER_DEV)
        lanes[1:2] = by_head([skip_gain[h] for h in range(HEADS_DEV)])
        row = iota((8, BLOCK), 0)
        bias = jnp.zeros((8, BLOCK), F32)
        rate = jnp.zeros((8, BLOCK), F32)
        for h in range(HEADS_DEV):
            bias = jnp.where(row == h, step_bias[h], bias)
            rate = jnp.where(row == h, decay_log[h], rate)
        hcols[0:8] = bias
        hcols[8:16] = jnp.where(row < HEADS_DEV, -jnp.exp(rate), 0.0)
        square = (BLOCK, BLOCK)
        upto[...] = jnp.where(iota(square, 0) <= iota(square, 1), 1.0, 0.0).astype(BF16)

    def norm(rows):
        rows = rows.astype(F32)
        scale = lax.rsqrt(jnp.mean(rows * rows, axis=1, keepdims=True) + EPSILON)
        return (rows * scale * gain[0:1]).astype(BF16)

    @at.when_first
    def _():
        ahead = norm(halo[...])
        into = jnp.concatenate([nn(ahead, wv[...]), nn(ahead, ws[...])], axis=1)
        into = into.astype(BF16).astype(F32)
        ext[0:8] = into[8:16]
        cin_halo_o[...] = into[8:16]
        state[...] = jnp.zeros_like(state)
        decay[...] = jnp.ones_like(decay)

    normed = norm(hidden[...])
    normed_o[...] = normed
    value_pre = nn(normed, wv[...])
    state_pre = nn(normed, ws[...])
    cin = jnp.concatenate([value_pre, state_pre], axis=1).astype(BF16)
    cin_o[...] = cin
    ext[8 : 8 + BLOCK] = cin.astype(F32)
    pre = taps[4:5] + taps[3:4] * ext[8 : 8 + BLOCK]
    since = blk.since_start()
    for lag in range(1, CONV):
        pre = pre + taps[3 - lag : 4 - lag] * (
            jnp.where(since >= lag, ext[8 - lag : 8 - lag + BLOCK], 0.0)
        )
    ext[0:8] = ext[BLOCK : BLOCK + 8]
    act, slope = silu_parts(pre)
    act = act.astype(BF16)
    xbc_o[...] = act
    slope_o[...] = slope.astype(BF16)

    raw = value_pre[:, 128:256].T[64:72] + hcols[0:8]
    dt = jnp.maximum(raw, 0.0) + jnp.log1p(jnp.exp(-jnp.abs(raw)))
    sig = 1.0 / (1.0 + jnp.exp(-raw))
    cum = running_sum(dt * hcols[8:16], upto[...])
    rows_o[0:8] = dt
    rows_o[8:16] = sig
    rows_o[16:24] = cum
    lead = blk.lead(cum)
    tail = blk.tail_base(cum) * dt
    cols = to_columns([tail])
    tail_lanes = by_head([column(cols, 0, h) for h in range(HEADS_DEV)])
    packed = (act[:, :WIDE].astype(F32) * tail_lanes).astype(BF16)
    fresh = tn(act[:, WIDE : WIDE + STATE], packed)
    last = last_by_lane(lead)
    state_o[0, 0:STATE] = state[...]
    state_o[0, STATE : STATE + 8] = decay[...]
    state[...] = last * state[...] + fresh
    decay[...] = last * decay[...]

    @at.when_last
    def _():
        device_o[...] = message(state[...], decay[...])


def intra_kernel(at, marks, normed, cot, weights, xbc, rows, lanes, z_o, e_o, yi_o):
    blk = Block(marks, at.index)
    z_o[...] = nn(normed[...], weights[:, 0:WIDE]).astype(BF16)
    e_o[...] = nn(cot[...], weights[:, WIDE : 2 * WIDE]).astype(BF16)
    dt = rows[0:8]
    cum = rows[16:24]
    x = xbc[:, :WIDE].astype(F32)
    scores = nt(xbc[:, WIDE + STATE :], xbc[:, WIDE : WIDE + STATE])
    allowed = blk.allowed()
    cols = to_columns([cum])
    out = lanes[1:2] * x
    for h in range(HEADS_DEV):
        decays = decay_of(allowed, column(cols, 0, h), cum[h : h + 1])
        mix = (scores * decays * dt[h : h + 1]).astype(BF16)
        out = out + nn(mix, of_head(x, h).astype(BF16))
    yi_o[...] = out.astype(BF16)


def gated_kernel(
    at, marks, yi, z, e, xbc, rows, states, one, two, three, lanes, weights,
    y_o, mixed_o, part_o, sums_o, prefix,
):
    @at.when_first
    def _():
        prefix[...] = carried((one, two, three))

    blk = Block(marks, at.index)
    lead = blk.lead(rows[16:24])
    cols = to_columns([lead])
    lead_lanes = by_head([column(cols, 0, h) for h in range(HEADS_DEV)])
    entering = states[0, 0:STATE] + states[0, STATE : STATE + 1] * prefix[...]
    y = yi[...].astype(F32) + lead_lanes * nn(xbc[:, WIDE + STATE :], entering.astype(BF16))
    y_o[...] = y.astype(BF16)
    gate, _ = silu_parts(z[...].astype(F32))
    v = y * gate
    mixed = (v * lanes[0:1]).astype(BF16)
    mixed_o[...] = mixed
    part_o[...] = nt(mixed, weights[:, WIDE : 2 * WIDE]).astype(BF16)
    row = iota((16, 2 * WIDE), 0)
    lane = iota((16, 2 * WIDE), 1)
    pick = jnp.where(((row == 0) & (lane < WIDE)) | ((row == 1) & (lane >= WIDE)), 1.0, 0.0)
    both = jnp.concatenate([v * v, e[...].astype(F32) * mixed.astype(F32)], axis=1)
    sums_o[...] = nt(pick.astype(BF16), both.astype(BF16))[0:2]


def gate_back_kernel(
    at, marks, y, z, e, xbc, rows, sums, lanes,
    dy_o, dz_o, reach_o, device_o, gains_o,
    carry, decay,
):
    blk = Block(marks, at.index)

    @at.when_last
    def _():
        carry[...] = jnp.zeros_like(carry)
        decay[...] = jnp.ones_like(decay)
        gains_o[...] = jnp.zeros_like(gains_o)

    lead = blk.lead(rows[16:24])
    root = lax.rsqrt(sums[0:1] / INNER + EPSILON)
    coef = sums[1:2] * root * root * root / INNER
    cols = to_columns([lead, jnp.broadcast_to(root, (8, BLOCK)), jnp.broadcast_to(coef, (8, BLOCK))])
    lead_lanes = by_head([column(cols, 0, h) for h in range(HEADS_DEV)])
    gate, slope = silu_parts(z[...].astype(F32))
    y_v = y[...].astype(F32)
    v = y_v * gate
    dm = column(cols, 1, 0) * e[...].astype(F32)
    dv = lanes[0:1] * dm - column(cols, 2, 0) * v
    dy = dv * gate
    dy_o[...] = dy.astype(BF16)
    dz_o[...] = (dv * y_v * slope).astype(BF16)
    x = xbc[:, :WIDE].astype(F32)
    gains_o[0:1] += jnp.sum(v * dm, axis=0, keepdims=True)
    gains_o[1:2] += jnp.sum(dy * x, axis=0, keepdims=True)
    reach = tn(xbc[:, WIDE + STATE :], (dy * lead_lanes).astype(BF16))
    last = last_by_lane(lead)
    reach_o[0, 0:STATE] = carry[...]
    reach_o[0, STATE : STATE + 8] = decay[...]
    carry[...] = last * carry[...] + reach
    decay[...] = last * decay[...]

    @at.when_first
    def _():
        device_o[...] = message(carry[...], decay[...])


def intra_back_kernel(
    at, marks, dy_r, xbc, rows, states, prefix, sums, mixed, cot, lanes,
    dxi_o, dbc_o, stats_o, grad_out_o,
):
    blk = Block(marks, at.index)

    @at.when_first
    def _():
        grad_out_o[...] = jnp.zeros_like(grad_out_o)

    dt = rows[0:8]
    cum = rows[16:24]
    lead = blk.lead(cum)
    root = lax.rsqrt(sums[0:1] / INNER + EPSILON)
    cols = to_columns([cum, lead, jnp.broadcast_to(root, (8, BLOCK))])
    lead_lanes = by_head([column(cols, 1, h) for h in range(HEADS_DEV)])
    rooted = (mixed[...].astype(F32) * column(cols, 2, 0)).astype(BF16)
    grad_out_o[...] += tn(cot[...], rooted)

    dy = dy_r[...].astype(F32)
    x_low = xbc[:, :WIDE]
    b_low = xbc[:, WIDE : WIDE + STATE]
    c_low = xbc[:, WIDE + STATE :]
    entering = states[0, 0:STATE] + states[0, STATE : STATE + 1] * prefix[...]
    held = entering.astype(BF16)
    masks = head_masks().astype(BF16)
    cross = nn(c_low, held)
    lead_grad = nt(masks, (dy * cross).astype(BF16))
    dc = nt((dy * lead_lanes).astype(BF16), held)
    scores = nt(c_low, b_low)
    allowed = blk.allowed()
    ds = jnp.zeros((BLOCK, BLOCK), F32)
    dx = lanes[1:2] * dy
    lane = iota((1, 128), 1)
    row8 = iota((8, 1), 0)
    row_sums = jnp.zeros((BLOCK, 128), F32)
    time_grad = jnp.zeros((8, BLOCK), F32)
    for h in range(HEADS_DEV):
        dt_h = dt[h : h + 1]
        dy_h = of_head(dy, h).astype(BF16)
        decays = decay_of(allowed, column(cols, 0, h), cum[h : h + 1])
        weighted = nt(dy_h, x_low) * decays
        ds = ds + weighted * dt_h
        scored = weighted * scores
        time_grad = time_grad + jnp.where(
            row8 == h, jnp.sum(scored, axis=0, keepdims=True), 0.0
        )
        row_sums = row_sums + jnp.where(
            lane == h, jnp.sum(scored * dt_h, axis=1, keepdims=True), 0.0
        )
        mix = (scores * decays * dt_h).astype(BF16)
        dx = dx + tn(mix, dy_h)
    ds_low = ds.astype(BF16)
    dxi_o[...] = dx.astype(BF16)
    dbc_o[:, 0:STATE] = tn(ds_low, c_low).astype(BF16)
    dbc_o[:, STATE : 2 * STATE] = (dc + nn(ds_low, b_low)).astype(BF16)
    stats_o[0:8] = time_grad
    stats_o[8:16] = row_sums.T[0:8] - time_grad * dt + lead_grad * lead


def input_back_kernel(
    at, marks, hidden, normed, halo, dz, dxi, dbc, xbc, slope, cin, cin_before, cin_halo,
    rows, stats, states, prefix, reaches, one, two, three, gain, later, weights, taps, hcols,
    grad_out_t, gains,
    dn_o, big_o, pack_o, spill_o,
    ext, ahead, suffix, since, wgrad_o, chan_o, step_o, norm_o,
):
    b = at.index
    blk = Block(marks, b)
    wg = later.at[:, 0:WIDE]
    wv = weights.at[:, 0:WIDE]
    ws = weights.at[:, WIDE : 2 * WIDE]

    @at.when_last
    def _():
        suffix[...] = carried((one, two, three))
        square = (BLOCK, BLOCK)
        since[...] = jnp.where(iota(square, 0) >= iota(square, 1), 1.0, 0.0).astype(BF16)
        wgrad_o[...] = jnp.zeros_like(wgrad_o)
        chan_o[...] = jnp.zeros_like(chan_o)
        step_o[...] = jnp.zeros_like(step_o)
        norm_o[...] = jnp.zeros_like(norm_o)
        ahead[BLOCK : BLOCK + 8] = jnp.zeros((8, CHAN), F32)

    dt = rows[0:8]
    sig = rows[8:16]
    cum = rows[16:24]
    rate = hcols[8:16]
    lead = blk.lead(cum)
    tail_base = blk.tail_base(cum)
    tail = tail_base * dt
    cols = to_columns([tail])
    tail_lanes = by_head([column(cols, 0, h) for h in range(HEADS_DEV)])
    entering = states[0, 0:STATE] + states[0, STATE : STATE + 1] * prefix[...]
    leaving = reaches[0, 0:STATE] + reaches[0, STATE : STATE + 1] * suffix[...]
    leaving_low = leaving.astype(BF16)
    x = xbc[:, :WIDE].astype(F32)
    dpacked = nn(xbc[:, WIDE : WIDE + STATE], leaving_low)
    packed = (x * tail_lanes).astype(BF16)
    masks = head_masks()
    tail_grad = nt(masks.astype(BF16), (dpacked * x).astype(BF16))
    dx = dxi[...].astype(F32) + dpacked * tail_lanes
    db = dbc[:, 0:STATE].astype(F32) + nt(packed, leaving_low)
    dc = dbc[:, STATE : 2 * STATE].astype(F32)

    tail_term = tail_grad * tail
    state_term = jnp.sum(leaving * entering, axis=0, keepdims=True)
    last_term = jnp.sum(tail_term, axis=1, keepdims=True) + (
        jnp.sum(masks * state_term, axis=1, keepdims=True) * lead[:, BLOCK - 1 : BLOCK]
    )
    dcum = stats[8:16] - tail_term + jnp.where(iota((8, BLOCK), 1) == BLOCK - 1, last_term, 0.0)
    dla = running_sum(dcum, since[...])
    ddt = stats[0:8] + tail_grad * tail_base + dla * rate
    dstep = jnp.where(iota((8, 1), 0) < HEADS_DEV, ddt * sig, 0.0)
    step_o[0:8] += dstep
    step_o[8:16] += dla * dt * rate
    placed = jnp.concatenate(
        [jnp.zeros((64, BLOCK), F32), dstep, jnp.zeros((56, BLOCK), F32)], axis=0
    ).T

    dpre = jnp.concatenate([dx, db, dc], axis=1) * slope[...].astype(F32)
    before = cin_before[...][8:16].astype(F32)
    ext[0:8] = jnp.where(b == 0, cin_halo[...], before) if at.can_be_first else before
    ext[8 : 8 + BLOCK] = cin[...].astype(F32)
    ahead[0:BLOCK] = dpre
    chan_o[4:5] += jnp.sum(dpre, axis=0, keepdims=True)
    chan_o[3:4] += jnp.sum(dpre * ext[8 : 8 + BLOCK], axis=0, keepdims=True)
    din = taps[3:4] * dpre
    reach_back = blk.since_start()
    reach_ahead = blk.until_end()
    for lag in range(1, CONV):
        tap = 3 - lag
        chan_o[tap : tap + 1] += jnp.sum(
            jnp.where(reach_back >= lag, dpre * ext[8 - lag : 8 - lag + BLOCK], 0.0),
            axis=0,
            keepdims=True,
        )
        din = din + taps[tap : tap + 1] * (
            jnp.where(reach_ahead > lag, ahead[lag : lag + BLOCK], 0.0)
        )
    ahead[BLOCK : BLOCK + 8] = dpre[0:8]

    dz_low = dz[...]
    dv_low = jnp.concatenate([din[:, 0:128], din[:, 128:256] + placed], axis=1).astype(BF16)
    ds_low = din[:, WIDE:].astype(BF16)
    dn = nt(dz_low, wg[...]) + nt(dv_low, wv[...]) + nt(ds_low, ws[...])
    dn_o[...] = dn.astype(BF16)
    wgrad_o[...] += tn(normed[...], jnp.concatenate([dz_low, dv_low, ds_low], axis=1))

    def unit_of(rows_in):
        rows_in = rows_in.astype(F32)
        return rows_in * lax.rsqrt(jnp.mean(rows_in * rows_in, axis=1, keepdims=True) + EPSILON)

    norm_o[0:1] += jnp.sum(dn * unit_of(hidden[...]), axis=0, keepdims=True)

    @at.when_first
    def _():
        ahead[0:8] = jnp.zeros((8, CHAN), F32)
        ahead[8:16] = dpre[0:8]
        ahead[16:24] = jnp.zeros((8, CHAN), F32)
        pos = blk.start - 8 + iota((8, 1), 0)
        left = end_of(marks, pos) - pos
        back = jnp.zeros((8, CHAN), F32)
        for lag in range(1, CONV):
            same = (left > lag) & (pos >= 0)
            back = back + taps[3 - lag : 4 - lag] * (
                ahead[lag : lag + 8] * jnp.where(same, 1.0, 0.0)
            )
        low = jnp.concatenate([jnp.zeros((8, CHAN), F32), back], axis=0).astype(BF16)
        given = nt(low[:, :WIDE], wv[...]) + nt(low[:, WIDE:], ws[...])
        spill_o[...] = given[8:16]
        unit_halo = unit_of(halo[...])
        norm_o[0:1] += jnp.sum(given[8:16] * unit_halo[8:16], axis=0, keepdims=True)
        wgrad_o[:, WIDE:] += tn((unit_halo * gain[0:1]).astype(BF16), low)
        big_o[:, 0 : 3 * WIDE] = wgrad_o[...].astype(BF16)
        big_o[:, 3 * WIDE :] = grad_out_t[...].astype(BF16)
        pack = jnp.concatenate(
            [
                jnp.concatenate([chan_o[0:5], jnp.zeros((5, CHAN), F32)], axis=1),
                jnp.concatenate([norm_o[0:1], step_o[8:9]], axis=1),
                jnp.concatenate([gains[0:1], gains[1:2], step_o[9:10], step_o[10:11]], axis=1),
                jnp.concatenate(
                    [step_o[0:1], step_o[1:2], step_o[2:3], jnp.zeros((1, WIDE), F32)], axis=1
                ),
            ],
            axis=0,
        )
        top = pack.astype(BF16).astype(F32)
        pack_o[...] = jnp.concatenate([top, pack - top], axis=0).astype(BF16)


def passed_along(values, axis, by):
    count = lax.axis_size(axis)
    pairs = [(i, i + by) for i in range(count) if 0 <= i + by < count]
    return lax.ppermute(values, axis, pairs)


def handed_to_all(values, axis):
    count = lax.axis_size(axis)
    return lax.all_to_all(
        jnp.broadcast_to(values[None], (count,) + values.shape), axis, 0, 0, tiled=False
    )


def sent_along(device, sign):
    return [passed_along(device, "context", sign * k) for k in (1, 2, 3)]


def padded(values, width):
    extra = width - values.shape[-1]
    return jnp.pad(values, [(0, 0)] * (values.ndim - 1) + [(0, extra)])


def body(
    hidden, cotangent, lengths, norm_gain, gate_proj, value_proj, state_proj, step_proj,
    conv_value, conv_state, value_bias, state_bias, step_bias, decay_log, skip_gain,
    mixer_gain, out_proj,
):
    tok = hidden.shape[0]
    blocks = tok // BLOCK
    ctx = lax.axis_index("context")
    rank = lax.axis_index("tensor")

    own_rows = state_proj.shape[0]
    first = jnp.concatenate(
        [state_proj.astype(F32), conv_state, state_bias[None], jnp.zeros((3, state_proj.shape[1]), F32)],
        axis=0,
    )
    first = handed_to_all(first, "tensor")
    first, lengths, gate_proj, out_proj, edge = lax.optimization_barrier(
        (first, lengths, gate_proj, out_proj, hidden[tok - 16 :])
    )
    first = first.transpose(1, 0, 2).reshape(own_rows + 8, 2 * STATE)
    conv_shared = first[own_rows : own_rows + 5]
    needed = jnp.concatenate(
        [
            value_proj, step_proj, jnp.zeros((own_rows, 61), BF16), first[:own_rows].astype(BF16),
        ],
        axis=1,
    )
    needed = handed_to_all(needed, CELLS).reshape(MODEL, 2 * WIDE)
    finishes = jnp.cumsum(lengths[0])
    marks = jnp.concatenate([finishes, (ctx * tok)[None], jnp.zeros((3,), jnp.int32)])
    marks = marks.astype(jnp.int32)
    later = jnp.concatenate([padded(gate_proj, WIDE), padded(out_proj.T, WIDE)], axis=1)
    later = handed_to_all(later, CELLS)
    halo = passed_along(edge, "context", 1)

    pair = whole((MODEL, 2 * WIDE))
    normed, xbc, slope, cin, cin_halo, rows, states, device, gain, taps, lanes, hcols = call(
        project_kernel, blocks, PARTS[0], False,
        [
            SMEM, SMEM, SMEM, SMEM, rows_of(MODEL), whole((16, MODEL)), whole((MODEL,)), pair,
            whole((4, INNER_DEV)), whole((INNER_DEV,)), whole((INNER_DEV,)), whole((5, 2 * STATE)),
        ],
        [
            (rows_of(MODEL), BF16), (rows_of(CHAN), BF16), (rows_of(CHAN), BF16),
            (rows_of(CHAN), BF16), (whole((8, CHAN)), F32), (lanes_of(24), F32), (STATES, F32),
            (whole(STATE_DIMS), F32), (whole((8, MODEL)), F32), (whole((8, CHAN)), F32),
            (whole((8, WIDE)), F32), (whole((16, BLOCK)), F32),
        ],
        [
            pltpu.VMEM((BLOCK + 8, CHAN), F32), pltpu.VMEM((STATE, WIDE), F32),
            pltpu.VMEM((8, WIDE), F32), pltpu.VMEM((BLOCK, BLOCK), BF16),
        ],
        14, marks, step_bias, decay_log, skip_gain, hidden, halo, norm_gain, needed, conv_value,
        value_bias, mixer_gain, conv_shared,
    )
    messages = sent_along(device, 1)
    later, xbc = lax.optimization_barrier((later, xbc))
    later = later.reshape(MODEL, 2 * WIDE)
    z, e, yi = call(
        intra_kernel, blocks, PARTS[1], False,
        [
            SMEM, rows_of(MODEL), rows_of(MODEL), pair, rows_of(CHAN), lanes_of(24),
            whole((8, WIDE)),
        ],
        [(rows_of(WIDE), BF16)] * 3,
        [], 12, marks, normed, cotangent, later, xbc, rows, lanes,
    )
    y, mixed, part, sums, prefix = call(
        gated_kernel, blocks, PARTS[2], False,
        [
            SMEM, rows_of(WIDE), rows_of(WIDE), rows_of(WIDE), rows_of(CHAN), lanes_of(24), STATES,
            whole(STATE_DIMS), whole(STATE_DIMS), whole(STATE_DIMS), whole((8, WIDE)), pair,
        ],
        [
            (rows_of(WIDE), BF16), (rows_of(WIDE), BF16), (rows_of(MODEL), BF16),
            (lanes_of(2), F32), (whole((STATE, WIDE)), F32),
        ],
        [], 10, marks, yi, z, e, xbc, rows, states, *messages, lanes, later,
    )
    sums = jnp.sum(handed_to_all(sums, "tensor"), axis=0)

    own = tok // lax.axis_size("tensor")
    place = rank * own
    own_hidden = lax.dynamic_slice_in_dim(hidden, place, own, 0).astype(F32)
    own_cot = lax.dynamic_slice_in_dim(cotangent, place, own, 0).astype(F32)
    own_root = lax.rsqrt(lax.dynamic_slice_in_dim(sums[0], place, own, 0) / INNER + EPSILON)
    projected = lax.psum_scatter(part, "tensor", scatter_dimension=0, tiled=True).astype(F32)
    own_out = (own_hidden + own_root[:, None] * projected).astype(BF16)

    dy, dz, reaches, back_device, gains = call(
        gate_back_kernel, blocks, PARTS[3], True,
        [
            SMEM, rows_of(WIDE), rows_of(WIDE), rows_of(WIDE), rows_of(CHAN), lanes_of(24),
            lanes_of(2), whole((8, WIDE)),
        ],
        [
            (rows_of(WIDE), BF16), (rows_of(WIDE), BF16), (STATES, F32), (whole(STATE_DIMS), F32),
            (whole((8, WIDE)), F32),
        ],
        [pltpu.VMEM((STATE, WIDE), F32), pltpu.VMEM((8, WIDE), F32)],
        9, marks, y, z, e, xbc, rows, sums, lanes,
    )
    messages = sent_along(back_device, -1)
    dxi, dbc, stats, grad_out_t = call(
        intra_back_kernel, blocks, PARTS[4], False,
        [
            SMEM, rows_of(WIDE), rows_of(CHAN), lanes_of(24), STATES, whole((STATE, WIDE)),
            lanes_of(2), rows_of(WIDE), rows_of(MODEL), whole((8, WIDE)),
        ],
        [
            (rows_of(WIDE), BF16), (rows_of(WIDE), BF16), (lanes_of(16), F32),
            (whole((MODEL, WIDE)), F32),
        ],
        [], 13, marks, dy, xbc, rows, states, prefix, sums, mixed, cotangent, lanes,
    )
    dxi, own_out, messages = lax.optimization_barrier((dxi, own_out, messages))
    output = lax.all_gather(own_out, "tensor", axis=0, tiled=True)
    dn, big, pack, spill = call(
        input_back_kernel, blocks, PARTS[5], True,
        [
            SMEM, rows_of(MODEL), rows_of(MODEL), whole((16, MODEL)), rows_of(WIDE), rows_of(WIDE),
            rows_of(WIDE), rows_of(CHAN), rows_of(CHAN), rows_of(CHAN), ("before", CHAN),
            whole((8, CHAN)), lanes_of(24), lanes_of(16), STATES, whole((STATE, WIDE)), STATES,
            whole(STATE_DIMS), whole(STATE_DIMS), whole(STATE_DIMS), whole((8, MODEL)), pair, pair, whole((8, CHAN)),
            whole((16, BLOCK)), whole((MODEL, WIDE)), whole((8, WIDE)),
        ],
        [
            (rows_of(MODEL), BF16), (whole((MODEL, 4 * WIDE)), BF16),
            (whole((16, 4 * WIDE)), BF16), (whole((8, MODEL)), F32),
        ],
        [
            pltpu.VMEM((BLOCK + 8, CHAN), F32), pltpu.VMEM((BLOCK + 8, CHAN), F32),
            pltpu.VMEM((STATE, WIDE), F32), pltpu.VMEM((BLOCK, BLOCK), BF16),
            pltpu.VMEM((MODEL, 3 * WIDE), F32), pltpu.VMEM((8, CHAN), F32),
            pltpu.VMEM((16, BLOCK), F32), pltpu.VMEM((8, MODEL), F32),
        ],
        22, marks, hidden, normed, halo, dz, dxi, dbc, xbc, slope, cin, cin, cin_halo,
        rows, stats, states, prefix, reaches, *messages, gain, later, needed, taps, hcols, grad_out_t, gains,
    )
    arrived = passed_along(spill, "context", -1)
    end = dn[tok - 8 :].astype(F32) + arrived
    dn = lax.dynamic_update_slice(dn, end.astype(BF16), (tok - 8, 0))
    dn, output = lax.optimization_barrier((dn, output))
    own_dn = lax.psum_scatter(dn, "tensor", scatter_dimension=0, tiled=True)

    cells = lax.axis_size("shard") * lax.axis_size("context")
    big = jnp.concatenate(
        [
            big.reshape(cells, own_rows, 4 * WIDE),
            jnp.broadcast_to(pack[None], (cells,) + pack.shape),
        ],
        axis=1,
    )
    big = jnp.sum(lax.all_to_all(big, CELLS, 0, 0, tiled=False).astype(F32), axis=0)
    own_dn, big = lax.optimization_barrier((own_dn, big))
    own_dn = own_dn.astype(F32)
    scaling = lax.rsqrt(jnp.mean(own_hidden * own_hidden, axis=1, keepdims=True) + EPSILON)
    unit = own_hidden * scaling
    scaled = own_dn * norm_gain[None]
    own_grad = own_cot + scaling * (
        scaled - unit * jnp.mean(scaled * unit, axis=1, keepdims=True)
    )
    grad_hidden = lax.all_gather(own_grad.astype(BF16), "tensor", axis=0, tiled=True)

    small = big[own_rows : own_rows + 8] + big[own_rows + 8 :]
    big = big[:own_rows]
    chan = small[:5, :CHAN]
    norm_cells = small[5, :MODEL]
    grad_mixer = small[6, :INNER_DEV]
    grad_skip = jnp.sum(small[6, WIDE : WIDE + INNER_DEV].reshape(HEADS_DEV, HEADDIM), axis=1)
    grad_step_bias = jnp.sum(small[7, : 3 * WIDE].reshape(HEADS_DEV, WIDE), axis=1)
    grad_decay = jnp.stack(
        [jnp.sum(small[5, MODEL:]), jnp.sum(small[6, 2 * WIDE : 3 * WIDE]), jnp.sum(small[6, 3 * WIDE :])]
    )
    share = 2 * STATE // lax.axis_size("tensor")
    shared = jnp.concatenate([big[:, 2 * WIDE : 3 * WIDE], chan[:, WIDE:]], axis=0)
    shared = shared.reshape(own_rows + 5, -1, share).transpose(1, 0, 2)
    shared = shared.reshape(shared.shape[0], -1)
    count = shared.shape[1]
    final = jnp.concatenate(
        [shared, jnp.broadcast_to(norm_cells[None], (shared.shape[0], MODEL))], axis=1
    )
    final = padded(final, 2560).reshape(-1, 20, 128)
    final = jnp.sum(lax.all_to_all(final, "tensor", 0, 0, tiled=False), axis=0).reshape(-1)
    state_all = final[:count].reshape(own_rows + 5, share)
    return (
        output,
        grad_hidden,
        final[count : count + MODEL],
        big[:, :INNER_DEV],
        big[:, WIDE : WIDE + INNER_DEV],
        state_all[:own_rows],
        big[:, WIDE + INNER_DEV : WIDE + INNER_DEV + HEADS_DEV],
        chan[:4, :INNER_DEV],
        state_all[own_rows : own_rows + 4],
        chan[4, :INNER_DEV],
        state_all[own_rows + 4],
        grad_step_bias,
        grad_decay,
        grad_skip,
        grad_mixer,
        big[:, 3 * WIDE : 3 * WIDE + INNER_DEV].T,
    )


def solution(mesh):
    cells = P(CELLS, None)
    split = P(CELLS, "tensor")
    return jax.shard_map(
        body,
        mesh=mesh,
        in_specs=(
            cells, cells, P("shard", None), P(), split, split, split, split, P(None, "tensor"),
            P(None, "tensor"), P("tensor"), P("tensor"), P("tensor"), P("tensor"), P("tensor"),
            P("tensor"), P("tensor", CELLS),
        ),
        out_specs=(
            cells, cells, P(), split, split, split, split, P(None, "tensor"), P(None, "tensor"),
            P("tensor"), P("tensor"), P("tensor"), P("tensor"), P("tensor"), P("tensor"),
            P("tensor", CELLS),
        ),
        check_vma=False,
    )
```

```python
import jax
import jax.numpy as jnp
from jax import lax
from jax.experimental import pallas as pl
from jax.experimental.pallas import tpu as pltpu
from jax.sharding import PartitionSpec as P

MODEL = 768
INNER = 1536
HEADDIM = 64
STATE = 128
CONV = 4
BLOCK = 256
HEADS_DEV = 3
INNER_DEV = 192
WIDE = 256
CHAN = 512
EPSILON = 1e-05
F32 = jnp.float32
BF16 = jnp.bfloat16
CELLS = ("shard", "context")
VMEM_LIMIT = 60 * 1024 * 1024
PARTS = (2, 2, 2, 2, 1, 2)


def nn(a, b):
    return lax.dot_general(a, b, (((1,), (0,)), ((), ())), preferred_element_type=F32)


def nt(a, b):
    return lax.dot_general(a, b, (((1,), (1,)), ((), ())), preferred_element_type=F32)


def tn(a, b):
    return lax.dot_general(a, b, (((0,), (0,)), ((), ())), preferred_element_type=F32)


def iota(shape, dim):
    return lax.broadcasted_iota(jnp.int32, shape, dim)


def start_of(marks, pos):
    start = jnp.zeros_like(pos)
    for k in range(3):
        start = jnp.where(pos >= marks[k], marks[k], start)
    return start


def end_of(marks, pos):
    end = jnp.full_like(pos, marks[3])
    for k in (2, 1, 0):
        end = jnp.where(pos < marks[k], marks[k], end)
    return end


def running_sum(rows, ones):
    top = rows.astype(BF16)
    rest = rows - top.astype(F32)
    mid = rest.astype(BF16)
    low = (rest - mid.astype(F32)).astype(BF16)
    pieces = [top.astype(F32), mid.astype(F32), low.astype(F32), jnp.zeros((8, BLOCK), F32)]
    sums = nn(jnp.concatenate(pieces, axis=0).astype(BF16), ones)
    return sums[0:8] + sums[8:16] + sums[16:24]


def by_head(cols, width=WIDE):
    lane = iota((1, width), 1)
    return jnp.where(
        lane < HEADDIM,
        cols[0],
        jnp.where(lane < 2 * HEADDIM, cols[1], jnp.where(lane < 3 * HEADDIM, cols[2], 0.0)),
    )


def head_masks():
    row = iota((8, WIDE), 0)
    lane = iota((8, WIDE), 1)
    low = row * HEADDIM
    return jnp.where((lane >= low) & (lane < low + HEADDIM) & (row < HEADS_DEV), 1.0, 0.0)


def of_head(values, h):
    lane = iota((1, WIDE), 1)
    return jnp.where((lane >= h * HEADDIM) & (lane < (h + 1) * HEADDIM), values, 0.0)


def to_columns(rows):
    have = 8 * len(rows)
    stacked = jnp.concatenate(list(rows) + [jnp.zeros((128 - have, BLOCK), F32)], axis=0)
    return stacked.T


def column(cols, part, h):
    at = 8 * part + h
    return cols[:, at : at + 1]


def silu_parts(values):
    sig = 1.0 / (1.0 + jnp.exp(-values))
    return values * sig, sig * (1.0 + values * (1.0 - sig))


class Block:
    def __init__(self, marks, b):
        self.marks = marks
        self.start = marks[4] + b * BLOCK
        self.pos_row = self.start + iota((1, BLOCK), 1)
        self.pos_col = self.start + iota((BLOCK, 1), 0)

    def lead(self, cum):
        carried = start_of(self.marks, self.pos_row) < self.start
        return jnp.where(carried, jnp.exp(cum), 0.0)

    def tail_base(self, cum):
        last = cum[:, BLOCK - 1 : BLOCK]
        kept = end_of(self.marks, self.pos_row) > self.start + BLOCK - 1
        return jnp.where(kept, jnp.exp(last - cum), 0.0)

    def allowed(self):
        first = start_of(self.marks, self.pos_col)
        return (self.pos_row >= first) & (self.pos_row <= self.pos_col)

    def since_start(self):
        return self.pos_col - start_of(self.marks, self.pos_col)

    def until_end(self):
        return end_of(self.marks, self.pos_col) - self.pos_col


def decay_of(allowed, cum_col, cum_row):
    return jnp.exp(jnp.where(allowed, cum_col - cum_row, -1e30))


def message(state, decay):
    return jnp.concatenate([state, decay], axis=0)


def carried(messages):
    one, two, three = (m[...] for m in messages)

    def join(near, far):
        return near[:STATE] + near[STATE : STATE + 1] * far

    return join(one, join(two, three[:STATE]))


def last_by_lane(rows):
    return by_head([rows[h : h + 1, BLOCK - 1 : BLOCK] for h in range(HEADS_DEV)])


class At:
    def __init__(self, index, blocks, part, parts):
        self.index = index
        self.count = blocks
        self.part = part
        self.parts = parts
        self.can_be_first = part == 0
        self.can_be_last = part == parts - 1

    def when_first(self, do):
        if self.can_be_first:
            pl.when(self.index == 0)(do)

    def when_last(self, do):
        if self.can_be_last:
            pl.when(self.index == self.count - 1)(do)


def rows_of(width):
    return ("rows", width)


def lanes_of(count):
    return ("lanes", count)


def whole(dims):
    return ("whole", dims)


STATE_DIMS = (STATE + 8, WIDE)
STATES = ("states",)
SMEM = ("smem",)


def call(kernel, blocks, parts, down, ins, outs, scratch, micros, *args):
    steps = blocks // parts
    tile = parts * BLOCK

    def step(s):
        return steps - 1 - s if down else s

    def spec(kind):
        what = kind[0]
        if what == "smem":
            return pl.BlockSpec(memory_space=pltpu.SMEM)
        if what in ("rows", "tile"):
            return pl.BlockSpec((tile, kind[1]), lambda s, marks: (step(s), 0))
        if what == "lanes":
            return pl.BlockSpec((kind[1], tile), lambda s, marks: (0, step(s)))
        if what == "states":
            return pl.BlockSpec((parts,) + STATE_DIMS, lambda s, marks: (step(s), 0, 0))
        return pl.BlockSpec(kind[1], lambda s, marks: (0,) * len(kind[1]))

    def view(refs, n, kind, k):
        ref = refs[n]
        if kind[0] == "rows":
            return ref.at[pl.ds(k * BLOCK, BLOCK)]
        if kind[0] == "lanes":
            return ref.at[:, pl.ds(k * BLOCK, BLOCK)]
        if kind[0] == "states":
            return ref.at[pl.ds(k, 1)]
        return ref

    kinds = list(ins) + [kind for kind, _ in outs]

    def run(*refs):
        order = range(parts - 1, -1, -1) if down else range(parts)
        for k in order:
            at = At(step(pl.program_id(0)) * parts + k, blocks, k, parts)
            views = [view(refs, n, kind, k) for n, kind in enumerate(kinds)]
            kernel(at, *views, *refs[len(kinds) :])

    def dims(kind):
        what = kind[0]
        if what in ("rows", "tile"):
            return (blocks * BLOCK, kind[1])
        if what == "lanes":
            return (kind[1], blocks * BLOCK)
        if what == "states":
            return (blocks,) + STATE_DIMS
        return kind[1]

    return pl.pallas_call(
        run,
        grid_spec=pltpu.PrefetchScalarGridSpec(
            num_scalar_prefetch=1,
            grid=(steps,),
            in_specs=[spec(kind) for kind in ins[1:]],
            out_specs=[spec(kind) for kind, _ in outs],
            scratch_shapes=scratch,
        ),
        out_shape=[jax.ShapeDtypeStruct(dims(kind), dtype) for kind, dtype in outs],
        compiler_params=pltpu.CompilerParams(
            dimension_semantics=("arbitrary",), vmem_limit_bytes=VMEM_LIMIT
        ),
        cost_estimate=pl.CostEstimate(
            flops=int(micros * 1.15e9), bytes_accessed=int(micros * 1e6), transcendentals=0
        ),
    )(*args)


def project_kernel(
    at, marks, step_bias, decay_log, skip_gain, hidden, halo, norm_gain, weights, conv_value,
    value_bias, mixer_gain, conv_shared,
    normed_o, xbc_o, slope_o, cin_o, cin_halo_o, rows_o, state_o, device_o,
    gain, taps, lanes, hcols,
    ext, state, decay, upto,
):
    blk = Block(marks, at.index)
    wv = weights.at[:, 0:WIDE]
    ws = weights.at[:, WIDE : 2 * WIDE]

    @at.when_first
    def _():
        gain[...] = jnp.broadcast_to(norm_gain[...].reshape(1, MODEL), (8, MODEL))
        taps[...] = jnp.zeros_like(taps)
        taps[0:4, 0:INNER_DEV] = conv_value[...]
        taps[4:5, 0:INNER_DEV] = value_bias[...].reshape(1, INNER_DEV)
        taps[0:5, WIDE:] = conv_shared[...]
        lanes[...] = jnp.zeros_like(lanes)
        lanes[0:1, 0:INNER_DEV] = mixer_gain[...].reshape(1, INNER_DEV)
        lanes[1:2] = by_head([skip_gain[h] for h in range(HEADS_DEV)])
        row = iota((8, BLOCK), 0)
        bias = jnp.zeros((8, BLOCK), F32)
        rate = jnp.zeros((8, BLOCK), F32)
        for h in range(HEADS_DEV):
            bias = jnp.where(row == h, step_bias[h], bias)
            rate = jnp.where(row == h, decay_log[h], rate)
        hcols[0:8] = bias
        hcols[8:16] = jnp.where(row < HEADS_DEV, -jnp.exp(rate), 0.0)
        square = (BLOCK, BLOCK)
        upto[...] = jnp.where(iota(square, 0) <= iota(square, 1), 1.0, 0.0).astype(BF16)

    def norm(rows):
        rows = rows.astype(F32)
        scale = lax.rsqrt(jnp.mean(rows * rows, axis=1, keepdims=True) + EPSILON)
        return (rows * scale * gain[0:1]).astype(BF16)

    @at.when_first
    def _():
        ahead = norm(halo[...])
        into = jnp.concatenate([nn(ahead, wv[...]), nn(ahead, ws[...])], axis=1)
        into = into.astype(BF16).astype(F32)
        ext[0:8] = into[8:16]
        cin_halo_o[...] = into[8:16]
        state[...] = jnp.zeros_like(state)
        decay[...] = jnp.ones_like(decay)

    normed = norm(hidden[...])
    normed_o[...] = normed
    value_pre = nn(normed, wv[...])
    state_pre = nn(normed, ws[...])
    cin = jnp.concatenate([value_pre, state_pre], axis=1).astype(BF16)
    cin_o[...] = cin
    ext[8 : 8 + BLOCK] = cin.astype(F32)
    pre = taps[4:5] + taps[3:4] * ext[8 : 8 + BLOCK]
    since = blk.since_start()
    for lag in range(1, CONV):
        pre = pre + taps[3 - lag : 4 - lag] * (
            jnp.where(since >= lag, ext[8 - lag : 8 - lag + BLOCK], 0.0)
        )
    ext[0:8] = ext[BLOCK : BLOCK + 8]
    act, slope = silu_parts(pre)
    act = act.astype(BF16)
    xbc_o[...] = act
    slope_o[...] = slope.astype(BF16)

    raw = value_pre[:, 128:256].T[64:72] + hcols[0:8]
    dt = jnp.maximum(raw, 0.0) + jnp.log1p(jnp.exp(-jnp.abs(raw)))
    sig = 1.0 / (1.0 + jnp.exp(-raw))
    cum = running_sum(dt * hcols[8:16], upto[...])
    rows_o[0:8] = dt
    rows_o[8:16] = sig
    rows_o[16:24] = cum
    lead = blk.lead(cum)
    tail = blk.tail_base(cum) * dt
    cols = to_columns([tail])
    tail_lanes = by_head([column(cols, 0, h) for h in range(HEADS_DEV)])
    packed = (act[:, :WIDE].astype(F32) * tail_lanes).astype(BF16)
    fresh = tn(act[:, WIDE : WIDE + STATE], packed)
    last = last_by_lane(lead)
    state_o[0, 0:STATE] = state[...]
    state_o[0, STATE : STATE + 8] = decay[...]
    state[...] = last * state[...] + fresh
    decay[...] = last * decay[...]

    @at.when_last
    def _():
        device_o[...] = message(state[...], decay[...])


def intra_kernel(at, marks, normed, cot, weights, xbc, rows, lanes, z_o, e_o, yi_o):
    blk = Block(marks, at.index)
    z_o[...] = nn(normed[...], weights[:, 0:WIDE]).astype(BF16)
    e_o[...] = nn(cot[...], weights[:, WIDE : 2 * WIDE]).astype(BF16)
    dt = rows[0:8]
    cum = rows[16:24]
    x = xbc[:, :WIDE].astype(F32)
    scores = nt(xbc[:, WIDE + STATE :], xbc[:, WIDE : WIDE + STATE])
    allowed = blk.allowed()
    cols = to_columns([cum])
    out = lanes[1:2] * x
    for h in range(HEADS_DEV):
        decays = decay_of(allowed, column(cols, 0, h), cum[h : h + 1])
        mix = (scores * decays * dt[h : h + 1]).astype(BF16)
        out = out + nn(mix, of_head(x, h).astype(BF16))
    yi_o[...] = out.astype(BF16)


def gated_kernel(
    at, marks, yi, z, e, xbc, rows, states, one, two, three, lanes, weights,
    y_o, mixed_o, part_o, sums_o, prefix,
):
    @at.when_first
    def _():
        prefix[...] = carried((one, two, three))

    blk = Block(marks, at.index)
    lead = blk.lead(rows[16:24])
    cols = to_columns([lead])
    lead_lanes = by_head([column(cols, 0, h) for h in range(HEADS_DEV)])
    entering = states[0, 0:STATE] + states[0, STATE : STATE + 1] * prefix[...]
    y = yi[...].astype(F32) + lead_lanes * nn(xbc[:, WIDE + STATE :], entering.astype(BF16))
    y_o[...] = y.astype(BF16)
    gate, _ = silu_parts(z[...].astype(F32))
    v = y * gate
    mixed = (v * lanes[0:1]).astype(BF16)
    mixed_o[...] = mixed
    part_o[...] = nt(mixed, weights[:, WIDE : 2 * WIDE]).astype(BF16)
    row = iota((16, 2 * WIDE), 0)
    lane = iota((16, 2 * WIDE), 1)
    pick = jnp.where(((row == 0) & (lane < WIDE)) | ((row == 1) & (lane >= WIDE)), 1.0, 0.0)
    both = jnp.concatenate([v * v, e[...].astype(F32) * mixed.astype(F32)], axis=1)
    sums_o[...] = nt(pick.astype(BF16), both.astype(BF16))[0:2]


def gate_back_kernel(
    at, marks, y, z, e, xbc, rows, sums, lanes,
    dy_o, dz_o, reach_o, device_o, gains_o,
    carry, decay,
):
    blk = Block(marks, at.index)

    @at.when_last
    def _():
        carry[...] = jnp.zeros_like(carry)
        decay[...] = jnp.ones_like(decay)
        gains_o[...] = jnp.zeros_like(gains_o)

    lead = blk.lead(rows[16:24])
    root = lax.rsqrt(sums[0:1] / INNER + EPSILON)
    coef = sums[1:2] * root * root * root / INNER
    cols = to_columns([lead, jnp.broadcast_to(root, (8, BLOCK)), jnp.broadcast_to(coef, (8, BLOCK))])
    lead_lanes = by_head([column(cols, 0, h) for h in range(HEADS_DEV)])
    gate, slope = silu_parts(z[...].astype(F32))
    y_v = y[...].astype(F32)
    v = y_v * gate
    dm = column(cols, 1, 0) * e[...].astype(F32)
    dv = lanes[0:1] * dm - column(cols, 2, 0) * v
    dy = dv * gate
    dy_o[...] = dy.astype(BF16)
    dz_o[...] = (dv * y_v * slope).astype(BF16)
    x = xbc[:, :WIDE].astype(F32)
    gains_o[0:1] += jnp.sum(v * dm, axis=0, keepdims=True)
    gains_o[1:2] += jnp.sum(dy * x, axis=0, keepdims=True)
    reach = tn(xbc[:, WIDE + STATE :], (dy * lead_lanes).astype(BF16))
    last = last_by_lane(lead)
    reach_o[0, 0:STATE] = carry[...]
    reach_o[0, STATE : STATE + 8] = decay[...]
    carry[...] = last * carry[...] + reach
    decay[...] = last * decay[...]

    @at.when_first
    def _():
        device_o[...] = message(carry[...], decay[...])


def intra_back_kernel(
    at, marks, dy_r, xbc, rows, states, prefix, sums, mixed, cot, lanes,
    dxi_o, dbc_o, stats_o, grad_out_o,
):
    blk = Block(marks, at.index)

    @at.when_first
    def _():
        grad_out_o[...] = jnp.zeros_like(grad_out_o)

    dt = rows[0:8]
    cum = rows[16:24]
    lead = blk.lead(cum)
    root = lax.rsqrt(sums[0:1] / INNER + EPSILON)
    cols = to_columns([cum, lead, jnp.broadcast_to(root, (8, BLOCK))])
    lead_lanes = by_head([column(cols, 1, h) for h in range(HEADS_DEV)])
    rooted = (mixed[...].astype(F32) * column(cols, 2, 0)).astype(BF16)
    grad_out_o[...] += tn(cot[...], rooted)

    dy = dy_r[...].astype(F32)
    x_low = xbc[:, :WIDE]
    b_low = xbc[:, WIDE : WIDE + STATE]
    c_low = xbc[:, WIDE + STATE :]
    entering = states[0, 0:STATE] + states[0, STATE : STATE + 1] * prefix[...]
    held = entering.astype(BF16)
    masks = head_masks().astype(BF16)
    cross = nn(c_low, held)
    lead_grad = nt(masks, (dy * cross).astype(BF16))
    dc = nt((dy * lead_lanes).astype(BF16), held)
    scores = nt(c_low, b_low)
    allowed = blk.allowed()
    ds = jnp.zeros((BLOCK, BLOCK), F32)
    dx = lanes[1:2] * dy
    lane = iota((1, 128), 1)
    row8 = iota((8, 1), 0)
    row_sums = jnp.zeros((BLOCK, 128), F32)
    time_grad = jnp.zeros((8, BLOCK), F32)
    for h in range(HEADS_DEV):
        dt_h = dt[h : h + 1]
        dy_h = of_head(dy, h).astype(BF16)
        decays = decay_of(allowed, column(cols, 0, h), cum[h : h + 1])
        weighted = nt(dy_h, x_low) * decays
        ds = ds + weighted * dt_h
        scored = weighted * scores
        time_grad = time_grad + jnp.where(
            row8 == h, jnp.sum(scored, axis=0, keepdims=True), 0.0
        )
        row_sums = row_sums + jnp.where(
            lane == h, jnp.sum(scored * dt_h, axis=1, keepdims=True), 0.0
        )
        mix = (scores * decays * dt_h).astype(BF16)
        dx = dx + tn(mix, dy_h)
    ds_low = ds.astype(BF16)
    dxi_o[...] = dx.astype(BF16)
    dbc_o[:, 0:STATE] = tn(ds_low, c_low).astype(BF16)
    dbc_o[:, STATE : 2 * STATE] = (dc + nn(ds_low, b_low)).astype(BF16)
    stats_o[0:8] = time_grad
    stats_o[8:16] = row_sums.T[0:8] - time_grad * dt + lead_grad * lead


def input_back_kernel(
    at, marks, normed, halo, dz, dxi, dbc, xbc, slope, cin, cin_halo,
    rows, stats, states, prefix, reaches, one, two, three, gain, later, weights, taps, hcols,
    grad_out_t, gains,
    dn_o, early_o, late_o, pack_o, spill_o,
    ahead, suffix, since, wgrad, chan, steps, norm, low, wide,
):
    blk = Block(marks, at.index)

    @at.when_last
    def _():
        suffix[...] = carried((one, two, three))
        square = (BLOCK, BLOCK)
        since[...] = jnp.where(iota(square, 0) >= iota(square, 1), 1.0, 0.0).astype(BF16)
        wide[:, 0:WIDE] = later[:, 0:WIDE]
        wide[:, WIDE : 3 * WIDE] = weights[...]
        wgrad[...] = jnp.zeros_like(wgrad)
        chan[...] = jnp.zeros_like(chan)
        steps[...] = jnp.zeros_like(steps)
        norm[...] = jnp.zeros_like(norm)
        ahead[BLOCK : BLOCK + 8] = jnp.zeros((8, CHAN), F32)

    dt = rows[0:8]
    sig = rows[8:16]
    cum = rows[16:24]
    rate = hcols[8:16]
    lead = blk.lead(cum)
    tail_base = blk.tail_base(cum)
    tail = tail_base * dt
    cols = to_columns([tail])
    tail_lanes = by_head([column(cols, 0, h) for h in range(HEADS_DEV)])
    entering = states[0, 0:STATE] + states[0, STATE : STATE + 1] * prefix[...]
    leaving = reaches[0, 0:STATE] + reaches[0, STATE : STATE + 1] * suffix[...]
    leaving_low = leaving.astype(BF16)
    x = xbc[:, :WIDE].astype(F32)
    dpacked = nn(xbc[:, WIDE : WIDE + STATE], leaving_low)
    packed = (x * tail_lanes).astype(BF16)
    masks = head_masks()
    tail_grad = nt(masks.astype(BF16), (dpacked * x).astype(BF16))
    dx = dxi[...].astype(F32) + dpacked * tail_lanes
    db = dbc[:, 0:STATE].astype(F32) + nt(packed, leaving_low)
    dc = dbc[:, STATE : 2 * STATE].astype(F32)

    tail_term = tail_grad * tail
    state_term = jnp.sum(leaving * entering, axis=0, keepdims=True)
    last_term = jnp.sum(tail_term, axis=1, keepdims=True) + (
        jnp.sum(masks * state_term, axis=1, keepdims=True) * lead[:, BLOCK - 1 : BLOCK]
    )
    dcum = stats[8:16] - tail_term + jnp.where(iota((8, BLOCK), 1) == BLOCK - 1, last_term, 0.0)
    dla = running_sum(dcum, since[...])
    ddt = stats[0:8] + tail_grad * tail_base + dla * rate
    dstep = jnp.where(iota((8, 1), 0) < HEADS_DEV, ddt * sig, 0.0)
    steps[0:8] += dstep
    steps[8:16] += dla * dt * rate
    placed = jnp.concatenate(
        [jnp.zeros((64, BLOCK), F32), dstep, jnp.zeros((56, BLOCK), F32)], axis=0
    ).T

    dpre = jnp.concatenate([dx, db, dc], axis=1) * slope[...].astype(F32)
    inputs = cin[...].astype(F32)
    ahead[0:BLOCK] = dpre
    chan[4:5] += jnp.sum(dpre, axis=0, keepdims=True)
    chan[3:4] += jnp.sum(dpre * inputs, axis=0, keepdims=True)
    din = taps[3:4] * dpre
    left = blk.until_end()
    for lag in range(1, CONV):
        tap = 3 - lag
        later_dpre = jnp.where(left > lag, ahead[lag : lag + BLOCK], 0.0)
        chan[tap : tap + 1] += jnp.sum(later_dpre * inputs, axis=0, keepdims=True)
        din = din + taps[tap : tap + 1] * later_dpre
    ahead[BLOCK : BLOCK + 8] = dpre[0:8]
    mine = pl.ds(at.part * BLOCK, BLOCK)
    low[mine, 0:WIDE] = dz[...]
    low[mine, WIDE : WIDE + 128] = din[:, 0:128].astype(BF16)
    low[mine, WIDE + 128 : 2 * WIDE] = (din[:, 128:256] + placed).astype(BF16)
    low[mine, 2 * WIDE :] = din[:, WIDE:].astype(BF16)

    if at.part > 0:
        return

    all_low = low[...]
    normed_all = normed[...]
    dn = nt(all_low, wide[...])
    wgrad[...] += tn(normed_all, all_low)
    norm[0:1] += jnp.sum(dn * normed_all.astype(F32), axis=0, keepdims=True)
    dn_o[...] = dn.astype(BF16)

    @at.when_first
    def _():
        ahead[0:8] = jnp.zeros((8, CHAN), F32)
        ahead[8:16] = ahead[BLOCK : BLOCK + 8]
        ahead[16:24] = jnp.zeros((8, CHAN), F32)
        pos = blk.start - 8 + iota((8, 1), 0)
        left = end_of(marks, pos) - pos
        back = jnp.zeros((8, CHAN), F32)
        for lag in range(1, CONV):
            tap = 3 - lag
            same = (left > lag) & (pos >= 0)
            later_dpre = jnp.where(same, ahead[lag : lag + 8], 0.0)
            chan[tap : tap + 1] += jnp.sum(later_dpre * cin_halo[...], axis=0, keepdims=True)
            back = back + taps[tap : tap + 1] * later_dpre
        spilled = jnp.concatenate([jnp.zeros((8, CHAN), F32), back], axis=0).astype(BF16)
        given = nt(spilled, wide[:, WIDE:])
        spill_o[...] = given[8:16]
        rows_in = halo[...].astype(F32)
        scale = lax.rsqrt(jnp.mean(rows_in * rows_in, axis=1, keepdims=True) + EPSILON)
        normed_halo = (rows_in * scale * gain[0:1]).astype(BF16)
        norm[0:1] += jnp.sum(given * normed_halo.astype(F32), axis=0, keepdims=True)
        wgrad[:, WIDE:] += tn(normed_halo, spilled)
        early_o[...] = wgrad[:, WIDE:].astype(BF16)
        late_o[...] = jnp.concatenate(
            [wgrad[:, 0:INNER_DEV], grad_out_t[:, 0:INNER_DEV]], axis=1
        ).astype(BF16)
        gained = norm[0:1] / gain[0:1]

        def beside(left, right):
            return jnp.concatenate([left, right], axis=1)

        pack = jnp.concatenate(
            [
                chan[0:5],
                gained[:, 0:CHAN],
                beside(gained[:, CHAN:], gains[0:1]),
                beside(gains[1:2], steps[8:9]),
                beside(steps[9:10], steps[10:11]),
                beside(steps[0:1], steps[1:2]),
                beside(steps[2:3], jnp.zeros((1, WIDE), F32)),
                jnp.zeros((5, CHAN), F32),
            ],
            axis=0,
        )
        pack_o[...] = pack.astype(BF16)


def copied_kernel(source, out, done):
    copy = pltpu.make_async_copy(source, out, done)
    copy.start()
    copy.wait()


def copied(values):
    return pl.pallas_call(
        copied_kernel,
        in_specs=[pl.BlockSpec(memory_space=pl.ANY)],
        out_specs=pl.BlockSpec(memory_space=pl.ANY),
        out_shape=jax.ShapeDtypeStruct(values.shape, values.dtype),
        scratch_shapes=[pltpu.SemaphoreType.DMA],
        compiler_params=pltpu.CompilerParams(vmem_limit_bytes=VMEM_LIMIT),
        cost_estimate=pl.CostEstimate(flops=int(2e9), bytes_accessed=int(6e6), transcendentals=0),
    )(values)


def passed_along(values, axis, by):
    count = lax.axis_size(axis)
    pairs = [(i, i + by) for i in range(count) if 0 <= i + by < count]
    return lax.ppermute(values, axis, pairs)


def handed_to_all(values, axis):
    count = lax.axis_size(axis)
    return lax.all_to_all(
        jnp.broadcast_to(values[None], (count,) + values.shape), axis, 0, 0, tiled=False
    )


def sent_along(device, sign):
    return [passed_along(device, "context", sign * k) for k in (1, 2, 3)]


def padded(values, width):
    extra = width - values.shape[-1]
    return jnp.pad(values, [(0, 0)] * (values.ndim - 1) + [(0, extra)])


def body(
    hidden, cotangent, lengths, norm_gain, gate_proj, value_proj, state_proj, step_proj,
    conv_value, conv_state, value_bias, state_bias, step_bias, decay_log, skip_gain,
    mixer_gain, out_proj,
):
    tok = hidden.shape[0]
    blocks = tok // BLOCK
    ctx = lax.axis_index("context")
    rank = lax.axis_index("tensor")

    own_rows = state_proj.shape[0]
    first = jnp.concatenate(
        [state_proj.astype(F32), conv_state, state_bias[None], jnp.zeros((3, state_proj.shape[1]), F32)],
        axis=0,
    )
    first = handed_to_all(first, "tensor")
    first, lengths, gate_proj, out_proj, edge = lax.optimization_barrier(
        (first, lengths, gate_proj, out_proj, hidden[tok - 16 :])
    )
    first = first.transpose(1, 0, 2).reshape(own_rows + 8, 2 * STATE)
    conv_shared = first[own_rows : own_rows + 5]
    needed = jnp.concatenate(
        [
            value_proj, step_proj, jnp.zeros((own_rows, 61), BF16), first[:own_rows].astype(BF16),
        ],
        axis=1,
    )
    needed = handed_to_all(needed, CELLS).reshape(MODEL, 2 * WIDE)
    finishes = jnp.cumsum(lengths[0])
    marks = jnp.concatenate(
        [finishes, jnp.stack([ctx * tok, 0 * ctx, 0 * ctx, 0 * ctx])]
    )
    marks = marks.astype(jnp.int32)
    later = jnp.concatenate([padded(gate_proj, WIDE), padded(out_proj.T, WIDE)], axis=1)
    later = handed_to_all(later, CELLS)
    halo = passed_along(edge, "context", 1)

    pair = whole((MODEL, 2 * WIDE))
    normed, xbc, slope, cin, cin_halo, rows, states, device, gain, taps, lanes, hcols = call(
        project_kernel, blocks, PARTS[0], False,
        [
            SMEM, SMEM, SMEM, SMEM, rows_of(MODEL), whole((16, MODEL)), whole((MODEL,)), pair,
            whole((4, INNER_DEV)), whole((INNER_DEV,)), whole((INNER_DEV,)), whole((5, 2 * STATE)),
        ],
        [
            (rows_of(MODEL), BF16), (rows_of(CHAN), BF16), (rows_of(CHAN), BF16),
            (rows_of(CHAN), BF16), (whole((8, CHAN)), F32), (lanes_of(24), F32), (STATES, F32),
            (whole(STATE_DIMS), F32), (whole((8, MODEL)), F32), (whole((8, CHAN)), F32),
            (whole((8, WIDE)), F32), (whole((16, BLOCK)), F32),
        ],
        [
            pltpu.VMEM((BLOCK + 8, CHAN), F32), pltpu.VMEM((STATE, WIDE), F32),
            pltpu.VMEM((8, WIDE), F32), pltpu.VMEM((BLOCK, BLOCK), BF16),
        ],
        14, marks, step_bias, decay_log, skip_gain, hidden, halo, norm_gain, needed, conv_value,
        value_bias, mixer_gain, conv_shared,
    )
    messages = sent_along(device, 1)
    later, xbc = lax.optimization_barrier((later, xbc))
    later = later.reshape(MODEL, 2 * WIDE)
    z, e, yi = call(
        intra_kernel, blocks, PARTS[1], False,
        [
            SMEM, rows_of(MODEL), rows_of(MODEL), pair, rows_of(CHAN), lanes_of(24),
            whole((8, WIDE)),
        ],
        [(rows_of(WIDE), BF16)] * 3,
        [], 12, marks, normed, cotangent, later, xbc, rows, lanes,
    )
    y, mixed, part, sums, prefix = call(
        gated_kernel, blocks, PARTS[2], False,
        [
            SMEM, rows_of(WIDE), rows_of(WIDE), rows_of(WIDE), rows_of(CHAN), lanes_of(24), STATES,
            whole(STATE_DIMS), whole(STATE_DIMS), whole(STATE_DIMS), whole((8, WIDE)), pair,
        ],
        [
            (rows_of(WIDE), BF16), (rows_of(WIDE), BF16), (rows_of(MODEL), BF16),
            (lanes_of(2), F32), (whole((STATE, WIDE)), F32),
        ],
        [], 10, marks, yi, z, e, xbc, rows, states, *messages, lanes, later,
    )
    sums = jnp.sum(handed_to_all(sums, "tensor"), axis=0)

    ranks = lax.axis_size("tensor")
    own = tok // ranks
    place = rank * own
    own_hidden = lax.dynamic_slice_in_dim(hidden, place, own, 0).astype(F32)
    own_cot = lax.dynamic_slice_in_dim(cotangent, place, own, 0).astype(F32)
    own_root = lax.rsqrt(lax.dynamic_slice_in_dim(sums[0], place, own, 0) / INNER + EPSILON)
    projected = lax.psum_scatter(part, "tensor", scatter_dimension=0, tiled=True).astype(F32)
    own_out = (own_hidden + own_root[:, None] * projected).astype(BF16)

    dy, dz, reaches, back_device, gains = call(
        gate_back_kernel, blocks, PARTS[3], True,
        [
            SMEM, rows_of(WIDE), rows_of(WIDE), rows_of(WIDE), rows_of(CHAN), lanes_of(24),
            lanes_of(2), whole((8, WIDE)),
        ],
        [
            (rows_of(WIDE), BF16), (rows_of(WIDE), BF16), (STATES, F32), (whole(STATE_DIMS), F32),
            (whole((8, WIDE)), F32),
        ],
        [pltpu.VMEM((STATE, WIDE), F32), pltpu.VMEM((8, WIDE), F32)],
        9, marks, y, z, e, xbc, rows, sums, lanes,
    )
    messages = sent_along(back_device, -1)
    dxi, dbc, stats, grad_out_t = call(
        intra_back_kernel, blocks, PARTS[4], False,
        [
            SMEM, rows_of(WIDE), rows_of(CHAN), lanes_of(24), STATES, whole((STATE, WIDE)),
            lanes_of(2), rows_of(WIDE), rows_of(MODEL), whole((8, WIDE)),
        ],
        [
            (rows_of(WIDE), BF16), (rows_of(WIDE), BF16), (lanes_of(16), F32),
            (whole((MODEL, WIDE)), F32),
        ],
        [], 13, marks, dy, xbc, rows, states, prefix, sums, mixed, cotangent, lanes,
    )
    dxi, own_out, messages = lax.optimization_barrier((dxi, own_out, messages))
    output = lax.all_gather(own_out, "tensor", axis=0, tiled=True)
    dn, early, late, pack, spill = call(
        input_back_kernel, blocks, PARTS[5], True,
        [
            SMEM, ("tile", MODEL), whole((16, MODEL)), rows_of(WIDE), rows_of(WIDE),
            rows_of(WIDE), rows_of(CHAN), rows_of(CHAN), rows_of(CHAN),
            whole((8, CHAN)), lanes_of(24), lanes_of(16), STATES, whole((STATE, WIDE)), STATES,
            whole(STATE_DIMS), whole(STATE_DIMS), whole(STATE_DIMS), whole((8, MODEL)), pair, pair,
            whole((8, CHAN)), whole((16, BLOCK)), whole((MODEL, WIDE)), whole((8, WIDE)),
        ],
        [
            (("tile", MODEL), BF16), (whole((MODEL, CHAN)), BF16),
            (whole((MODEL, 2 * INNER_DEV)), BF16), (whole((16, CHAN)), BF16),
            (whole((8, MODEL)), F32),
        ],
        [
            pltpu.VMEM((BLOCK + 8, CHAN), F32), pltpu.VMEM((STATE, WIDE), F32),
            pltpu.VMEM((BLOCK, BLOCK), BF16), pltpu.VMEM((MODEL, 3 * WIDE), F32),
            pltpu.VMEM((8, CHAN), F32), pltpu.VMEM((16, BLOCK), F32), pltpu.VMEM((8, MODEL), F32),
            pltpu.VMEM((PARTS[5] * BLOCK, 3 * WIDE), BF16), pltpu.VMEM((MODEL, 3 * WIDE), BF16),
        ],
        22, marks, normed, halo, dz, dxi, dbc, xbc, slope, cin, cin_halo,
        rows, stats, states, prefix, reaches, *messages, gain, later, needed, taps, hcols,
        grad_out_t, gains,
    )

    arrived = passed_along(spill, "context", -1)
    end = dn[tok - 8 :].astype(F32) + arrived
    dn = lax.dynamic_update_slice(dn, end.astype(BF16), (tok - 8, 0))
    dn, output = lax.optimization_barrier((dn, output))
    own_dn = lax.psum_scatter(dn, "tensor", scatter_dimension=0, tiled=True)

    cells = lax.axis_size("shard") * lax.axis_size("context")
    early = jnp.concatenate(
        [
            early.reshape(cells, own_rows, CHAN),
            jnp.broadcast_to(pack[None], (cells,) + pack.shape),
        ],
        axis=1,
    )
    early = lax.all_to_all(early, CELLS, 0, 0, tiled=False)
    output = copied(output)
    own_dn, early, output = lax.optimization_barrier((own_dn, early, output))
    early = jnp.sum(early.astype(F32), axis=0)
    own_dn = own_dn.astype(F32)
    scaling = lax.rsqrt(jnp.mean(own_hidden * own_hidden, axis=1, keepdims=True) + EPSILON)
    unit = own_hidden * scaling
    scaled = own_dn * norm_gain[None]
    own_grad = own_cot + scaling * (
        scaled - unit * jnp.mean(scaled * unit, axis=1, keepdims=True)
    )
    own_grad, late = lax.optimization_barrier((own_grad.astype(BF16), late))
    grad_hidden = lax.all_gather(own_grad, "tensor", axis=0, tiled=True)
    late = lax.all_to_all(late.reshape(cells, own_rows, 2 * INNER_DEV), CELLS, 0, 0, tiled=False)
    late = jnp.sum(late.astype(F32), axis=0)

    big, small = early[:own_rows], early[own_rows:]
    chan = small[:5]
    norm_cells = jnp.concatenate([small[5], small[6, :WIDE]])
    grad_mixer = small[6, WIDE : WIDE + INNER_DEV]
    grad_skip = jnp.sum(small[7, :INNER_DEV].reshape(HEADS_DEV, HEADDIM), axis=1)
    lines = jnp.sum(small[7:11].reshape(8, WIDE), axis=1)
    grad_decay = lines[1:4]
    grad_step_bias = lines[4:7]
    share = 2 * STATE // lax.axis_size("tensor")
    shared = jnp.concatenate([big[:, WIDE:], chan[:, WIDE:]], axis=0)
    shared = shared.reshape(own_rows + 5, -1, share).transpose(1, 0, 2)
    shared = shared.reshape(shared.shape[0], -1)
    count = shared.shape[1]
    final = jnp.concatenate(
        [shared, jnp.broadcast_to(norm_cells[None], (shared.shape[0], MODEL))], axis=1
    )
    final = padded(final, 2560).reshape(-1, 20, 128)
    final = jnp.sum(lax.all_to_all(final, "tensor", 0, 0, tiled=False), axis=0).reshape(-1)
    state_all = final[:count].reshape(own_rows + 5, share)
    return (
        output,
        grad_hidden,
        final[count : count + MODEL],
        late[:, :INNER_DEV],
        big[:, :INNER_DEV],
        state_all[:own_rows],
        big[:, INNER_DEV : INNER_DEV + HEADS_DEV],
        chan[:4, :INNER_DEV],
        state_all[own_rows : own_rows + 4],
        chan[4, :INNER_DEV],
        state_all[own_rows + 4],
        grad_step_bias,
        grad_decay,
        grad_skip,
        grad_mixer,
        late[:, INNER_DEV:].T,
    )


def solution(mesh):
    cells = P(CELLS, None)
    split = P(CELLS, "tensor")
    return jax.shard_map(
        body,
        mesh=mesh,
        in_specs=(
            cells, cells, P("shard", None), P(), split, split, split, split, P(None, "tensor"),
            P(None, "tensor"), P("tensor"), P("tensor"), P("tensor"), P("tensor"), P("tensor"),
            P("tensor"), P("tensor", CELLS),
        ),
        out_specs=(
            cells, cells, P(), split, split, split, split, P(None, "tensor"), P(None, "tensor"),
            P("tensor"), P("tensor"), P("tensor"), P("tensor"), P("tensor"), P("tensor"),
            P("tensor", CELLS),
        ),
        check_vma=False,
    )
```

```python
import jax
import jax.numpy as jnp
from jax import lax
from jax.experimental import pallas as pl
from jax.experimental.pallas import tpu as pltpu
from jax.sharding import PartitionSpec as P

MODEL = 768
INNER = 1536
HEADDIM = 64
STATE = 128
CONV = 4
BLOCK = 256
HEADS_DEV = 3
INNER_DEV = 192
WIDE = 256
CHAN = 512
EPSILON = 1e-05
F32 = jnp.float32
BF16 = jnp.bfloat16
CELLS = ("shard", "context")
VMEM_LIMIT = 60 * 1024 * 1024
PARTS = (2, 2, 2, 2, 1, 2)


def nn(a, b):
    return lax.dot_general(a, b, (((1,), (0,)), ((), ())), preferred_element_type=F32)


def nt(a, b):
    return lax.dot_general(a, b, (((1,), (1,)), ((), ())), preferred_element_type=F32)


def tn(a, b):
    return lax.dot_general(a, b, (((0,), (0,)), ((), ())), preferred_element_type=F32)


def iota(shape, dim):
    return lax.broadcasted_iota(jnp.int32, shape, dim)


def start_of(marks, pos):
    start = jnp.zeros_like(pos)
    for k in range(3):
        start = jnp.where(pos >= marks[k], marks[k], start)
    return start


def end_of(marks, pos):
    end = jnp.full_like(pos, marks[3])
    for k in (2, 1, 0):
        end = jnp.where(pos < marks[k], marks[k], end)
    return end


def running_sum(rows, ones):
    top = rows.astype(BF16)
    rest = rows - top.astype(F32)
    mid = rest.astype(BF16)
    low = (rest - mid.astype(F32)).astype(BF16)
    pieces = [top.astype(F32), mid.astype(F32), low.astype(F32), jnp.zeros((8, BLOCK), F32)]
    sums = nn(jnp.concatenate(pieces, axis=0).astype(BF16), ones)
    return sums[0:8] + sums[8:16] + sums[16:24]


def by_head(cols, width=WIDE):
    lane = iota((1, width), 1)
    return jnp.where(
        lane < HEADDIM,
        cols[0],
        jnp.where(lane < 2 * HEADDIM, cols[1], jnp.where(lane < 3 * HEADDIM, cols[2], 0.0)),
    )


def head_masks():
    row = iota((8, WIDE), 0)
    lane = iota((8, WIDE), 1)
    low = row * HEADDIM
    return jnp.where((lane >= low) & (lane < low + HEADDIM) & (row < HEADS_DEV), 1.0, 0.0)


def of_head(values, h):
    lane = iota((1, WIDE), 1)
    return jnp.where((lane >= h * HEADDIM) & (lane < (h + 1) * HEADDIM), values, 0.0)


def to_columns(rows):
    have = 8 * len(rows)
    stacked = jnp.concatenate(list(rows) + [jnp.zeros((128 - have, BLOCK), F32)], axis=0)
    return stacked.T


def column(cols, part, h):
    at = 8 * part + h
    return cols[:, at : at + 1]


def silu_parts(values):
    sig = 1.0 / (1.0 + jnp.exp(-values))
    return values * sig, sig * (1.0 + values * (1.0 - sig))


class Block:
    def __init__(self, marks, b):
        self.marks = marks
        self.start = marks[4] + b * BLOCK
        self.pos_row = self.start + iota((1, BLOCK), 1)
        self.pos_col = self.start + iota((BLOCK, 1), 0)

    def lead(self, cum):
        carried = start_of(self.marks, self.pos_row) < self.start
        return jnp.where(carried, jnp.exp(cum), 0.0)

    def tail_base(self, cum):
        last = cum[:, BLOCK - 1 : BLOCK]
        kept = end_of(self.marks, self.pos_row) > self.start + BLOCK - 1
        return jnp.where(kept, jnp.exp(last - cum), 0.0)

    def allowed(self):
        first = start_of(self.marks, self.pos_col)
        return (self.pos_row >= first) & (self.pos_row <= self.pos_col)

    def since_start(self):
        return self.pos_col - start_of(self.marks, self.pos_col)

    def until_end(self):
        return end_of(self.marks, self.pos_col) - self.pos_col


def decay_of(allowed, cum_col, cum_row):
    return jnp.exp(jnp.where(allowed, cum_col - cum_row, -1e30))


def message(state, decay):
    return jnp.concatenate([state, decay], axis=0)


def carried(messages):
    one, two, three = (m[...] for m in messages)

    def join(near, far):
        return near[:STATE] + near[STATE : STATE + 1] * far

    return join(one, join(two, three[:STATE]))


def last_by_lane(rows):
    return by_head([rows[h : h + 1, BLOCK - 1 : BLOCK] for h in range(HEADS_DEV)])


class At:
    def __init__(self, index, blocks, part, parts):
        self.index = index
        self.count = blocks
        self.part = part
        self.parts = parts
        self.can_be_first = part == 0
        self.can_be_last = part == parts - 1

    def when_first(self, do):
        if self.can_be_first:
            pl.when(self.index == 0)(do)

    def when_last(self, do):
        if self.can_be_last:
            pl.when(self.index == self.count - 1)(do)


def rows_of(width):
    return ("rows", width)


def lanes_of(count):
    return ("lanes", count)


def whole(dims):
    return ("whole", dims)


STATE_DIMS = (STATE + 8, WIDE)
STATES = ("states",)
SMEM = ("smem",)


def call(kernel, blocks, parts, down, ins, outs, scratch, micros, *args):
    steps = blocks // parts
    tile = parts * BLOCK

    def step(s):
        return steps - 1 - s if down else s

    def spec(kind):
        what = kind[0]
        if what == "smem":
            return pl.BlockSpec(memory_space=pltpu.SMEM)
        if what in ("rows", "tile"):
            return pl.BlockSpec((tile, kind[1]), lambda s: (step(s), 0))
        if what == "lanes":
            return pl.BlockSpec((kind[1], tile), lambda s: (0, step(s)))
        if what == "states":
            return pl.BlockSpec((parts,) + STATE_DIMS, lambda s: (step(s), 0, 0))
        return pl.BlockSpec(kind[1], lambda s: (0,) * len(kind[1]))

    def view(refs, n, kind, k):
        ref = refs[n]
        if kind[0] == "rows":
            return ref.at[pl.ds(k * BLOCK, BLOCK)]
        if kind[0] == "lanes":
            return ref.at[:, pl.ds(k * BLOCK, BLOCK)]
        if kind[0] == "states":
            return ref.at[pl.ds(k, 1)]
        return ref

    kinds = list(ins) + [kind for kind, _ in outs]

    def run(*refs):
        order = range(parts - 1, -1, -1) if down else range(parts)
        for k in order:
            at = At(step(pl.program_id(0)) * parts + k, blocks, k, parts)
            views = [view(refs, n, kind, k) for n, kind in enumerate(kinds)]
            kernel(at, *views, *refs[len(kinds) :])

    def dims(kind):
        what = kind[0]
        if what in ("rows", "tile"):
            return (blocks * BLOCK, kind[1])
        if what == "lanes":
            return (kind[1], blocks * BLOCK)
        if what == "states":
            return (blocks,) + STATE_DIMS
        return kind[1]

    return pl.pallas_call(
        run,
        grid=(steps,),
        in_specs=[spec(kind) for kind in ins],
        out_specs=[spec(kind) for kind, _ in outs],
        scratch_shapes=scratch,
        out_shape=[jax.ShapeDtypeStruct(dims(kind), dtype) for kind, dtype in outs],
        compiler_params=pltpu.CompilerParams(
            dimension_semantics=("arbitrary",), vmem_limit_bytes=VMEM_LIMIT
        ),
        cost_estimate=pl.CostEstimate(
            flops=int(micros * 1.15e9), bytes_accessed=int(micros * 1e6), transcendentals=0
        ),
    )(*args)


def project_kernel(
    at, marks, step_bias, decay_log, skip_gain, hidden, halo, norm_gain, weights, conv_value,
    value_bias, mixer_gain, conv_shared,
    normed_o, xbc_o, slope_o, cin_o, cin_halo_o, rows_o, state_o, device_o,
    gain, taps, lanes, hcols,
    ext, state, decay, upto,
):
    blk = Block(marks, at.index)
    wv = weights.at[:, 0:WIDE]
    ws = weights.at[:, WIDE : 2 * WIDE]

    @at.when_first
    def _():
        gain[...] = jnp.broadcast_to(norm_gain[...].reshape(1, MODEL), (8, MODEL))
        taps[...] = jnp.zeros_like(taps)
        taps[0:4, 0:INNER_DEV] = conv_value[...]
        taps[4:5, 0:INNER_DEV] = value_bias[...].reshape(1, INNER_DEV)
        taps[0:5, WIDE:] = conv_shared[...]
        lanes[...] = jnp.zeros_like(lanes)
        lanes[0:1, 0:INNER_DEV] = mixer_gain[...].reshape(1, INNER_DEV)
        lanes[1:2] = by_head([skip_gain[h] for h in range(HEADS_DEV)])
        row = iota((8, BLOCK), 0)
        bias = jnp.zeros((8, BLOCK), F32)
        rate = jnp.zeros((8, BLOCK), F32)
        for h in range(HEADS_DEV):
            bias = jnp.where(row == h, step_bias[h], bias)
            rate = jnp.where(row == h, decay_log[h], rate)
        hcols[0:8] = bias
        hcols[8:16] = jnp.where(row < HEADS_DEV, -jnp.exp(rate), 0.0)
        square = (BLOCK, BLOCK)
        upto[...] = jnp.where(iota(square, 0) <= iota(square, 1), 1.0, 0.0).astype(BF16)

    def norm(rows):
        rows = rows.astype(F32)
        scale = lax.rsqrt(jnp.mean(rows * rows, axis=1, keepdims=True) + EPSILON)
        return (rows * scale * gain[0:1]).astype(BF16)

    @at.when_first
    def _():
        ahead = norm(halo[...])
        into = jnp.concatenate([nn(ahead, wv[...]), nn(ahead, ws[...])], axis=1)
        into = into.astype(BF16).astype(F32)
        ext[0:8] = into[8:16]
        cin_halo_o[...] = into[8:16]
        state[...] = jnp.zeros_like(state)
        decay[...] = jnp.ones_like(decay)

    normed = norm(hidden[...])
    normed_o[...] = normed
    value_pre = nn(normed, wv[...])
    state_pre = nn(normed, ws[...])
    cin = jnp.concatenate([value_pre, state_pre], axis=1).astype(BF16)
    cin_o[...] = cin
    ext[8 : 8 + BLOCK] = cin.astype(F32)
    pre = taps[4:5] + taps[3:4] * ext[8 : 8 + BLOCK]
    since = blk.since_start()
    for lag in range(1, CONV):
        pre = pre + taps[3 - lag : 4 - lag] * (
            jnp.where(since >= lag, ext[8 - lag : 8 - lag + BLOCK], 0.0)
        )
    ext[0:8] = ext[BLOCK : BLOCK + 8]
    act, slope = silu_parts(pre)
    act = act.astype(BF16)
    xbc_o[...] = act
    slope_o[...] = slope.astype(BF16)

    raw = value_pre[:, 128:256].T[64:72] + hcols[0:8]
    dt = jnp.maximum(raw, 0.0) + jnp.log1p(jnp.exp(-jnp.abs(raw)))
    sig = 1.0 / (1.0 + jnp.exp(-raw))
    cum = running_sum(dt * hcols[8:16], upto[...])
    rows_o[0:8] = dt
    rows_o[8:16] = sig
    rows_o[16:24] = cum
    lead = blk.lead(cum)
    tail = blk.tail_base(cum) * dt
    cols = to_columns([tail])
    tail_lanes = by_head([column(cols, 0, h) for h in range(HEADS_DEV)])
    packed = (act[:, :WIDE].astype(F32) * tail_lanes).astype(BF16)
    fresh = tn(act[:, WIDE : WIDE + STATE], packed)
    last = last_by_lane(lead)
    state_o[0, 0:STATE] = state[...]
    state_o[0, STATE : STATE + 8] = decay[...]
    state[...] = last * state[...] + fresh
    decay[...] = last * decay[...]

    @at.when_last
    def _():
        device_o[...] = message(state[...], decay[...])


def intra_kernel(at, marks, normed, cot, weights, xbc, rows, lanes, z_o, e_o, yi_o):
    blk = Block(marks, at.index)
    z_o[...] = nn(normed[...], weights[:, 0:WIDE]).astype(BF16)
    e_o[...] = nn(cot[...], weights[:, WIDE : 2 * WIDE]).astype(BF16)
    dt = rows[0:8]
    cum = rows[16:24]
    x = xbc[:, :WIDE].astype(F32)
    scores = nt(xbc[:, WIDE + STATE :], xbc[:, WIDE : WIDE + STATE])
    allowed = blk.allowed()
    cols = to_columns([cum])
    out = lanes[1:2] * x
    for h in range(HEADS_DEV):
        decays = decay_of(allowed, column(cols, 0, h), cum[h : h + 1])
        mix = (scores * decays * dt[h : h + 1]).astype(BF16)
        out = out + nn(mix, of_head(x, h).astype(BF16))
    yi_o[...] = out.astype(BF16)


def gated_kernel(
    at, marks, yi, z, e, xbc, rows, states, one, two, three, lanes, weights,
    y_o, mixed_o, part_o, sums_o, prefix,
):
    @at.when_first
    def _():
        prefix[...] = carried((one, two, three))

    blk = Block(marks, at.index)
    lead = blk.lead(rows[16:24])
    cols = to_columns([lead])
    lead_lanes = by_head([column(cols, 0, h) for h in range(HEADS_DEV)])
    entering = states[0, 0:STATE] + states[0, STATE : STATE + 1] * prefix[...]
    y = yi[...].astype(F32) + lead_lanes * nn(xbc[:, WIDE + STATE :], entering.astype(BF16))
    y_o[...] = y.astype(BF16)
    gate, _ = silu_parts(z[...].astype(F32))
    v = y * gate
    mixed = (v * lanes[0:1]).astype(BF16)
    mixed_o[...] = mixed
    part_o[...] = nt(mixed, weights[:, WIDE : 2 * WIDE]).astype(BF16)
    row = iota((16, 2 * WIDE), 0)
    lane = iota((16, 2 * WIDE), 1)
    pick = jnp.where(((row == 0) & (lane < WIDE)) | ((row == 1) & (lane >= WIDE)), 1.0, 0.0)
    both = jnp.concatenate([v * v, e[...].astype(F32) * mixed.astype(F32)], axis=1)
    sums_o[...] = nt(pick.astype(BF16), both.astype(BF16))[0:2]


def gate_back_kernel(
    at, marks, y, z, e, xbc, rows, sums, lanes,
    dy_o, dz_o, reach_o, device_o, gains_o,
    carry, decay,
):
    blk = Block(marks, at.index)

    @at.when_last
    def _():
        carry[...] = jnp.zeros_like(carry)
        decay[...] = jnp.ones_like(decay)
        gains_o[...] = jnp.zeros_like(gains_o)

    lead = blk.lead(rows[16:24])
    root = lax.rsqrt(sums[0:1] / INNER + EPSILON)
    coef = sums[1:2] * root * root * root / INNER
    cols = to_columns([lead, jnp.broadcast_to(root, (8, BLOCK)), jnp.broadcast_to(coef, (8, BLOCK))])
    lead_lanes = by_head([column(cols, 0, h) for h in range(HEADS_DEV)])
    gate, slope = silu_parts(z[...].astype(F32))
    y_v = y[...].astype(F32)
    v = y_v * gate
    dm = column(cols, 1, 0) * e[...].astype(F32)
    dv = lanes[0:1] * dm - column(cols, 2, 0) * v
    dy = dv * gate
    dy_o[...] = dy.astype(BF16)
    dz_o[...] = (dv * y_v * slope).astype(BF16)
    x = xbc[:, :WIDE].astype(F32)
    gains_o[0:1] += jnp.sum(v * dm, axis=0, keepdims=True)
    gains_o[1:2] += jnp.sum(dy * x, axis=0, keepdims=True)
    reach = tn(xbc[:, WIDE + STATE :], (dy * lead_lanes).astype(BF16))
    last = last_by_lane(lead)
    reach_o[0, 0:STATE] = carry[...]
    reach_o[0, STATE : STATE + 8] = decay[...]
    carry[...] = last * carry[...] + reach
    decay[...] = last * decay[...]

    @at.when_first
    def _():
        device_o[...] = message(carry[...], decay[...])


def intra_back_kernel(
    at, marks, dy_r, xbc, rows, states, prefix, sums, mixed, cot, lanes,
    dxi_o, dbc_o, stats_o, grad_out_o,
):
    blk = Block(marks, at.index)

    @at.when_first
    def _():
        grad_out_o[...] = jnp.zeros_like(grad_out_o)

    dt = rows[0:8]
    cum = rows[16:24]
    lead = blk.lead(cum)
    root = lax.rsqrt(sums[0:1] / INNER + EPSILON)
    cols = to_columns([cum, lead, jnp.broadcast_to(root, (8, BLOCK))])
    lead_lanes = by_head([column(cols, 1, h) for h in range(HEADS_DEV)])
    rooted = (mixed[...].astype(F32) * column(cols, 2, 0)).astype(BF16)
    grad_out_o[...] += tn(cot[...], rooted)

    dy = dy_r[...].astype(F32)
    x_low = xbc[:, :WIDE]
    b_low = xbc[:, WIDE : WIDE + STATE]
    c_low = xbc[:, WIDE + STATE :]
    entering = states[0, 0:STATE] + states[0, STATE : STATE + 1] * prefix[...]
    held = entering.astype(BF16)
    masks = head_masks().astype(BF16)
    cross = nn(c_low, held)
    lead_grad = nt(masks, (dy * cross).astype(BF16))
    dc = nt((dy * lead_lanes).astype(BF16), held)
    scores = nt(c_low, b_low)
    allowed = blk.allowed()
    ds = jnp.zeros((BLOCK, BLOCK), F32)
    dx = lanes[1:2] * dy
    lane = iota((1, 128), 1)
    row8 = iota((8, 1), 0)
    row_sums = jnp.zeros((BLOCK, 128), F32)
    time_grad = jnp.zeros((8, BLOCK), F32)
    for h in range(HEADS_DEV):
        dt_h = dt[h : h + 1]
        dy_h = of_head(dy, h).astype(BF16)
        decays = decay_of(allowed, column(cols, 0, h), cum[h : h + 1])
        weighted = nt(dy_h, x_low) * decays
        ds = ds + weighted * dt_h
        scored = weighted * scores
        time_grad = time_grad + jnp.where(
            row8 == h, jnp.sum(scored, axis=0, keepdims=True), 0.0
        )
        row_sums = row_sums + jnp.where(
            lane == h, jnp.sum(scored * dt_h, axis=1, keepdims=True), 0.0
        )
        mix = (scores * decays * dt_h).astype(BF16)
        dx = dx + tn(mix, dy_h)
    ds_low = ds.astype(BF16)
    dxi_o[...] = dx.astype(BF16)
    dbc_o[:, 0:STATE] = tn(ds_low, c_low).astype(BF16)
    dbc_o[:, STATE : 2 * STATE] = (dc + nn(ds_low, b_low)).astype(BF16)
    stats_o[0:8] = time_grad
    stats_o[8:16] = row_sums.T[0:8] - time_grad * dt + lead_grad * lead


def input_back_kernel(
    at, marks, normed, halo, dz, dxi, dbc, xbc, slope, cin, cin_halo,
    rows, stats, states, prefix, reaches, one, two, three, gain, later, weights, taps, hcols,
    grad_out_t, gains,
    dn_o, early_o, late_o, pack_o, spill_o,
    ahead, suffix, since, wgrad, chan, steps, norm, low, wide,
):
    blk = Block(marks, at.index)

    @at.when_last
    def _():
        suffix[...] = carried((one, two, three))
        square = (BLOCK, BLOCK)
        since[...] = jnp.where(iota(square, 0) >= iota(square, 1), 1.0, 0.0).astype(BF16)
        wide[:, 0:WIDE] = later[:, 0:WIDE]
        wide[:, WIDE : 3 * WIDE] = weights[...]
        wgrad[...] = jnp.zeros_like(wgrad)
        chan[...] = jnp.zeros_like(chan)
        steps[...] = jnp.zeros_like(steps)
        norm[...] = jnp.zeros_like(norm)
        ahead[BLOCK : BLOCK + 8] = jnp.zeros((8, CHAN), F32)

    dt = rows[0:8]
    sig = rows[8:16]
    cum = rows[16:24]
    rate = hcols[8:16]
    lead = blk.lead(cum)
    tail_base = blk.tail_base(cum)
    tail = tail_base * dt
    cols = to_columns([tail])
    tail_lanes = by_head([column(cols, 0, h) for h in range(HEADS_DEV)])
    entering = states[0, 0:STATE] + states[0, STATE : STATE + 1] * prefix[...]
    leaving = reaches[0, 0:STATE] + reaches[0, STATE : STATE + 1] * suffix[...]
    leaving_low = leaving.astype(BF16)
    x = xbc[:, :WIDE].astype(F32)
    dpacked = nn(xbc[:, WIDE : WIDE + STATE], leaving_low)
    packed = (x * tail_lanes).astype(BF16)
    masks = head_masks()
    tail_grad = nt(masks.astype(BF16), (dpacked * x).astype(BF16))
    dx = dxi[...].astype(F32) + dpacked * tail_lanes
    db = dbc[:, 0:STATE].astype(F32) + nt(packed, leaving_low)
    dc = dbc[:, STATE : 2 * STATE].astype(F32)

    tail_term = tail_grad * tail
    state_term = jnp.sum(leaving * entering, axis=0, keepdims=True)
    last_term = jnp.sum(tail_term, axis=1, keepdims=True) + (
        jnp.sum(masks * state_term, axis=1, keepdims=True) * lead[:, BLOCK - 1 : BLOCK]
    )
    dcum = stats[8:16] - tail_term + jnp.where(iota((8, BLOCK), 1) == BLOCK - 1, last_term, 0.0)
    dla = running_sum(dcum, since[...])
    ddt = stats[0:8] + tail_grad * tail_base + dla * rate
    dstep = jnp.where(iota((8, 1), 0) < HEADS_DEV, ddt * sig, 0.0)
    steps[0:8] += dstep
    steps[8:16] += dla * dt * rate
    placed = jnp.concatenate(
        [jnp.zeros((64, BLOCK), F32), dstep, jnp.zeros((56, BLOCK), F32)], axis=0
    ).T

    dpre = jnp.concatenate([dx, db, dc], axis=1) * slope[...].astype(F32)
    inputs = cin[...].astype(F32)
    ahead[0:BLOCK] = dpre
    chan[4:5] += jnp.sum(dpre, axis=0, keepdims=True)
    chan[3:4] += jnp.sum(dpre * inputs, axis=0, keepdims=True)
    din = taps[3:4] * dpre
    left = blk.until_end()
    for lag in range(1, CONV):
        tap = 3 - lag
        later_dpre = jnp.where(left > lag, ahead[lag : lag + BLOCK], 0.0)
        chan[tap : tap + 1] += jnp.sum(later_dpre * inputs, axis=0, keepdims=True)
        din = din + taps[tap : tap + 1] * later_dpre
    ahead[BLOCK : BLOCK + 8] = dpre[0:8]
    mine = pl.ds(at.part * BLOCK, BLOCK)
    low[mine, 0:WIDE] = dz[...]
    low[mine, WIDE : WIDE + 128] = din[:, 0:128].astype(BF16)
    low[mine, WIDE + 128 : 2 * WIDE] = (din[:, 128:256] + placed).astype(BF16)
    low[mine, 2 * WIDE :] = din[:, WIDE:].astype(BF16)

    if at.part > 0:
        return

    all_low = low[...]
    normed_all = normed[...]
    dn = nt(all_low, wide[...])
    wgrad[...] += tn(normed_all, all_low)
    norm[0:1] += jnp.sum(dn * normed_all.astype(F32), axis=0, keepdims=True)
    dn_o[...] = dn.astype(BF16)

    @at.when_first
    def _():
        ahead[0:8] = jnp.zeros((8, CHAN), F32)
        ahead[8:16] = ahead[BLOCK : BLOCK + 8]
        ahead[16:24] = jnp.zeros((8, CHAN), F32)
        pos = blk.start - 8 + iota((8, 1), 0)
        left = end_of(marks, pos) - pos
        back = jnp.zeros((8, CHAN), F32)
        for lag in range(1, CONV):
            tap = 3 - lag
            same = (left > lag) & (pos >= 0)
            later_dpre = jnp.where(same, ahead[lag : lag + 8], 0.0)
            chan[tap : tap + 1] += jnp.sum(later_dpre * cin_halo[...], axis=0, keepdims=True)
            back = back + taps[tap : tap + 1] * later_dpre
        spilled = jnp.concatenate([jnp.zeros((8, CHAN), F32), back], axis=0).astype(BF16)
        given = nt(spilled, wide[:, WIDE:])
        spill_o[...] = given[8:16]
        rows_in = halo[...].astype(F32)
        scale = lax.rsqrt(jnp.mean(rows_in * rows_in, axis=1, keepdims=True) + EPSILON)
        normed_halo = (rows_in * scale * gain[0:1]).astype(BF16)
        norm[0:1] += jnp.sum(given * normed_halo.astype(F32), axis=0, keepdims=True)
        wgrad[:, WIDE:] += tn(normed_halo, spilled)
        early_o[...] = wgrad[:, WIDE:].astype(BF16)
        late_o[...] = jnp.concatenate(
            [wgrad[:, 0:INNER_DEV], grad_out_t[:, 0:INNER_DEV]], axis=1
        ).astype(BF16)
        gained = norm[0:1] / gain[0:1]

        def beside(left, right):
            return jnp.concatenate([left, right], axis=1)

        pack = jnp.concatenate(
            [
                chan[0:5],
                gained[:, 0:CHAN],
                beside(gained[:, CHAN:], gains[0:1]),
                beside(gains[1:2], steps[8:9]),
                beside(steps[9:10], steps[10:11]),
                beside(steps[0:1], steps[1:2]),
                beside(steps[2:3], jnp.zeros((1, WIDE), F32)),
                jnp.zeros((5, CHAN), F32),
            ],
            axis=0,
        )
        pack_o[...] = pack.astype(BF16)


def copied_kernel(source, out):
    out[...] = source[...]


def copied(values):
    rows, width = values.shape
    block = pl.BlockSpec((rows // 4, width), lambda s: (s, 0))
    return pl.pallas_call(
        copied_kernel,
        grid=(4,),
        in_specs=[block],
        out_specs=block,
        out_shape=jax.ShapeDtypeStruct(values.shape, values.dtype),
        compiler_params=pltpu.CompilerParams(
            dimension_semantics=("arbitrary",), vmem_limit_bytes=VMEM_LIMIT
        ),
        cost_estimate=pl.CostEstimate(flops=int(3e9), bytes_accessed=int(6e6), transcendentals=0),
    )(values)


def passed_along(values, axis, by):
    count = lax.axis_size(axis)
    pairs = [(i, i + by) for i in range(count) if 0 <= i + by < count]
    return lax.ppermute(values, axis, pairs)


def handed_to_all(values, axis):
    count = lax.axis_size(axis)
    return lax.all_to_all(
        jnp.broadcast_to(values[None], (count,) + values.shape), axis, 0, 0, tiled=False
    )


def sent_along(device, sign):
    return [passed_along(device, "context", sign * k) for k in (1, 2, 3)]


def padded(values, width):
    extra = width - values.shape[-1]
    return jnp.pad(values, [(0, 0)] * (values.ndim - 1) + [(0, extra)])


def body(
    hidden, cotangent, lengths, norm_gain, gate_proj, value_proj, state_proj, step_proj,
    conv_value, conv_state, value_bias, state_bias, step_bias, decay_log, skip_gain,
    mixer_gain, out_proj,
):
    tok = hidden.shape[0]
    blocks = tok // BLOCK
    ctx = lax.axis_index("context")
    rank = lax.axis_index("tensor")

    own_rows = state_proj.shape[0]
    first = jnp.concatenate(
        [state_proj.astype(F32), conv_state, state_bias[None], jnp.zeros((3, state_proj.shape[1]), F32)],
        axis=0,
    )
    first = handed_to_all(first, "tensor")
    first, lengths, gate_proj, out_proj, edge = lax.optimization_barrier(
        (first, lengths, gate_proj, out_proj, hidden[tok - 16 :])
    )
    first = first.transpose(1, 0, 2).reshape(own_rows + 8, 2 * STATE)
    conv_shared = first[own_rows : own_rows + 5]
    needed = jnp.concatenate(
        [
            value_proj, step_proj, jnp.zeros((own_rows, 61), BF16), first[:own_rows].astype(BF16),
        ],
        axis=1,
    )
    needed = handed_to_all(needed, CELLS).reshape(MODEL, 2 * WIDE)
    finishes = jnp.cumsum(lengths[0])
    marks = jnp.concatenate(
        [finishes, jnp.stack([ctx * tok, 0 * ctx, 0 * ctx, 0 * ctx])]
    )
    marks = marks.astype(jnp.int32)
    later = jnp.concatenate([padded(gate_proj, WIDE), padded(out_proj.T, WIDE)], axis=1)
    later = handed_to_all(later, CELLS)
    halo = passed_along(edge, "context", 1)

    pair = whole((MODEL, 2 * WIDE))
    normed, xbc, slope, cin, cin_halo, rows, states, device, gain, taps, lanes, hcols = call(
        project_kernel, blocks, PARTS[0], False,
        [
            SMEM, SMEM, SMEM, SMEM, rows_of(MODEL), whole((16, MODEL)), whole((MODEL,)), pair,
            whole((4, INNER_DEV)), whole((INNER_DEV,)), whole((INNER_DEV,)), whole((5, 2 * STATE)),
        ],
        [
            (rows_of(MODEL), BF16), (rows_of(CHAN), BF16), (rows_of(CHAN), BF16),
            (rows_of(CHAN), BF16), (whole((8, CHAN)), F32), (lanes_of(24), F32), (STATES, F32),
            (whole(STATE_DIMS), F32), (whole((8, MODEL)), F32), (whole((8, CHAN)), F32),
            (whole((8, WIDE)), F32), (whole((16, BLOCK)), F32),
        ],
        [
            pltpu.VMEM((BLOCK + 8, CHAN), F32), pltpu.VMEM((STATE, WIDE), F32),
            pltpu.VMEM((8, WIDE), F32), pltpu.VMEM((BLOCK, BLOCK), BF16),
        ],
        14, marks, step_bias, decay_log, skip_gain, hidden, halo, norm_gain, needed, conv_value,
        value_bias, mixer_gain, conv_shared,
    )
    messages = sent_along(device, 1)
    later, xbc = lax.optimization_barrier((later, xbc))
    later = later.reshape(MODEL, 2 * WIDE)
    z, e, yi = call(
        intra_kernel, blocks, PARTS[1], False,
        [
            SMEM, rows_of(MODEL), rows_of(MODEL), pair, rows_of(CHAN), lanes_of(24),
            whole((8, WIDE)),
        ],
        [(rows_of(WIDE), BF16)] * 3,
        [], 12, marks, normed, cotangent, later, xbc, rows, lanes,
    )
    y, mixed, part, sums, prefix = call(
        gated_kernel, blocks, PARTS[2], False,
        [
            SMEM, rows_of(WIDE), rows_of(WIDE), rows_of(WIDE), rows_of(CHAN), lanes_of(24), STATES,
            whole(STATE_DIMS), whole(STATE_DIMS), whole(STATE_DIMS), whole((8, WIDE)), pair,
        ],
        [
            (rows_of(WIDE), BF16), (rows_of(WIDE), BF16), (rows_of(MODEL), BF16),
            (lanes_of(2), F32), (whole((STATE, WIDE)), F32),
        ],
        [], 10, marks, yi, z, e, xbc, rows, states, *messages, lanes, later,
    )
    sums = jnp.sum(handed_to_all(sums, "tensor"), axis=0)

    ranks = lax.axis_size("tensor")
    own = tok // ranks
    place = rank * own
    own_hidden = lax.dynamic_slice_in_dim(hidden, place, own, 0).astype(F32)
    own_cot = lax.dynamic_slice_in_dim(cotangent, place, own, 0).astype(F32)
    own_root = lax.rsqrt(lax.dynamic_slice_in_dim(sums[0], place, own, 0) / INNER + EPSILON)
    projected = lax.psum_scatter(part, "tensor", scatter_dimension=0, tiled=True).astype(F32)
    own_out = (own_hidden + own_root[:, None] * projected).astype(BF16)

    dy, dz, reaches, back_device, gains = call(
        gate_back_kernel, blocks, PARTS[3], True,
        [
            SMEM, rows_of(WIDE), rows_of(WIDE), rows_of(WIDE), rows_of(CHAN), lanes_of(24),
            lanes_of(2), whole((8, WIDE)),
        ],
        [
            (rows_of(WIDE), BF16), (rows_of(WIDE), BF16), (STATES, F32), (whole(STATE_DIMS), F32),
            (whole((8, WIDE)), F32),
        ],
        [pltpu.VMEM((STATE, WIDE), F32), pltpu.VMEM((8, WIDE), F32)],
        9, marks, y, z, e, xbc, rows, sums, lanes,
    )
    messages = sent_along(back_device, -1)
    dxi, dbc, stats, grad_out_t = call(
        intra_back_kernel, blocks, PARTS[4], False,
        [
            SMEM, rows_of(WIDE), rows_of(CHAN), lanes_of(24), STATES, whole((STATE, WIDE)),
            lanes_of(2), rows_of(WIDE), rows_of(MODEL), whole((8, WIDE)),
        ],
        [
            (rows_of(WIDE), BF16), (rows_of(WIDE), BF16), (lanes_of(16), F32),
            (whole((MODEL, WIDE)), F32),
        ],
        [], 13, marks, dy, xbc, rows, states, prefix, sums, mixed, cotangent, lanes,
    )
    dxi, own_out, messages = lax.optimization_barrier((dxi, own_out, messages))
    output = lax.all_gather(own_out, "tensor", axis=0, tiled=True)
    dn, early, late, pack, spill = call(
        input_back_kernel, blocks, PARTS[5], True,
        [
            SMEM, ("tile", MODEL), whole((16, MODEL)), rows_of(WIDE), rows_of(WIDE),
            rows_of(WIDE), rows_of(CHAN), rows_of(CHAN), rows_of(CHAN),
            whole((8, CHAN)), lanes_of(24), lanes_of(16), STATES, whole((STATE, WIDE)), STATES,
            whole(STATE_DIMS), whole(STATE_DIMS), whole(STATE_DIMS), whole((8, MODEL)), pair, pair,
            whole((8, CHAN)), whole((16, BLOCK)), whole((MODEL, WIDE)), whole((8, WIDE)),
        ],
        [
            (("tile", MODEL), BF16), (whole((MODEL, CHAN)), BF16),
            (whole((MODEL, 2 * INNER_DEV)), BF16), (whole((16, CHAN)), BF16),
            (whole((8, MODEL)), F32),
        ],
        [
            pltpu.VMEM((BLOCK + 8, CHAN), F32), pltpu.VMEM((STATE, WIDE), F32),
            pltpu.VMEM((BLOCK, BLOCK), BF16), pltpu.VMEM((MODEL, 3 * WIDE), F32),
            pltpu.VMEM((8, CHAN), F32), pltpu.VMEM((16, BLOCK), F32), pltpu.VMEM((8, MODEL), F32),
            pltpu.VMEM((PARTS[5] * BLOCK, 3 * WIDE), BF16), pltpu.VMEM((MODEL, 3 * WIDE), BF16),
        ],
        22, marks, normed, halo, dz, dxi, dbc, xbc, slope, cin, cin_halo,
        rows, stats, states, prefix, reaches, *messages, gain, later, needed, taps, hcols,
        grad_out_t, gains,
    )

    arrived = passed_along(spill, "context", -1)
    end = dn[tok - 8 :].astype(F32) + arrived
    dn = lax.dynamic_update_slice(dn, end.astype(BF16), (tok - 8, 0))
    dn, output = lax.optimization_barrier((dn, output))
    own_dn = lax.psum_scatter(dn, "tensor", scatter_dimension=0, tiled=True)

    cells = lax.axis_size("shard") * lax.axis_size("context")
    early = jnp.concatenate(
        [
            early.reshape(cells, own_rows, CHAN),
            jnp.broadcast_to(pack[None], (cells,) + pack.shape),
        ],
        axis=1,
    )
    early = lax.all_to_all(early, CELLS, 0, 0, tiled=False)
    output = copied(output)
    own_dn, early, output = lax.optimization_barrier((own_dn, early, output))
    early = jnp.sum(early.astype(F32), axis=0)
    own_dn = own_dn.astype(F32)
    scaling = lax.rsqrt(jnp.mean(own_hidden * own_hidden, axis=1, keepdims=True) + EPSILON)
    unit = own_hidden * scaling
    scaled = own_dn * norm_gain[None]
    own_grad = own_cot + scaling * (
        scaled - unit * jnp.mean(scaled * unit, axis=1, keepdims=True)
    )
    own_grad, late = lax.optimization_barrier((own_grad.astype(BF16), late))
    grad_hidden = lax.all_gather(own_grad, "tensor", axis=0, tiled=True)
    late = lax.all_to_all(late.reshape(cells, own_rows, 2 * INNER_DEV), CELLS, 0, 0, tiled=False)
    late = jnp.sum(late.astype(F32), axis=0)

    big, small = early[:own_rows], early[own_rows:]
    chan = small[:5]
    norm_cells = jnp.concatenate([small[5], small[6, :WIDE]])
    grad_mixer = small[6, WIDE : WIDE + INNER_DEV]
    grad_skip = jnp.sum(small[7, :INNER_DEV].reshape(HEADS_DEV, HEADDIM), axis=1)
    lines = jnp.sum(small[7:11].reshape(8, WIDE), axis=1)
    grad_decay = lines[1:4]
    grad_step_bias = lines[4:7]
    share = 2 * STATE // lax.axis_size("tensor")
    shared = jnp.concatenate([big[:, WIDE:], chan[:, WIDE:]], axis=0)
    shared = shared.reshape(own_rows + 5, -1, share).transpose(1, 0, 2)
    shared = shared.reshape(shared.shape[0], -1)
    count = shared.shape[1]
    final = jnp.concatenate(
        [shared, jnp.broadcast_to(norm_cells[None], (shared.shape[0], MODEL))], axis=1
    )
    final = padded(final, 2560).reshape(-1, 20, 128)
    final = jnp.sum(lax.all_to_all(final, "tensor", 0, 0, tiled=False), axis=0).reshape(-1)
    state_all = final[:count].reshape(own_rows + 5, share)
    return (
        output,
        grad_hidden,
        final[count : count + MODEL],
        late[:, :INNER_DEV],
        big[:, :INNER_DEV],
        state_all[:own_rows],
        big[:, INNER_DEV : INNER_DEV + HEADS_DEV],
        chan[:4, :INNER_DEV],
        state_all[own_rows : own_rows + 4],
        chan[4, :INNER_DEV],
        state_all[own_rows + 4],
        grad_step_bias,
        grad_decay,
        grad_skip,
        grad_mixer,
        late[:, INNER_DEV:].T,
    )


def solution(mesh):
    cells = P(CELLS, None)
    split = P(CELLS, "tensor")
    return jax.shard_map(
        body,
        mesh=mesh,
        in_specs=(
            cells, cells, P("shard", None), P(), split, split, split, split, P(None, "tensor"),
            P(None, "tensor"), P("tensor"), P("tensor"), P("tensor"), P("tensor"), P("tensor"),
            P("tensor"), P("tensor", CELLS),
        ),
        out_specs=(
            cells, cells, P(), split, split, split, split, P(None, "tensor"), P(None, "tensor"),
            P("tensor"), P("tensor"), P("tensor"), P("tensor"), P("tensor"), P("tensor"),
            P("tensor", CELLS),
        ),
        check_vma=False,
    )
```

```python
import jax
import jax.numpy as jnp
from jax import lax
from jax.experimental import pallas as pl
from jax.experimental.pallas import tpu as pltpu
from jax.sharding import PartitionSpec as P

MODEL = 768
INNER = 1536
HEADDIM = 64
STATE = 128
CONV = 4
BLOCK = 256
HEADS_DEV = 3
INNER_DEV = 192
WIDE = 256
CHAN = 512
EPSILON = 1e-05
F32 = jnp.float32
BF16 = jnp.bfloat16
CELLS = ("shard", "context")
VMEM_LIMIT = 60 * 1024 * 1024
PARTS = (2, 2, 4, 2, 1, 2)


def nn(a, b):
    return lax.dot_general(a, b, (((1,), (0,)), ((), ())), preferred_element_type=F32)


def nt(a, b):
    return lax.dot_general(a, b, (((1,), (1,)), ((), ())), preferred_element_type=F32)


def tn(a, b):
    return lax.dot_general(a, b, (((0,), (0,)), ((), ())), preferred_element_type=F32)


def iota(shape, dim):
    return lax.broadcasted_iota(jnp.int32, shape, dim)


def start_of(marks, pos):
    start = jnp.zeros_like(pos)
    for k in range(3):
        start = jnp.where(pos >= marks[k], marks[k], start)
    return start


def end_of(marks, pos):
    end = jnp.full_like(pos, marks[3])
    for k in (2, 1, 0):
        end = jnp.where(pos < marks[k], marks[k], end)
    return end


def running_sum(rows, ones):
    top = rows.astype(BF16)
    rest = rows - top.astype(F32)
    mid = rest.astype(BF16)
    low = (rest - mid.astype(F32)).astype(BF16)
    pieces = [top.astype(F32), mid.astype(F32), low.astype(F32), jnp.zeros((8, BLOCK), F32)]
    sums = nn(jnp.concatenate(pieces, axis=0).astype(BF16), ones)
    return sums[0:8] + sums[8:16] + sums[16:24]


def by_head(cols, width=WIDE):
    lane = iota((1, width), 1)
    return jnp.where(
        lane < HEADDIM,
        cols[0],
        jnp.where(lane < 2 * HEADDIM, cols[1], jnp.where(lane < 3 * HEADDIM, cols[2], 0.0)),
    )


def head_masks():
    row = iota((8, WIDE), 0)
    lane = iota((8, WIDE), 1)
    low = row * HEADDIM
    return jnp.where((lane >= low) & (lane < low + HEADDIM) & (row < HEADS_DEV), 1.0, 0.0)


def of_head(values, h):
    lane = iota((1, WIDE), 1)
    return jnp.where((lane >= h * HEADDIM) & (lane < (h + 1) * HEADDIM), values, 0.0)


def to_columns(rows):
    have = 8 * len(rows)
    stacked = jnp.concatenate(list(rows) + [jnp.zeros((128 - have, BLOCK), F32)], axis=0)
    return stacked.T


def column(cols, part, h):
    at = 8 * part + h
    return cols[:, at : at + 1]


def silu_parts(values):
    sig = 1.0 / (1.0 + jnp.exp(-values))
    return values * sig, sig * (1.0 + values * (1.0 - sig))


class Block:
    def __init__(self, marks, b):
        self.marks = marks
        self.start = marks[4] + b * BLOCK
        self.pos_row = self.start + iota((1, BLOCK), 1)
        self.pos_col = self.start + iota((BLOCK, 1), 0)

    def lead(self, cum):
        carried = start_of(self.marks, self.pos_row) < self.start
        return jnp.where(carried, jnp.exp(cum), 0.0)

    def tail_base(self, cum):
        last = cum[:, BLOCK - 1 : BLOCK]
        kept = end_of(self.marks, self.pos_row) > self.start + BLOCK - 1
        return jnp.where(kept, jnp.exp(last - cum), 0.0)

    def allowed(self):
        first = start_of(self.marks, self.pos_col)
        return (self.pos_row >= first) & (self.pos_row <= self.pos_col)

    def since_start(self):
        return self.pos_col - start_of(self.marks, self.pos_col)

    def until_end(self):
        return end_of(self.marks, self.pos_col) - self.pos_col


def decay_of(allowed, cum_col, cum_row):
    return jnp.exp(jnp.where(allowed, cum_col - cum_row, -1e30))


def message(state, decay):
    return jnp.concatenate([state, decay], axis=0)


def carried(messages):
    one, two, three = (m[...] for m in messages)

    def join(near, far):
        return near[:STATE] + near[STATE : STATE + 1] * far

    return join(one, join(two, three[:STATE]))


def last_by_lane(rows):
    return by_head([rows[h : h + 1, BLOCK - 1 : BLOCK] for h in range(HEADS_DEV)])


class At:
    def __init__(self, index, blocks, part, parts):
        self.index = index
        self.count = blocks
        self.part = part
        self.parts = parts
        self.can_be_first = part == 0
        self.can_be_last = part == parts - 1

    def when_first(self, do):
        if self.can_be_first:
            pl.when(self.index == 0)(do)

    def when_last(self, do):
        if self.can_be_last:
            pl.when(self.index == self.count - 1)(do)


def rows_of(width):
    return ("rows", width)


def lanes_of(count):
    return ("lanes", count)


def whole(dims):
    return ("whole", dims)


STATE_DIMS = (STATE + 8, WIDE)
STATES = ("states",)
SMEM = ("smem",)


def call(kernel, blocks, parts, down, ins, outs, scratch, micros, *args):
    steps = blocks // parts
    tile = parts * BLOCK

    def step(s):
        return steps - 1 - s if down else s

    def spec(kind):
        what = kind[0]
        if what == "smem":
            return pl.BlockSpec(memory_space=pltpu.SMEM)
        if what in ("rows", "tile"):
            return pl.BlockSpec((tile, kind[1]), lambda s: (step(s), 0))
        if what == "lanes":
            return pl.BlockSpec((kind[1], tile), lambda s: (0, step(s)))
        if what == "states":
            return pl.BlockSpec((parts,) + STATE_DIMS, lambda s: (step(s), 0, 0))
        return pl.BlockSpec(kind[1], lambda s: (0,) * len(kind[1]))

    def view(refs, n, kind, k):
        ref = refs[n]
        if kind[0] == "rows":
            return ref.at[pl.ds(k * BLOCK, BLOCK)]
        if kind[0] == "lanes":
            return ref.at[:, pl.ds(k * BLOCK, BLOCK)]
        if kind[0] == "states":
            return ref.at[pl.ds(k, 1)]
        return ref

    kinds = list(ins) + [kind for kind, _ in outs]

    def run(*refs):
        order = range(parts - 1, -1, -1) if down else range(parts)
        for k in order:
            at = At(step(pl.program_id(0)) * parts + k, blocks, k, parts)
            views = [view(refs, n, kind, k) for n, kind in enumerate(kinds)]
            kernel(at, *views, *refs[len(kinds) :])

    def dims(kind):
        what = kind[0]
        if what in ("rows", "tile"):
            return (blocks * BLOCK, kind[1])
        if what == "lanes":
            return (kind[1], blocks * BLOCK)
        if what == "states":
            return (blocks,) + STATE_DIMS
        return kind[1]

    return pl.pallas_call(
        run,
        grid=(steps,),
        in_specs=[spec(kind) for kind in ins],
        out_specs=[spec(kind) for kind, _ in outs],
        scratch_shapes=scratch,
        out_shape=[jax.ShapeDtypeStruct(dims(kind), dtype) for kind, dtype in outs],
        compiler_params=pltpu.CompilerParams(
            dimension_semantics=("arbitrary",), vmem_limit_bytes=VMEM_LIMIT
        ),
        cost_estimate=pl.CostEstimate(
            flops=int(micros * 1.15e9), bytes_accessed=int(micros * 1e6), transcendentals=0
        ),
    )(*args)


def project_kernel(
    at, marks, step_bias, decay_log, skip_gain, hidden, halo, norm_gain, weights, conv_value,
    value_bias, mixer_gain, conv_shared,
    normed_o, xbc_o, slope_o, cin_o, cin_halo_o, rows_o, state_o, device_o,
    gain, taps, lanes, hcols,
    ext, state, decay, upto,
):
    blk = Block(marks, at.index)
    wv = weights.at[:, 0:WIDE]
    ws = weights.at[:, WIDE : 2 * WIDE]

    @at.when_first
    def _():
        gain[...] = jnp.broadcast_to(norm_gain[...].reshape(1, MODEL), (8, MODEL))
        taps[...] = jnp.zeros_like(taps)
        taps[0:4, 0:INNER_DEV] = conv_value[...]
        taps[4:5, 0:INNER_DEV] = value_bias[...].reshape(1, INNER_DEV)
        taps[0:5, WIDE:] = conv_shared[...]
        lanes[...] = jnp.zeros_like(lanes)
        lanes[0:1, 0:INNER_DEV] = mixer_gain[...].reshape(1, INNER_DEV)
        lanes[1:2] = by_head([skip_gain[h] for h in range(HEADS_DEV)])
        row = iota((8, BLOCK), 0)
        bias = jnp.zeros((8, BLOCK), F32)
        rate = jnp.zeros((8, BLOCK), F32)
        for h in range(HEADS_DEV):
            bias = jnp.where(row == h, step_bias[h], bias)
            rate = jnp.where(row == h, decay_log[h], rate)
        hcols[0:8] = bias
        hcols[8:16] = jnp.where(row < HEADS_DEV, -jnp.exp(rate), 0.0)
        square = (BLOCK, BLOCK)
        upto[...] = jnp.where(iota(square, 0) <= iota(square, 1), 1.0, 0.0).astype(BF16)

    def norm(rows):
        rows = rows.astype(F32)
        scale = lax.rsqrt(jnp.mean(rows * rows, axis=1, keepdims=True) + EPSILON)
        return (rows * scale * gain[0:1]).astype(BF16)

    @at.when_first
    def _():
        ahead = norm(halo[...])
        into = jnp.concatenate([nn(ahead, wv[...]), nn(ahead, ws[...])], axis=1)
        into = into.astype(BF16).astype(F32)
        ext[0:8] = into[8:16]
        cin_halo_o[...] = into[8:16]
        state[...] = jnp.zeros_like(state)
        decay[...] = jnp.ones_like(decay)

    normed = norm(hidden[...])
    normed_o[...] = normed
    value_pre = nn(normed, wv[...])
    state_pre = nn(normed, ws[...])
    cin = jnp.concatenate([value_pre, state_pre], axis=1).astype(BF16)
    cin_o[...] = cin
    ext[8 : 8 + BLOCK] = cin.astype(F32)
    pre = taps[4:5] + taps[3:4] * ext[8 : 8 + BLOCK]
    since = blk.since_start()
    for lag in range(1, CONV):
        pre = pre + taps[3 - lag : 4 - lag] * (
            jnp.where(since >= lag, ext[8 - lag : 8 - lag + BLOCK], 0.0)
        )
    ext[0:8] = ext[BLOCK : BLOCK + 8]
    act, slope = silu_parts(pre)
    act = act.astype(BF16)
    xbc_o[...] = act
    slope_o[...] = slope.astype(BF16)

    raw = value_pre[:, 128:256].T[64:72] + hcols[0:8]
    dt = jnp.maximum(raw, 0.0) + jnp.log1p(jnp.exp(-jnp.abs(raw)))
    sig = 1.0 / (1.0 + jnp.exp(-raw))
    cum = running_sum(dt * hcols[8:16], upto[...])
    rows_o[0:8] = dt
    rows_o[8:16] = sig
    rows_o[16:24] = cum
    lead = blk.lead(cum)
    tail = blk.tail_base(cum) * dt
    cols = to_columns([tail])
    tail_lanes = by_head([column(cols, 0, h) for h in range(HEADS_DEV)])
    packed = (act[:, :WIDE].astype(F32) * tail_lanes).astype(BF16)
    fresh = tn(act[:, WIDE : WIDE + STATE], packed)
    last = last_by_lane(lead)
    state_o[0, 0:STATE] = state[...]
    state_o[0, STATE : STATE + 8] = decay[...]
    state[...] = last * state[...] + fresh
    decay[...] = last * decay[...]

    @at.when_last
    def _():
        device_o[...] = message(state[...], decay[...])


def intra_kernel(at, marks, normed, cot, weights, xbc, rows, lanes, z_o, e_o, yi_o):
    blk = Block(marks, at.index)
    z_o[...] = nn(normed[...], weights[:, 0:WIDE]).astype(BF16)
    e_o[...] = nn(cot[...], weights[:, WIDE : 2 * WIDE]).astype(BF16)
    dt = rows[0:8]
    cum = rows[16:24]
    x = xbc[:, :WIDE].astype(F32)
    scores = nt(xbc[:, WIDE + STATE :], xbc[:, WIDE : WIDE + STATE])
    allowed = blk.allowed()
    cols = to_columns([cum])
    out = lanes[1:2] * x
    for h in range(HEADS_DEV):
        decays = decay_of(allowed, column(cols, 0, h), cum[h : h + 1])
        mix = (scores * decays * dt[h : h + 1]).astype(BF16)
        out = out + nn(mix, of_head(x, h).astype(BF16))
    yi_o[...] = out.astype(BF16)


def gated_kernel(
    at, marks, yi, z, e, xbc, rows, states, one, two, three, lanes, weights,
    y_o, mixed_o, part_o, sums_o, prefix,
):
    @at.when_first
    def _():
        prefix[...] = carried((one, two, three))

    blk = Block(marks, at.index)
    lead = blk.lead(rows[16:24])
    cols = to_columns([lead])
    lead_lanes = by_head([column(cols, 0, h) for h in range(HEADS_DEV)])
    entering = states[0, 0:STATE] + states[0, STATE : STATE + 1] * prefix[...]
    y = yi[...].astype(F32) + lead_lanes * nn(xbc[:, WIDE + STATE :], entering.astype(BF16))
    y_o[...] = y.astype(BF16)
    gate, _ = silu_parts(z[...].astype(F32))
    v = y * gate
    mixed = (v * lanes[0:1]).astype(BF16)
    mixed_o[...] = mixed
    part_o[...] = nt(mixed, weights[:, WIDE : 2 * WIDE]).astype(BF16)
    row = iota((16, 2 * WIDE), 0)
    lane = iota((16, 2 * WIDE), 1)
    pick = jnp.where(((row == 0) & (lane < WIDE)) | ((row == 1) & (lane >= WIDE)), 1.0, 0.0)
    both = jnp.concatenate([v * v, e[...].astype(F32) * mixed.astype(F32)], axis=1)
    sums_o[...] = nt(pick.astype(BF16), both.astype(BF16))[0:2]


def gate_back_kernel(
    at, marks, y, z, e, xbc, rows, sums, lanes,
    dy_o, dz_o, reach_o, device_o, gains_o,
    carry, decay,
):
    blk = Block(marks, at.index)

    @at.when_last
    def _():
        carry[...] = jnp.zeros_like(carry)
        decay[...] = jnp.ones_like(decay)
        gains_o[...] = jnp.zeros_like(gains_o)

    lead = blk.lead(rows[16:24])
    root = lax.rsqrt(sums[0:1] / INNER + EPSILON)
    coef = sums[1:2] * root * root * root / INNER
    cols = to_columns([lead, jnp.broadcast_to(root, (8, BLOCK)), jnp.broadcast_to(coef, (8, BLOCK))])
    lead_lanes = by_head([column(cols, 0, h) for h in range(HEADS_DEV)])
    gate, slope = silu_parts(z[...].astype(F32))
    y_v = y[...].astype(F32)
    v = y_v * gate
    dm = column(cols, 1, 0) * e[...].astype(F32)
    dv = lanes[0:1] * dm - column(cols, 2, 0) * v
    dy = dv * gate
    dy_o[...] = dy.astype(BF16)
    dz_o[...] = (dv * y_v * slope).astype(BF16)
    x = xbc[:, :WIDE].astype(F32)
    gains_o[0:1] += jnp.sum(v * dm, axis=0, keepdims=True)
    gains_o[1:2] += jnp.sum(dy * x, axis=0, keepdims=True)
    reach = tn(xbc[:, WIDE + STATE :], (dy * lead_lanes).astype(BF16))
    last = last_by_lane(lead)
    reach_o[0, 0:STATE] = carry[...]
    reach_o[0, STATE : STATE + 8] = decay[...]
    carry[...] = last * carry[...] + reach
    decay[...] = last * decay[...]

    @at.when_first
    def _():
        device_o[...] = message(carry[...], decay[...])


def intra_back_kernel(
    at, marks, dy_r, xbc, rows, states, prefix, sums, mixed, cot, lanes,
    dxi_o, dbc_o, stats_o, grad_out_o,
):
    blk = Block(marks, at.index)

    @at.when_first
    def _():
        grad_out_o[...] = jnp.zeros_like(grad_out_o)

    dt = rows[0:8]
    cum = rows[16:24]
    lead = blk.lead(cum)
    root = lax.rsqrt(sums[0:1] / INNER + EPSILON)
    cols = to_columns([cum, lead, jnp.broadcast_to(root, (8, BLOCK))])
    lead_lanes = by_head([column(cols, 1, h) for h in range(HEADS_DEV)])
    rooted = (mixed[...].astype(F32) * column(cols, 2, 0)).astype(BF16)
    grad_out_o[...] += tn(cot[...], rooted)

    dy = dy_r[...].astype(F32)
    x_low = xbc[:, :WIDE]
    b_low = xbc[:, WIDE : WIDE + STATE]
    c_low = xbc[:, WIDE + STATE :]
    entering = states[0, 0:STATE] + states[0, STATE : STATE + 1] * prefix[...]
    held = entering.astype(BF16)
    masks = head_masks().astype(BF16)
    cross = nn(c_low, held)
    lead_grad = nt(masks, (dy * cross).astype(BF16))
    dc = nt((dy * lead_lanes).astype(BF16), held)
    scores = nt(c_low, b_low)
    allowed = blk.allowed()
    ds = jnp.zeros((BLOCK, BLOCK), F32)
    dx = lanes[1:2] * dy
    lane = iota((1, 128), 1)
    row8 = iota((8, 1), 0)
    row_sums = jnp.zeros((BLOCK, 128), F32)
    time_grad = jnp.zeros((8, BLOCK), F32)
    for h in range(HEADS_DEV):
        dt_h = dt[h : h + 1]
        dy_h = of_head(dy, h).astype(BF16)
        decays = decay_of(allowed, column(cols, 0, h), cum[h : h + 1])
        weighted = nt(dy_h, x_low) * decays
        ds = ds + weighted * dt_h
        scored = weighted * scores
        time_grad = time_grad + jnp.where(
            row8 == h, jnp.sum(scored, axis=0, keepdims=True), 0.0
        )
        row_sums = row_sums + jnp.where(
            lane == h, jnp.sum(scored * dt_h, axis=1, keepdims=True), 0.0
        )
        mix = (scores * decays * dt_h).astype(BF16)
        dx = dx + tn(mix, dy_h)
    ds_low = ds.astype(BF16)
    dxi_o[...] = dx.astype(BF16)
    dbc_o[:, 0:STATE] = tn(ds_low, c_low).astype(BF16)
    dbc_o[:, STATE : 2 * STATE] = (dc + nn(ds_low, b_low)).astype(BF16)
    stats_o[0:8] = time_grad
    stats_o[8:16] = row_sums.T[0:8] - time_grad * dt + lead_grad * lead


def input_back_kernel(
    at, marks, normed, halo, dz, dxi, dbc, xbc, slope, cin, cin_halo,
    rows, stats, states, prefix, reaches, one, two, three, gain, later, weights, taps, hcols,
    grad_out_t, gains,
    dn_o, early_o, late_o, pack_o, spill_o,
    ahead, suffix, since, wgrad, chan, steps, norm, low, wide,
):
    blk = Block(marks, at.index)

    @at.when_last
    def _():
        suffix[...] = carried((one, two, three))
        square = (BLOCK, BLOCK)
        since[...] = jnp.where(iota(square, 0) >= iota(square, 1), 1.0, 0.0).astype(BF16)
        wide[:, 0:WIDE] = later[:, 0:WIDE]
        wide[:, WIDE : 3 * WIDE] = weights[...]
        wgrad[...] = jnp.zeros_like(wgrad)
        chan[...] = jnp.zeros_like(chan)
        steps[...] = jnp.zeros_like(steps)
        norm[...] = jnp.zeros_like(norm)
        ahead[BLOCK : BLOCK + 8] = jnp.zeros((8, CHAN), F32)

    dt = rows[0:8]
    sig = rows[8:16]
    cum = rows[16:24]
    rate = hcols[8:16]
    lead = blk.lead(cum)
    tail_base = blk.tail_base(cum)
    tail = tail_base * dt
    cols = to_columns([tail])
    tail_lanes = by_head([column(cols, 0, h) for h in range(HEADS_DEV)])
    entering = states[0, 0:STATE] + states[0, STATE : STATE + 1] * prefix[...]
    leaving = reaches[0, 0:STATE] + reaches[0, STATE : STATE + 1] * suffix[...]
    leaving_low = leaving.astype(BF16)
    x = xbc[:, :WIDE].astype(F32)
    dpacked = nn(xbc[:, WIDE : WIDE + STATE], leaving_low)
    packed = (x * tail_lanes).astype(BF16)
    masks = head_masks()
    tail_grad = nt(masks.astype(BF16), (dpacked * x).astype(BF16))
    dx = dxi[...].astype(F32) + dpacked * tail_lanes
    db = dbc[:, 0:STATE].astype(F32) + nt(packed, leaving_low)
    dc = dbc[:, STATE : 2 * STATE].astype(F32)

    tail_term = tail_grad * tail
    state_term = jnp.sum(leaving * entering, axis=0, keepdims=True)
    last_term = jnp.sum(tail_term, axis=1, keepdims=True) + (
        jnp.sum(masks * state_term, axis=1, keepdims=True) * lead[:, BLOCK - 1 : BLOCK]
    )
    dcum = stats[8:16] - tail_term + jnp.where(iota((8, BLOCK), 1) == BLOCK - 1, last_term, 0.0)
    dla = running_sum(dcum, since[...])
    ddt = stats[0:8] + tail_grad * tail_base + dla * rate
    dstep = jnp.where(iota((8, 1), 0) < HEADS_DEV, ddt * sig, 0.0)
    steps[0:8] += dstep
    steps[8:16] += dla * dt * rate
    placed = jnp.concatenate(
        [jnp.zeros((64, BLOCK), F32), dstep, jnp.zeros((56, BLOCK), F32)], axis=0
    ).T

    dpre = jnp.concatenate([dx, db, dc], axis=1) * slope[...].astype(F32)
    inputs = cin[...].astype(F32)
    ahead[0:BLOCK] = dpre
    chan[4:5] += jnp.sum(dpre, axis=0, keepdims=True)
    chan[3:4] += jnp.sum(dpre * inputs, axis=0, keepdims=True)
    din = taps[3:4] * dpre
    left = blk.until_end()
    for lag in range(1, CONV):
        tap = 3 - lag
        later_dpre = jnp.where(left > lag, ahead[lag : lag + BLOCK], 0.0)
        chan[tap : tap + 1] += jnp.sum(later_dpre * inputs, axis=0, keepdims=True)
        din = din + taps[tap : tap + 1] * later_dpre
    ahead[BLOCK : BLOCK + 8] = dpre[0:8]
    mine = pl.ds(at.part * BLOCK, BLOCK)
    low[mine, 0:WIDE] = dz[...]
    low[mine, WIDE : WIDE + 128] = din[:, 0:128].astype(BF16)
    low[mine, WIDE + 128 : 2 * WIDE] = (din[:, 128:256] + placed).astype(BF16)
    low[mine, 2 * WIDE :] = din[:, WIDE:].astype(BF16)

    if at.part > 0:
        return

    all_low = low[...]
    normed_all = normed[...]
    dn = nt(all_low, wide[...])
    wgrad[...] += tn(normed_all, all_low)
    norm[0:1] += jnp.sum(dn * normed_all.astype(F32), axis=0, keepdims=True)
    dn_o[...] = dn.astype(BF16)

    @at.when_first
    def _():
        ahead[0:8] = jnp.zeros((8, CHAN), F32)
        ahead[8:16] = ahead[BLOCK : BLOCK + 8]
        ahead[16:24] = jnp.zeros((8, CHAN), F32)
        pos = blk.start - 8 + iota((8, 1), 0)
        left = end_of(marks, pos) - pos
        back = jnp.zeros((8, CHAN), F32)
        for lag in range(1, CONV):
            tap = 3 - lag
            same = (left > lag) & (pos >= 0)
            later_dpre = jnp.where(same, ahead[lag : lag + 8], 0.0)
            chan[tap : tap + 1] += jnp.sum(later_dpre * cin_halo[...], axis=0, keepdims=True)
            back = back + taps[tap : tap + 1] * later_dpre
        spilled = jnp.concatenate([jnp.zeros((8, CHAN), F32), back], axis=0).astype(BF16)
        given = nt(spilled, wide[:, WIDE:])
        spill_o[...] = given[8:16]
        rows_in = halo[...].astype(F32)
        scale = lax.rsqrt(jnp.mean(rows_in * rows_in, axis=1, keepdims=True) + EPSILON)
        normed_halo = (rows_in * scale * gain[0:1]).astype(BF16)
        norm[0:1] += jnp.sum(given * normed_halo.astype(F32), axis=0, keepdims=True)
        wgrad[:, WIDE:] += tn(normed_halo, spilled)
        early_o[...] = wgrad[:, WIDE:].astype(BF16)
        late_o[...] = jnp.concatenate(
            [wgrad[:, 0:INNER_DEV], grad_out_t[:, 0:INNER_DEV]], axis=1
        ).astype(BF16)
        gained = norm[0:1] / gain[0:1]

        def beside(left, right):
            return jnp.concatenate([left, right], axis=1)

        pack = jnp.concatenate(
            [
                chan[0:5],
                gained[:, 0:CHAN],
                beside(gained[:, CHAN:], gains[0:1]),
                beside(gains[1:2], steps[8:9]),
                beside(steps[9:10], steps[10:11]),
                beside(steps[0:1], steps[1:2]),
                beside(steps[2:3], jnp.zeros((1, WIDE), F32)),
                jnp.zeros((5, CHAN), F32),
            ],
            axis=0,
        )
        pack_o[...] = pack.astype(BF16)


def copied_kernel(source, out):
    out[...] = source[...]


def copied(values):
    rows, width = values.shape
    block = pl.BlockSpec((rows // 4, width), lambda s: (s, 0))
    return pl.pallas_call(
        copied_kernel,
        grid=(4,),
        in_specs=[block],
        out_specs=block,
        out_shape=jax.ShapeDtypeStruct(values.shape, values.dtype),
        compiler_params=pltpu.CompilerParams(
            dimension_semantics=("arbitrary",), vmem_limit_bytes=VMEM_LIMIT
        ),
        cost_estimate=pl.CostEstimate(flops=int(3e9), bytes_accessed=int(6e6), transcendentals=0),
    )(values)


def passed_along(values, axis, by):
    count = lax.axis_size(axis)
    pairs = [(i, i + by) for i in range(count) if 0 <= i + by < count]
    return lax.ppermute(values, axis, pairs)


def handed_to_all(values, axis):
    count = lax.axis_size(axis)
    return lax.all_to_all(
        jnp.broadcast_to(values[None], (count,) + values.shape), axis, 0, 0, tiled=False
    )


def sent_along(device, sign):
    return [passed_along(device, "context", sign * k) for k in (1, 2, 3)]


def padded(values, width):
    extra = width - values.shape[-1]
    return jnp.pad(values, [(0, 0)] * (values.ndim - 1) + [(0, extra)])


def body(
    hidden, cotangent, lengths, norm_gain, gate_proj, value_proj, state_proj, step_proj,
    conv_value, conv_state, value_bias, state_bias, step_bias, decay_log, skip_gain,
    mixer_gain, out_proj,
):
    tok = hidden.shape[0]
    blocks = tok // BLOCK
    ctx = lax.axis_index("context")
    rank = lax.axis_index("tensor")

    own_rows = state_proj.shape[0]
    first = jnp.concatenate(
        [state_proj.astype(F32), conv_state, state_bias[None], jnp.zeros((3, state_proj.shape[1]), F32)],
        axis=0,
    )
    first = handed_to_all(first, "tensor")
    first, lengths, gate_proj, out_proj, edge = lax.optimization_barrier(
        (first, lengths, gate_proj, out_proj, hidden[tok - 16 :])
    )
    first = first.transpose(1, 0, 2).reshape(own_rows + 8, 2 * STATE)
    conv_shared = first[own_rows : own_rows + 5]
    needed = jnp.concatenate(
        [
            value_proj, step_proj, jnp.zeros((own_rows, 61), BF16), first[:own_rows].astype(BF16),
        ],
        axis=1,
    )
    needed = handed_to_all(needed, CELLS).reshape(MODEL, 2 * WIDE)
    finishes = jnp.cumsum(lengths[0])
    marks = jnp.concatenate(
        [finishes, jnp.stack([ctx * tok, 0 * ctx, 0 * ctx, 0 * ctx])]
    )
    marks = marks.astype(jnp.int32)
    later = jnp.concatenate([padded(gate_proj, WIDE), padded(out_proj.T, WIDE)], axis=1)
    later = handed_to_all(later, CELLS)
    halo = passed_along(edge, "context", 1)

    pair = whole((MODEL, 2 * WIDE))
    normed, xbc, slope, cin, cin_halo, rows, states, device, gain, taps, lanes, hcols = call(
        project_kernel, blocks, PARTS[0], False,
        [
            SMEM, SMEM, SMEM, SMEM, rows_of(MODEL), whole((16, MODEL)), whole((MODEL,)), pair,
            whole((4, INNER_DEV)), whole((INNER_DEV,)), whole((INNER_DEV,)), whole((5, 2 * STATE)),
        ],
        [
            (rows_of(MODEL), BF16), (rows_of(CHAN), BF16), (rows_of(CHAN), BF16),
            (rows_of(CHAN), BF16), (whole((8, CHAN)), F32), (lanes_of(24), F32), (STATES, F32),
            (whole(STATE_DIMS), F32), (whole((8, MODEL)), F32), (whole((8, CHAN)), F32),
            (whole((8, WIDE)), F32), (whole((16, BLOCK)), F32),
        ],
        [
            pltpu.VMEM((BLOCK + 8, CHAN), F32), pltpu.VMEM((STATE, WIDE), F32),
            pltpu.VMEM((8, WIDE), F32), pltpu.VMEM((BLOCK, BLOCK), BF16),
        ],
        14, marks, step_bias, decay_log, skip_gain, hidden, halo, norm_gain, needed, conv_value,
        value_bias, mixer_gain, conv_shared,
    )
    messages = sent_along(device, 1)
    later, xbc = lax.optimization_barrier((later, xbc))
    later = later.reshape(MODEL, 2 * WIDE)
    z, e, yi = call(
        intra_kernel, blocks, PARTS[1], False,
        [
            SMEM, rows_of(MODEL), rows_of(MODEL), pair, rows_of(CHAN), lanes_of(24),
            whole((8, WIDE)),
        ],
        [(rows_of(WIDE), BF16)] * 3,
        [], 12, marks, normed, cotangent, later, xbc, rows, lanes,
    )
    y, mixed, part, sums, prefix = call(
        gated_kernel, blocks, PARTS[2], False,
        [
            SMEM, rows_of(WIDE), rows_of(WIDE), rows_of(WIDE), rows_of(CHAN), lanes_of(24), STATES,
            whole(STATE_DIMS), whole(STATE_DIMS), whole(STATE_DIMS), whole((8, WIDE)), pair,
        ],
        [
            (rows_of(WIDE), BF16), (rows_of(WIDE), BF16), (rows_of(MODEL), BF16),
            (lanes_of(2), F32), (whole((STATE, WIDE)), F32),
        ],
        [], 10, marks, yi, z, e, xbc, rows, states, *messages, lanes, later,
    )
    sums = jnp.sum(handed_to_all(sums, "tensor"), axis=0)

    ranks = lax.axis_size("tensor")
    own = tok // ranks
    place = rank * own
    own_hidden = lax.dynamic_slice_in_dim(hidden, place, own, 0).astype(F32)
    own_cot = lax.dynamic_slice_in_dim(cotangent, place, own, 0).astype(F32)
    own_root = lax.rsqrt(lax.dynamic_slice_in_dim(sums[0], place, own, 0) / INNER + EPSILON)
    projected = lax.psum_scatter(part, "tensor", scatter_dimension=0, tiled=True).astype(F32)
    own_out = (own_hidden + own_root[:, None] * projected).astype(BF16)

    dy, dz, reaches, back_device, gains = call(
        gate_back_kernel, blocks, PARTS[3], True,
        [
            SMEM, rows_of(WIDE), rows_of(WIDE), rows_of(WIDE), rows_of(CHAN), lanes_of(24),
            lanes_of(2), whole((8, WIDE)),
        ],
        [
            (rows_of(WIDE), BF16), (rows_of(WIDE), BF16), (STATES, F32), (whole(STATE_DIMS), F32),
            (whole((8, WIDE)), F32),
        ],
        [pltpu.VMEM((STATE, WIDE), F32), pltpu.VMEM((8, WIDE), F32)],
        9, marks, y, z, e, xbc, rows, sums, lanes,
    )
    messages = sent_along(back_device, -1)
    dxi, dbc, stats, grad_out_t = call(
        intra_back_kernel, blocks, PARTS[4], False,
        [
            SMEM, rows_of(WIDE), rows_of(CHAN), lanes_of(24), STATES, whole((STATE, WIDE)),
            lanes_of(2), rows_of(WIDE), rows_of(MODEL), whole((8, WIDE)),
        ],
        [
            (rows_of(WIDE), BF16), (rows_of(WIDE), BF16), (lanes_of(16), F32),
            (whole((MODEL, WIDE)), F32),
        ],
        [], 13, marks, dy, xbc, rows, states, prefix, sums, mixed, cotangent, lanes,
    )
    dxi, own_out, messages = lax.optimization_barrier((dxi, own_out, messages))
    output = lax.all_gather(own_out, "tensor", axis=0, tiled=True)
    dn, early, late, pack, spill = call(
        input_back_kernel, blocks, PARTS[5], True,
        [
            SMEM, ("tile", MODEL), whole((16, MODEL)), rows_of(WIDE), rows_of(WIDE),
            rows_of(WIDE), rows_of(CHAN), rows_of(CHAN), rows_of(CHAN),
            whole((8, CHAN)), lanes_of(24), lanes_of(16), STATES, whole((STATE, WIDE)), STATES,
            whole(STATE_DIMS), whole(STATE_DIMS), whole(STATE_DIMS), whole((8, MODEL)), pair, pair,
            whole((8, CHAN)), whole((16, BLOCK)), whole((MODEL, WIDE)), whole((8, WIDE)),
        ],
        [
            (("tile", MODEL), BF16), (whole((MODEL, CHAN)), BF16),
            (whole((MODEL, 2 * INNER_DEV)), BF16), (whole((16, CHAN)), BF16),
            (whole((8, MODEL)), F32),
        ],
        [
            pltpu.VMEM((BLOCK + 8, CHAN), F32), pltpu.VMEM((STATE, WIDE), F32),
            pltpu.VMEM((BLOCK, BLOCK), BF16), pltpu.VMEM((MODEL, 3 * WIDE), F32),
            pltpu.VMEM((8, CHAN), F32), pltpu.VMEM((16, BLOCK), F32), pltpu.VMEM((8, MODEL), F32),
            pltpu.VMEM((PARTS[5] * BLOCK, 3 * WIDE), BF16), pltpu.VMEM((MODEL, 3 * WIDE), BF16),
        ],
        22, marks, normed, halo, dz, dxi, dbc, xbc, slope, cin, cin_halo,
        rows, stats, states, prefix, reaches, *messages, gain, later, needed, taps, hcols,
        grad_out_t, gains,
    )

    arrived = passed_along(spill, "context", -1)
    end = dn[tok - 8 :].astype(F32) + arrived
    dn = lax.dynamic_update_slice(dn, end.astype(BF16), (tok - 8, 0))
    dn, output = lax.optimization_barrier((dn, output))
    own_dn = lax.psum_scatter(dn, "tensor", scatter_dimension=0, tiled=True)

    cells = lax.axis_size("shard") * lax.axis_size("context")
    early = jnp.concatenate(
        [
            early.reshape(cells, own_rows, CHAN),
            jnp.broadcast_to(pack[None], (cells,) + pack.shape),
        ],
        axis=1,
    )
    early = lax.all_to_all(early, CELLS, 0, 0, tiled=False)
    output = copied(output)
    own_dn, early, output = lax.optimization_barrier((own_dn, early, output))
    early = jnp.sum(early.astype(F32), axis=0)
    own_dn = own_dn.astype(F32)
    scaling = lax.rsqrt(jnp.mean(own_hidden * own_hidden, axis=1, keepdims=True) + EPSILON)
    unit = own_hidden * scaling
    scaled = own_dn * norm_gain[None]
    own_grad = own_cot + scaling * (
        scaled - unit * jnp.mean(scaled * unit, axis=1, keepdims=True)
    )
    own_grad = own_grad.astype(BF16)
    grad_hidden = lax.all_gather(own_grad, "tensor", axis=0, tiled=True)
    late = lax.all_to_all(late.reshape(cells, own_rows, 2 * INNER_DEV), CELLS, 0, 0, tiled=False)
    late = jnp.sum(late.astype(F32), axis=0)

    big, small = early[:own_rows], early[own_rows:]
    chan = small[:5]
    norm_cells = jnp.concatenate([small[5], small[6, :WIDE]])
    grad_mixer = small[6, WIDE : WIDE + INNER_DEV]
    grad_skip = jnp.sum(small[7, :INNER_DEV].reshape(HEADS_DEV, HEADDIM), axis=1)
    lines = jnp.sum(small[7:11].reshape(8, WIDE), axis=1)
    grad_decay = lines[1:4]
    grad_step_bias = lines[4:7]
    share = 2 * STATE // lax.axis_size("tensor")
    shared = jnp.concatenate([big[:, WIDE:], chan[:, WIDE:]], axis=0)
    shared = shared.reshape(own_rows + 5, -1, share).transpose(1, 0, 2)
    shared = shared.reshape(shared.shape[0], -1)
    count = shared.shape[1]
    final = jnp.concatenate(
        [shared, jnp.broadcast_to(norm_cells[None], (shared.shape[0], MODEL))], axis=1
    )
    final = padded(final, 2560).reshape(-1, 20, 128)
    final = jnp.sum(lax.all_to_all(final, "tensor", 0, 0, tiled=False), axis=0).reshape(-1)
    state_all = final[:count].reshape(own_rows + 5, share)
    return (
        output,
        grad_hidden,
        final[count : count + MODEL],
        late[:, :INNER_DEV],
        big[:, :INNER_DEV],
        state_all[:own_rows],
        big[:, INNER_DEV : INNER_DEV + HEADS_DEV],
        chan[:4, :INNER_DEV],
        state_all[own_rows : own_rows + 4],
        chan[4, :INNER_DEV],
        state_all[own_rows + 4],
        grad_step_bias,
        grad_decay,
        grad_skip,
        grad_mixer,
        late[:, INNER_DEV:].T,
    )


def solution(mesh):
    cells = P(CELLS, None)
    split = P(CELLS, "tensor")
    return jax.shard_map(
        body,
        mesh=mesh,
        in_specs=(
            cells, cells, P("shard", None), P(), split, split, split, split, P(None, "tensor"),
            P(None, "tensor"), P("tensor"), P("tensor"), P("tensor"), P("tensor"), P("tensor"),
            P("tensor"), P("tensor", CELLS),
        ),
        out_specs=(
            cells, cells, P(), split, split, split, split, P(None, "tensor"), P(None, "tensor"),
            P("tensor"), P("tensor"), P("tensor"), P("tensor"), P("tensor"), P("tensor"),
            P("tensor", CELLS),
        ),
        check_vma=False,
    )
```

```python
import jax
import jax.numpy as jnp
from jax import lax
from jax.experimental import pallas as pl
from jax.experimental.pallas import tpu as pltpu
from jax.sharding import PartitionSpec as P

MODEL = 768
INNER = 1536
HEADDIM = 64
STATE = 128
CONV = 4
BLOCK = 256
HEADS_DEV = 3
INNER_DEV = 192
WIDE = 256
CHAN = 512
EPSILON = 1e-05
F32 = jnp.float32
BF16 = jnp.bfloat16
CELLS = ("shard", "context")
VMEM_LIMIT = 60 * 1024 * 1024
PARTS = (2, 2, 2, 2, 1, 2)


def nn(a, b):
    return lax.dot_general(a, b, (((1,), (0,)), ((), ())), preferred_element_type=F32)


def nt(a, b):
    return lax.dot_general(a, b, (((1,), (1,)), ((), ())), preferred_element_type=F32)


def tn(a, b):
    return lax.dot_general(a, b, (((0,), (0,)), ((), ())), preferred_element_type=F32)


def iota(shape, dim):
    return lax.broadcasted_iota(jnp.int32, shape, dim)


def start_of(marks, pos):
    start = jnp.zeros_like(pos)
    for k in range(3):
        start = jnp.where(pos >= marks[k], marks[k], start)
    return start


def end_of(marks, pos):
    end = jnp.full_like(pos, marks[3])
    for k in (2, 1, 0):
        end = jnp.where(pos < marks[k], marks[k], end)
    return end


def running_sum(rows, ones):
    top = rows.astype(BF16)
    rest = rows - top.astype(F32)
    mid = rest.astype(BF16)
    low = (rest - mid.astype(F32)).astype(BF16)
    pieces = [top.astype(F32), mid.astype(F32), low.astype(F32), jnp.zeros((8, BLOCK), F32)]
    sums = nn(jnp.concatenate(pieces, axis=0).astype(BF16), ones)
    return sums[0:8] + sums[8:16] + sums[16:24]


def by_head(cols, width=WIDE):
    lane = iota((1, width), 1)
    return jnp.where(
        lane < HEADDIM,
        cols[0],
        jnp.where(lane < 2 * HEADDIM, cols[1], jnp.where(lane < 3 * HEADDIM, cols[2], 0.0)),
    )


def head_masks():
    row = iota((8, WIDE), 0)
    lane = iota((8, WIDE), 1)
    low = row * HEADDIM
    return jnp.where((lane >= low) & (lane < low + HEADDIM) & (row < HEADS_DEV), 1.0, 0.0)


def of_head(values, h):
    lane = iota((1, WIDE), 1)
    return jnp.where((lane >= h * HEADDIM) & (lane < (h + 1) * HEADDIM), values, 0.0)


def to_columns(rows):
    have = 8 * len(rows)
    stacked = jnp.concatenate(list(rows) + [jnp.zeros((128 - have, BLOCK), F32)], axis=0)
    return stacked.T


def column(cols, part, h):
    at = 8 * part + h
    return cols[:, at : at + 1]


def silu_parts(values):
    sig = 1.0 / (1.0 + jnp.exp(-values))
    return values * sig, sig * (1.0 + values * (1.0 - sig))


class Block:
    def __init__(self, marks, b):
        self.marks = marks
        self.start = marks[4] + b * BLOCK
        self.pos_row = self.start + iota((1, BLOCK), 1)
        self.pos_col = self.start + iota((BLOCK, 1), 0)

    def lead(self, cum):
        carried = start_of(self.marks, self.pos_row) < self.start
        return jnp.where(carried, jnp.exp(cum), 0.0)

    def tail_base(self, cum):
        last = cum[:, BLOCK - 1 : BLOCK]
        kept = end_of(self.marks, self.pos_row) > self.start + BLOCK - 1
        return jnp.where(kept, jnp.exp(last - cum), 0.0)

    def allowed(self):
        first = start_of(self.marks, self.pos_col)
        return (self.pos_row >= first) & (self.pos_row <= self.pos_col)

    def since_start(self):
        return self.pos_col - start_of(self.marks, self.pos_col)

    def until_end(self):
        return end_of(self.marks, self.pos_col) - self.pos_col


def decay_of(allowed, cum_col, cum_row):
    return jnp.exp(jnp.where(allowed, cum_col - cum_row, -1e30))


def message(state, decay):
    return jnp.concatenate([state, decay], axis=0)


def carried(messages):
    one, two, three = (m[...] for m in messages)

    def join(near, far):
        return near[:STATE] + near[STATE : STATE + 1] * far

    return join(one, join(two, three[:STATE]))


def last_by_lane(rows):
    return by_head([rows[h : h + 1, BLOCK - 1 : BLOCK] for h in range(HEADS_DEV)])


class At:
    def __init__(self, index, blocks, part, parts):
        self.index = index
        self.count = blocks
        self.part = part
        self.parts = parts
        self.can_be_first = part == 0
        self.can_be_last = part == parts - 1

    def when_first(self, do):
        if self.can_be_first:
            pl.when(self.index == 0)(do)

    def when_last(self, do):
        if self.can_be_last:
            pl.when(self.index == self.count - 1)(do)


def rows_of(width):
    return ("rows", width)


def lanes_of(count):
    return ("lanes", count)


def whole(dims):
    return ("whole", dims)


STATE_DIMS = (STATE + 8, WIDE)
STATES = ("states",)
SMEM = ("smem",)


def call(kernel, blocks, parts, down, ins, outs, scratch, micros, *args):
    steps = blocks // parts
    tile = parts * BLOCK

    def step(s):
        return steps - 1 - s if down else s

    def spec(kind):
        what = kind[0]
        if what == "smem":
            return pl.BlockSpec(memory_space=pltpu.SMEM)
        if what in ("rows", "tile"):
            return pl.BlockSpec((tile, kind[1]), lambda s: (step(s), 0))
        if what == "lanes":
            return pl.BlockSpec((kind[1], tile), lambda s: (0, step(s)))
        if what == "states":
            return pl.BlockSpec((parts,) + STATE_DIMS, lambda s: (step(s), 0, 0))
        return pl.BlockSpec(kind[1], lambda s: (0,) * len(kind[1]))

    def view(refs, n, kind, k):
        ref = refs[n]
        if kind[0] == "rows":
            return ref.at[pl.ds(k * BLOCK, BLOCK)]
        if kind[0] == "lanes":
            return ref.at[:, pl.ds(k * BLOCK, BLOCK)]
        if kind[0] == "states":
            return ref.at[pl.ds(k, 1)]
        return ref

    kinds = list(ins) + [kind for kind, _ in outs]

    def run(*refs):
        order = range(parts - 1, -1, -1) if down else range(parts)
        for k in order:
            at = At(step(pl.program_id(0)) * parts + k, blocks, k, parts)
            views = [view(refs, n, kind, k) for n, kind in enumerate(kinds)]
            kernel(at, *views, *refs[len(kinds) :])

    def dims(kind):
        what = kind[0]
        if what in ("rows", "tile"):
            return (blocks * BLOCK, kind[1])
        if what == "lanes":
            return (kind[1], blocks * BLOCK)
        if what == "states":
            return (blocks,) + STATE_DIMS
        return kind[1]

    return pl.pallas_call(
        run,
        grid=(steps,),
        in_specs=[spec(kind) for kind in ins],
        out_specs=[spec(kind) for kind, _ in outs],
        scratch_shapes=scratch,
        out_shape=[jax.ShapeDtypeStruct(dims(kind), dtype) for kind, dtype in outs],
        compiler_params=pltpu.CompilerParams(
            dimension_semantics=("arbitrary",), vmem_limit_bytes=VMEM_LIMIT
        ),
        cost_estimate=pl.CostEstimate(
            flops=int(micros * 1.15e9), bytes_accessed=int(micros * 1e6), transcendentals=0
        ),
    )(*args)


def project_kernel(
    at, marks, step_bias, decay_log, skip_gain, hidden, halo, norm_gain, weights, conv_value,
    value_bias, mixer_gain, conv_shared,
    normed_o, xbc_o, slope_o, cin_o, cin_halo_o, rows_o, state_o, device_o,
    gain, taps, lanes, hcols,
    ext, state, decay, upto,
):
    blk = Block(marks, at.index)
    wv = weights.at[:, 0:WIDE]
    ws = weights.at[:, WIDE : 2 * WIDE]

    @at.when_first
    def _():
        gain[...] = jnp.broadcast_to(norm_gain[...].reshape(1, MODEL), (8, MODEL))
        taps[...] = jnp.zeros_like(taps)
        taps[0:4, 0:INNER_DEV] = conv_value[...]
        taps[4:5, 0:INNER_DEV] = value_bias[...].reshape(1, INNER_DEV)
        taps[0:5, WIDE:] = conv_shared[...]
        lanes[...] = jnp.zeros_like(lanes)
        lanes[0:1, 0:INNER_DEV] = mixer_gain[...].reshape(1, INNER_DEV)
        lanes[1:2] = by_head([skip_gain[h] for h in range(HEADS_DEV)])
        row = iota((8, BLOCK), 0)
        bias = jnp.zeros((8, BLOCK), F32)
        rate = jnp.zeros((8, BLOCK), F32)
        for h in range(HEADS_DEV):
            bias = jnp.where(row == h, step_bias[h], bias)
            rate = jnp.where(row == h, decay_log[h], rate)
        hcols[0:8] = bias
        hcols[8:16] = jnp.where(row < HEADS_DEV, -jnp.exp(rate), 0.0)
        square = (BLOCK, BLOCK)
        upto[...] = jnp.where(iota(square, 0) <= iota(square, 1), 1.0, 0.0).astype(BF16)

    def norm(rows):
        rows = rows.astype(F32)
        scale = lax.rsqrt(jnp.mean(rows * rows, axis=1, keepdims=True) + EPSILON)
        return (rows * scale * gain[0:1]).astype(BF16)

    @at.when_first
    def _():
        ahead = norm(halo[...])
        into = jnp.concatenate([nn(ahead, wv[...]), nn(ahead, ws[...])], axis=1)
        into = into.astype(BF16).astype(F32)
        ext[0:8] = into[8:16]
        cin_halo_o[...] = into[8:16]
        state[...] = jnp.zeros_like(state)
        decay[...] = jnp.ones_like(decay)

    normed = norm(hidden[...])
    normed_o[...] = normed
    value_pre = nn(normed, wv[...])
    state_pre = nn(normed, ws[...])
    cin = jnp.concatenate([value_pre, state_pre], axis=1).astype(BF16)
    cin_o[...] = cin
    ext[8 : 8 + BLOCK] = cin.astype(F32)
    pre = taps[4:5] + taps[3:4] * ext[8 : 8 + BLOCK]
    since = blk.since_start()
    for lag in range(1, CONV):
        pre = pre + taps[3 - lag : 4 - lag] * (
            jnp.where(since >= lag, ext[8 - lag : 8 - lag + BLOCK], 0.0)
        )
    ext[0:8] = ext[BLOCK : BLOCK + 8]
    act, slope = silu_parts(pre)
    act = act.astype(BF16)
    xbc_o[...] = act
    slope_o[...] = slope.astype(BF16)

    raw = value_pre[:, 128:256].T[64:72] + hcols[0:8]
    dt = jnp.maximum(raw, 0.0) + jnp.log1p(jnp.exp(-jnp.abs(raw)))
    sig = 1.0 / (1.0 + jnp.exp(-raw))
    cum = running_sum(dt * hcols[8:16], upto[...])
    rows_o[0:8] = dt
    rows_o[8:16] = sig
    rows_o[16:24] = cum
    lead = blk.lead(cum)
    tail = blk.tail_base(cum) * dt
    cols = to_columns([tail])
    tail_lanes = by_head([column(cols, 0, h) for h in range(HEADS_DEV)])
    packed = (act[:, :WIDE].astype(F32) * tail_lanes).astype(BF16)
    fresh = tn(act[:, WIDE : WIDE + STATE], packed)
    last = last_by_lane(lead)
    state_o[0, 0:STATE] = state[...]
    state_o[0, STATE : STATE + 8] = decay[...]
    state[...] = last * state[...] + fresh
    decay[...] = last * decay[...]

    @at.when_last
    def _():
        device_o[...] = message(state[...], decay[...])


def intra_kernel(at, marks, normed, cot, weights, xbc, rows, lanes, z_o, e_o, yi_o):
    blk = Block(marks, at.index)
    z_o[...] = nn(normed[...], weights[:, 0:WIDE]).astype(BF16)
    e_o[...] = nn(cot[...], weights[:, WIDE : 2 * WIDE]).astype(BF16)
    dt = rows[0:8]
    cum = rows[16:24]
    x = xbc[:, :WIDE].astype(F32)
    scores = nt(xbc[:, WIDE + STATE :], xbc[:, WIDE : WIDE + STATE])
    allowed = blk.allowed()
    cols = to_columns([cum])
    out = lanes[1:2] * x
    for h in range(HEADS_DEV):
        decays = decay_of(allowed, column(cols, 0, h), cum[h : h + 1])
        mix = (scores * decays * dt[h : h + 1]).astype(BF16)
        out = out + nn(mix, of_head(x, h).astype(BF16))
    yi_o[...] = out.astype(BF16)


def gated_kernel(
    at, marks, yi, z, e, xbc, rows, states, one, two, three, lanes, weights,
    y_o, mixed_o, part_o, sums_o, prefix,
):
    @at.when_first
    def _():
        prefix[...] = carried((one, two, three))

    blk = Block(marks, at.index)
    lead = blk.lead(rows[16:24])
    cols = to_columns([lead])
    lead_lanes = by_head([column(cols, 0, h) for h in range(HEADS_DEV)])
    entering = states[0, 0:STATE] + states[0, STATE : STATE + 1] * prefix[...]
    y = yi[...].astype(F32) + lead_lanes * nn(xbc[:, WIDE + STATE :], entering.astype(BF16))
    y_o[...] = y.astype(BF16)
    gate, _ = silu_parts(z[...].astype(F32))
    v = y * gate
    mixed = (v * lanes[0:1]).astype(BF16)
    mixed_o[...] = mixed
    part_o[...] = nt(mixed, weights[:, WIDE : 2 * WIDE]).astype(BF16)
    row = iota((16, 2 * WIDE), 0)
    lane = iota((16, 2 * WIDE), 1)
    pick = jnp.where(((row == 0) & (lane < WIDE)) | ((row == 1) & (lane >= WIDE)), 1.0, 0.0)
    both = jnp.concatenate([v * v, e[...].astype(F32) * mixed.astype(F32)], axis=1)
    sums_o[...] = nt(pick.astype(BF16), both.astype(BF16))[0:2]


def gate_back_kernel(
    at, marks, y, z, e, xbc, rows, sums, lanes,
    dy_o, dz_o, reach_o, device_o, gains_o,
    carry, decay,
):
    blk = Block(marks, at.index)

    @at.when_last
    def _():
        carry[...] = jnp.zeros_like(carry)
        decay[...] = jnp.ones_like(decay)
        gains_o[...] = jnp.zeros_like(gains_o)

    lead = blk.lead(rows[16:24])
    root = lax.rsqrt(sums[0:1] / INNER + EPSILON)
    coef = sums[1:2] * root * root * root / INNER
    cols = to_columns([lead, jnp.broadcast_to(root, (8, BLOCK)), jnp.broadcast_to(coef, (8, BLOCK))])
    lead_lanes = by_head([column(cols, 0, h) for h in range(HEADS_DEV)])
    gate, slope = silu_parts(z[...].astype(F32))
    y_v = y[...].astype(F32)
    v = y_v * gate
    dm = column(cols, 1, 0) * e[...].astype(F32)
    dv = lanes[0:1] * dm - column(cols, 2, 0) * v
    dy = dv * gate
    dy_o[...] = dy.astype(BF16)
    dz_o[...] = (dv * y_v * slope).astype(BF16)
    x = xbc[:, :WIDE].astype(F32)
    gains_o[0:1] += jnp.sum(v * dm, axis=0, keepdims=True)
    gains_o[1:2] += jnp.sum(dy * x, axis=0, keepdims=True)
    reach = tn(xbc[:, WIDE + STATE :], (dy * lead_lanes).astype(BF16))
    last = last_by_lane(lead)
    reach_o[0, 0:STATE] = carry[...]
    reach_o[0, STATE : STATE + 8] = decay[...]
    carry[...] = last * carry[...] + reach
    decay[...] = last * decay[...]

    @at.when_first
    def _():
        device_o[...] = message(carry[...], decay[...])


def intra_back_kernel(
    at, marks, dy_r, xbc, rows, states, prefix, sums, mixed, cot, lanes,
    dxi_o, dbc_o, stats_o, grad_out_o,
):
    blk = Block(marks, at.index)

    @at.when_first
    def _():
        grad_out_o[...] = jnp.zeros_like(grad_out_o)

    dt = rows[0:8]
    cum = rows[16:24]
    lead = blk.lead(cum)
    root = lax.rsqrt(sums[0:1] / INNER + EPSILON)
    cols = to_columns([cum, lead, jnp.broadcast_to(root, (8, BLOCK))])
    lead_lanes = by_head([column(cols, 1, h) for h in range(HEADS_DEV)])
    rooted = (mixed[...].astype(F32) * column(cols, 2, 0)).astype(BF16)
    grad_out_o[...] += tn(cot[...], rooted)

    dy = dy_r[...].astype(F32)
    x_low = xbc[:, :WIDE]
    b_low = xbc[:, WIDE : WIDE + STATE]
    c_low = xbc[:, WIDE + STATE :]
    entering = states[0, 0:STATE] + states[0, STATE : STATE + 1] * prefix[...]
    held = entering.astype(BF16)
    masks = head_masks().astype(BF16)
    cross = nn(c_low, held)
    lead_grad = nt(masks, (dy * cross).astype(BF16))
    dc = nt((dy * lead_lanes).astype(BF16), held)
    scores = nt(c_low, b_low)
    allowed = blk.allowed()
    ds = jnp.zeros((BLOCK, BLOCK), F32)
    dx = lanes[1:2] * dy
    lane = iota((1, 128), 1)
    row8 = iota((8, 1), 0)
    row_sums = jnp.zeros((BLOCK, 128), F32)
    time_grad = jnp.zeros((8, BLOCK), F32)
    for h in range(HEADS_DEV):
        dt_h = dt[h : h + 1]
        dy_h = of_head(dy, h).astype(BF16)
        decays = decay_of(allowed, column(cols, 0, h), cum[h : h + 1])
        weighted = nt(dy_h, x_low) * decays
        ds = ds + weighted * dt_h
        scored = weighted * scores
        time_grad = time_grad + jnp.where(
            row8 == h, jnp.sum(scored, axis=0, keepdims=True), 0.0
        )
        row_sums = row_sums + jnp.where(
            lane == h, jnp.sum(scored * dt_h, axis=1, keepdims=True), 0.0
        )
        mix = (scores * decays * dt_h).astype(BF16)
        dx = dx + tn(mix, dy_h)
    ds_low = ds.astype(BF16)
    dxi_o[...] = dx.astype(BF16)
    dbc_o[:, 0:STATE] = tn(ds_low, c_low).astype(BF16)
    dbc_o[:, STATE : 2 * STATE] = (dc + nn(ds_low, b_low)).astype(BF16)
    stats_o[0:8] = time_grad
    stats_o[8:16] = row_sums.T[0:8] - time_grad * dt + lead_grad * lead


def input_back_kernel(
    at, marks, normed, halo, dz, dxi, dbc, xbc, slope, cin, cin_halo,
    rows, stats, states, prefix, reaches, one, two, three, gain, later, weights, taps, hcols,
    grad_out_t, gains,
    dn_o, early_o, late_o, pack_o, spill_o,
    ahead, suffix, since, wgrad, chan, steps, norm, low, wide,
):
    blk = Block(marks, at.index)

    @at.when_last
    def _():
        suffix[...] = carried((one, two, three))
        square = (BLOCK, BLOCK)
        since[...] = jnp.where(iota(square, 0) >= iota(square, 1), 1.0, 0.0).astype(BF16)
        wide[:, 0:WIDE] = later[:, 0:WIDE]
        wide[:, WIDE : 3 * WIDE] = weights[...]
        wgrad[...] = jnp.zeros_like(wgrad)
        chan[...] = jnp.zeros_like(chan)
        steps[...] = jnp.zeros_like(steps)
        norm[...] = jnp.zeros_like(norm)
        ahead[BLOCK : BLOCK + 8] = jnp.zeros((8, CHAN), F32)

    dt = rows[0:8]
    sig = rows[8:16]
    cum = rows[16:24]
    rate = hcols[8:16]
    lead = blk.lead(cum)
    tail_base = blk.tail_base(cum)
    tail = tail_base * dt
    cols = to_columns([tail])
    tail_lanes = by_head([column(cols, 0, h) for h in range(HEADS_DEV)])
    entering = states[0, 0:STATE] + states[0, STATE : STATE + 1] * prefix[...]
    leaving = reaches[0, 0:STATE] + reaches[0, STATE : STATE + 1] * suffix[...]
    leaving_low = leaving.astype(BF16)
    x = xbc[:, :WIDE].astype(F32)
    dpacked = nn(xbc[:, WIDE : WIDE + STATE], leaving_low)
    packed = (x * tail_lanes).astype(BF16)
    masks = head_masks()
    tail_grad = nt(masks.astype(BF16), (dpacked * x).astype(BF16))
    dx = dxi[...].astype(F32) + dpacked * tail_lanes
    db = dbc[:, 0:STATE].astype(F32) + nt(packed, leaving_low)
    dc = dbc[:, STATE : 2 * STATE].astype(F32)

    tail_term = tail_grad * tail
    state_term = jnp.sum(leaving * entering, axis=0, keepdims=True)
    last_term = jnp.sum(tail_term, axis=1, keepdims=True) + (
        jnp.sum(masks * state_term, axis=1, keepdims=True) * lead[:, BLOCK - 1 : BLOCK]
    )
    dcum = stats[8:16] - tail_term + jnp.where(iota((8, BLOCK), 1) == BLOCK - 1, last_term, 0.0)
    dla = running_sum(dcum, since[...])
    ddt = stats[0:8] + tail_grad * tail_base + dla * rate
    dstep = jnp.where(iota((8, 1), 0) < HEADS_DEV, ddt * sig, 0.0)
    steps[0:8] += dstep
    steps[8:16] += dla * dt * rate
    placed = jnp.concatenate(
        [jnp.zeros((64, BLOCK), F32), dstep, jnp.zeros((56, BLOCK), F32)], axis=0
    ).T

    dpre = jnp.concatenate([dx, db, dc], axis=1) * slope[...].astype(F32)
    inputs = cin[...].astype(F32)
    ahead[0:BLOCK] = dpre
    chan[4:5] += jnp.sum(dpre, axis=0, keepdims=True)
    chan[3:4] += jnp.sum(dpre * inputs, axis=0, keepdims=True)
    din = taps[3:4] * dpre
    left = blk.until_end()
    for lag in range(1, CONV):
        tap = 3 - lag
        later_dpre = jnp.where(left > lag, ahead[lag : lag + BLOCK], 0.0)
        chan[tap : tap + 1] += jnp.sum(later_dpre * inputs, axis=0, keepdims=True)
        din = din + taps[tap : tap + 1] * later_dpre
    ahead[BLOCK : BLOCK + 8] = dpre[0:8]
    mine = pl.ds(at.part * BLOCK, BLOCK)
    low[mine, 0:WIDE] = dz[...]
    low[mine, WIDE : WIDE + 128] = din[:, 0:128].astype(BF16)
    low[mine, WIDE + 128 : 2 * WIDE] = (din[:, 128:256] + placed).astype(BF16)
    low[mine, 2 * WIDE :] = din[:, WIDE:].astype(BF16)

    if at.part > 0:
        return

    all_low = low[...]
    normed_all = normed[...]
    dn = nt(all_low, wide[...])
    wgrad[...] += tn(normed_all, all_low)
    norm[0:1] += jnp.sum(dn * normed_all.astype(F32), axis=0, keepdims=True)
    dn_o[...] = dn.astype(BF16)

    @at.when_first
    def _():
        ahead[0:8] = jnp.zeros((8, CHAN), F32)
        ahead[8:16] = ahead[BLOCK : BLOCK + 8]
        ahead[16:24] = jnp.zeros((8, CHAN), F32)
        pos = blk.start - 8 + iota((8, 1), 0)
        left = end_of(marks, pos) - pos
        back = jnp.zeros((8, CHAN), F32)
        for lag in range(1, CONV):
            tap = 3 - lag
            same = (left > lag) & (pos >= 0)
            later_dpre = jnp.where(same, ahead[lag : lag + 8], 0.0)
            chan[tap : tap + 1] += jnp.sum(later_dpre * cin_halo[...], axis=0, keepdims=True)
            back = back + taps[tap : tap + 1] * later_dpre
        spilled = jnp.concatenate([jnp.zeros((8, CHAN), F32), back], axis=0).astype(BF16)
        given = nt(spilled, wide[:, WIDE:])
        spill_o[...] = given[8:16]
        rows_in = halo[...].astype(F32)
        scale = lax.rsqrt(jnp.mean(rows_in * rows_in, axis=1, keepdims=True) + EPSILON)
        normed_halo = (rows_in * scale * gain[0:1]).astype(BF16)
        norm[0:1] += jnp.sum(given * normed_halo.astype(F32), axis=0, keepdims=True)
        wgrad[:, WIDE:] += tn(normed_halo, spilled)
        early_o[...] = wgrad[:, WIDE:].astype(BF16)
        late_o[...] = jnp.concatenate(
            [wgrad[:, 0:INNER_DEV], grad_out_t[:, 0:INNER_DEV]], axis=1
        ).astype(BF16)
        gained = norm[0:1] / gain[0:1]

        def beside(left, right):
            return jnp.concatenate([left, right], axis=1)

        pack = jnp.concatenate(
            [
                chan[0:5],
                gained[:, 0:CHAN],
                beside(gained[:, CHAN:], gains[0:1]),
                beside(gains[1:2], steps[8:9]),
                beside(steps[9:10], steps[10:11]),
                beside(steps[0:1], steps[1:2]),
                beside(steps[2:3], jnp.zeros((1, WIDE), F32)),
                jnp.zeros((5, CHAN), F32),
            ],
            axis=0,
        )
        pack_o[...] = pack.astype(BF16)


def copied_kernel(source, out):
    out[...] = source[...]


def copied(values):
    rows, width = values.shape
    block = pl.BlockSpec((rows // 4, width), lambda s: (s, 0))
    return pl.pallas_call(
        copied_kernel,
        grid=(4,),
        in_specs=[block],
        out_specs=block,
        out_shape=jax.ShapeDtypeStruct(values.shape, values.dtype),
        compiler_params=pltpu.CompilerParams(
            dimension_semantics=("arbitrary",), vmem_limit_bytes=VMEM_LIMIT
        ),
        cost_estimate=pl.CostEstimate(flops=int(3e9), bytes_accessed=int(6e6), transcendentals=0),
    )(values)


def finish_kernel(dn, hidden, cot, gain, out):
    rows = hidden[...].astype(F32)
    scale = lax.rsqrt(jnp.mean(rows * rows, axis=1, keepdims=True) + EPSILON)
    unit = rows * scale
    scaled = dn[...].astype(F32) * gain[0:1]
    across = jnp.mean(scaled * unit, axis=1, keepdims=True)
    out[...] = (cot[...].astype(F32) + scale * (scaled - unit * across)).astype(BF16)


def finished(dn, hidden, cot, gain):
    rows, width = dn.shape
    block = pl.BlockSpec((rows // 2, width), lambda s: (s, 0))
    return pl.pallas_call(
        finish_kernel,
        grid=(2,),
        in_specs=[block, block, block, pl.BlockSpec((8, width), lambda s: (0, 0))],
        out_specs=block,
        out_shape=jax.ShapeDtypeStruct(dn.shape, BF16),
        compiler_params=pltpu.CompilerParams(
            dimension_semantics=("arbitrary",), vmem_limit_bytes=VMEM_LIMIT
        ),
        cost_estimate=pl.CostEstimate(flops=int(2e9), bytes_accessed=int(2e6), transcendentals=0),
    )(dn, hidden, cot, gain)


def passed_along(values, axis, by):
    count = lax.axis_size(axis)
    pairs = [(i, i + by) for i in range(count) if 0 <= i + by < count]
    return lax.ppermute(values, axis, pairs)


def handed_to_all(values, axis):
    count = lax.axis_size(axis)
    return lax.all_to_all(
        jnp.broadcast_to(values[None], (count,) + values.shape), axis, 0, 0, tiled=False
    )


def sent_along(device, sign):
    return [passed_along(device, "context", sign * k) for k in (1, 2, 3)]


def padded(values, width):
    extra = width - values.shape[-1]
    return jnp.pad(values, [(0, 0)] * (values.ndim - 1) + [(0, extra)])


def body(
    hidden, cotangent, lengths, norm_gain, gate_proj, value_proj, state_proj, step_proj,
    conv_value, conv_state, value_bias, state_bias, step_bias, decay_log, skip_gain,
    mixer_gain, out_proj,
):
    tok = hidden.shape[0]
    blocks = tok // BLOCK
    ctx = lax.axis_index("context")
    rank = lax.axis_index("tensor")

    own_rows = state_proj.shape[0]
    first = jnp.concatenate(
        [state_proj.astype(F32), conv_state, state_bias[None], jnp.zeros((3, state_proj.shape[1]), F32)],
        axis=0,
    )
    first = handed_to_all(first, "tensor")
    first, lengths, gate_proj, out_proj, edge = lax.optimization_barrier(
        (first, lengths, gate_proj, out_proj, hidden[tok - 16 :])
    )
    first = first.transpose(1, 0, 2).reshape(own_rows + 8, 2 * STATE)
    conv_shared = first[own_rows : own_rows + 5]
    needed = jnp.concatenate(
        [
            value_proj, step_proj, jnp.zeros((own_rows, 61), BF16), first[:own_rows].astype(BF16),
        ],
        axis=1,
    )
    needed = handed_to_all(needed, CELLS).reshape(MODEL, 2 * WIDE)
    finishes = jnp.cumsum(lengths[0])
    marks = jnp.concatenate(
        [finishes, jnp.stack([ctx * tok, 0 * ctx, 0 * ctx, 0 * ctx])]
    )
    marks = marks.astype(jnp.int32)
    later = jnp.concatenate([padded(gate_proj, WIDE), padded(out_proj.T, WIDE)], axis=1)
    later = handed_to_all(later, CELLS)
    halo = passed_along(edge, "context", 1)

    pair = whole((MODEL, 2 * WIDE))
    normed, xbc, slope, cin, cin_halo, rows, states, device, gain, taps, lanes, hcols = call(
        project_kernel, blocks, PARTS[0], False,
        [
            SMEM, SMEM, SMEM, SMEM, rows_of(MODEL), whole((16, MODEL)), whole((MODEL,)), pair,
            whole((4, INNER_DEV)), whole((INNER_DEV,)), whole((INNER_DEV,)), whole((5, 2 * STATE)),
        ],
        [
            (rows_of(MODEL), BF16), (rows_of(CHAN), BF16), (rows_of(CHAN), BF16),
            (rows_of(CHAN), BF16), (whole((8, CHAN)), F32), (lanes_of(24), F32), (STATES, F32),
            (whole(STATE_DIMS), F32), (whole((8, MODEL)), F32), (whole((8, CHAN)), F32),
            (whole((8, WIDE)), F32), (whole((16, BLOCK)), F32),
        ],
        [
            pltpu.VMEM((BLOCK + 8, CHAN), F32), pltpu.VMEM((STATE, WIDE), F32),
            pltpu.VMEM((8, WIDE), F32), pltpu.VMEM((BLOCK, BLOCK), BF16),
        ],
        14, marks, step_bias, decay_log, skip_gain, hidden, halo, norm_gain, needed, conv_value,
        value_bias, mixer_gain, conv_shared,
    )
    messages = sent_along(device, 1)
    later, xbc = lax.optimization_barrier((later, xbc))
    later = later.reshape(MODEL, 2 * WIDE)
    z, e, yi = call(
        intra_kernel, blocks, PARTS[1], False,
        [
            SMEM, rows_of(MODEL), rows_of(MODEL), pair, rows_of(CHAN), lanes_of(24),
            whole((8, WIDE)),
        ],
        [(rows_of(WIDE), BF16)] * 3,
        [], 12, marks, normed, cotangent, later, xbc, rows, lanes,
    )
    y, mixed, part, sums, prefix = call(
        gated_kernel, blocks, PARTS[2], False,
        [
            SMEM, rows_of(WIDE), rows_of(WIDE), rows_of(WIDE), rows_of(CHAN), lanes_of(24), STATES,
            whole(STATE_DIMS), whole(STATE_DIMS), whole(STATE_DIMS), whole((8, WIDE)), pair,
        ],
        [
            (rows_of(WIDE), BF16), (rows_of(WIDE), BF16), (rows_of(MODEL), BF16),
            (lanes_of(2), F32), (whole((STATE, WIDE)), F32),
        ],
        [], 10, marks, yi, z, e, xbc, rows, states, *messages, lanes, later,
    )
    sums = jnp.sum(handed_to_all(sums, "tensor"), axis=0)

    ranks = lax.axis_size("tensor")
    own = tok // ranks
    place = rank * own
    own_hidden = lax.dynamic_slice_in_dim(hidden, place, own, 0).astype(F32)
    own_root = lax.rsqrt(lax.dynamic_slice_in_dim(sums[0], place, own, 0) / INNER + EPSILON)
    projected = lax.psum_scatter(part, "tensor", scatter_dimension=0, tiled=True).astype(F32)
    own_out = (own_hidden + own_root[:, None] * projected).astype(BF16)

    dy, dz, reaches, back_device, gains = call(
        gate_back_kernel, blocks, PARTS[3], True,
        [
            SMEM, rows_of(WIDE), rows_of(WIDE), rows_of(WIDE), rows_of(CHAN), lanes_of(24),
            lanes_of(2), whole((8, WIDE)),
        ],
        [
            (rows_of(WIDE), BF16), (rows_of(WIDE), BF16), (STATES, F32), (whole(STATE_DIMS), F32),
            (whole((8, WIDE)), F32),
        ],
        [pltpu.VMEM((STATE, WIDE), F32), pltpu.VMEM((8, WIDE), F32)],
        9, marks, y, z, e, xbc, rows, sums, lanes,
    )
    messages = sent_along(back_device, -1)
    dxi, dbc, stats, grad_out_t = call(
        intra_back_kernel, blocks, PARTS[4], False,
        [
            SMEM, rows_of(WIDE), rows_of(CHAN), lanes_of(24), STATES, whole((STATE, WIDE)),
            lanes_of(2), rows_of(WIDE), rows_of(MODEL), whole((8, WIDE)),
        ],
        [
            (rows_of(WIDE), BF16), (rows_of(WIDE), BF16), (lanes_of(16), F32),
            (whole((MODEL, WIDE)), F32),
        ],
        [], 13, marks, dy, xbc, rows, states, prefix, sums, mixed, cotangent, lanes,
    )
    dxi, own_out, messages = lax.optimization_barrier((dxi, own_out, messages))
    output = lax.all_gather(own_out, "tensor", axis=0, tiled=True)
    dn, early, late, pack, spill = call(
        input_back_kernel, blocks, PARTS[5], True,
        [
            SMEM, ("tile", MODEL), whole((16, MODEL)), rows_of(WIDE), rows_of(WIDE),
            rows_of(WIDE), rows_of(CHAN), rows_of(CHAN), rows_of(CHAN),
            whole((8, CHAN)), lanes_of(24), lanes_of(16), STATES, whole((STATE, WIDE)), STATES,
            whole(STATE_DIMS), whole(STATE_DIMS), whole(STATE_DIMS), whole((8, MODEL)), pair, pair,
            whole((8, CHAN)), whole((16, BLOCK)), whole((MODEL, WIDE)), whole((8, WIDE)),
        ],
        [
            (("tile", MODEL), BF16), (whole((MODEL, CHAN)), BF16),
            (whole((MODEL, 2 * INNER_DEV)), BF16), (whole((16, CHAN)), BF16),
            (whole((8, MODEL)), F32),
        ],
        [
            pltpu.VMEM((BLOCK + 8, CHAN), F32), pltpu.VMEM((STATE, WIDE), F32),
            pltpu.VMEM((BLOCK, BLOCK), BF16), pltpu.VMEM((MODEL, 3 * WIDE), F32),
            pltpu.VMEM((8, CHAN), F32), pltpu.VMEM((16, BLOCK), F32), pltpu.VMEM((8, MODEL), F32),
            pltpu.VMEM((PARTS[5] * BLOCK, 3 * WIDE), BF16), pltpu.VMEM((MODEL, 3 * WIDE), BF16),
        ],
        22, marks, normed, halo, dz, dxi, dbc, xbc, slope, cin, cin_halo,
        rows, stats, states, prefix, reaches, *messages, gain, later, needed, taps, hcols,
        grad_out_t, gains,
    )

    arrived = passed_along(spill, "context", -1)
    end = dn[tok - 8 :].astype(F32) + arrived
    dn = lax.dynamic_update_slice(dn, end.astype(BF16), (tok - 8, 0))
    dn, output, hidden_late, cot_late = lax.optimization_barrier((dn, output, hidden, cotangent))
    own_dn = lax.psum_scatter(dn, "tensor", scatter_dimension=0, tiled=True)

    cells = lax.axis_size("shard") * lax.axis_size("context")
    early = jnp.concatenate(
        [
            early.reshape(cells, own_rows, CHAN),
            jnp.broadcast_to(pack[None], (cells,) + pack.shape),
        ],
        axis=1,
    )
    early = lax.all_to_all(early, CELLS, 0, 0, tiled=False)
    output = copied(output)
    own_rows_in = lax.dynamic_slice_in_dim(hidden_late, place, own, 0)
    own_cot = lax.dynamic_slice_in_dim(cot_late, place, own, 0)
    own_dn, early, output, own_rows_in, own_cot = lax.optimization_barrier(
        (own_dn, early, output, own_rows_in, own_cot)
    )
    early = jnp.sum(early.astype(F32), axis=0)
    own_grad = finished(own_dn, own_rows_in, own_cot, gain)
    own_grad, late = lax.optimization_barrier((own_grad, late))
    grad_hidden = lax.all_gather(own_grad, "tensor", axis=0, tiled=True)
    late = lax.all_to_all(late.reshape(cells, own_rows, 2 * INNER_DEV), CELLS, 0, 0, tiled=False)
    late = jnp.sum(late.astype(F32), axis=0)

    big, small = early[:own_rows], early[own_rows:]
    chan = small[:5]
    norm_cells = jnp.concatenate([small[5], small[6, :WIDE]])
    grad_mixer = small[6, WIDE : WIDE + INNER_DEV]
    grad_skip = jnp.sum(small[7, :INNER_DEV].reshape(HEADS_DEV, HEADDIM), axis=1)
    lines = jnp.sum(small[7:11].reshape(8, WIDE), axis=1)
    grad_decay = lines[1:4]
    grad_step_bias = lines[4:7]
    share = 2 * STATE // lax.axis_size("tensor")
    shared = jnp.concatenate([big[:, WIDE:], chan[:, WIDE:]], axis=0)
    shared = shared.reshape(own_rows + 5, -1, share).transpose(1, 0, 2)
    shared = shared.reshape(shared.shape[0], -1)
    count = shared.shape[1]
    final = jnp.concatenate(
        [shared, jnp.broadcast_to(norm_cells[None], (shared.shape[0], MODEL))], axis=1
    )
    final = padded(final, 2560).reshape(-1, 20, 128)
    final = jnp.sum(lax.all_to_all(final, "tensor", 0, 0, tiled=False), axis=0).reshape(-1)
    state_all = final[:count].reshape(own_rows + 5, share)
    return (
        output,
        grad_hidden,
        final[count : count + MODEL],
        late[:, :INNER_DEV],
        big[:, :INNER_DEV],
        state_all[:own_rows],
        big[:, INNER_DEV : INNER_DEV + HEADS_DEV],
        chan[:4, :INNER_DEV],
        state_all[own_rows : own_rows + 4],
        chan[4, :INNER_DEV],
        state_all[own_rows + 4],
        grad_step_bias,
        grad_decay,
        grad_skip,
        grad_mixer,
        late[:, INNER_DEV:].T,
    )


def solution(mesh):
    cells = P(CELLS, None)
    split = P(CELLS, "tensor")
    return jax.shard_map(
        body,
        mesh=mesh,
        in_specs=(
            cells, cells, P("shard", None), P(), split, split, split, split, P(None, "tensor"),
            P(None, "tensor"), P("tensor"), P("tensor"), P("tensor"), P("tensor"), P("tensor"),
            P("tensor"), P("tensor", CELLS),
        ),
        out_specs=(
            cells, cells, P(), split, split, split, split, P(None, "tensor"), P(None, "tensor"),
            P("tensor"), P("tensor"), P("tensor"), P("tensor"), P("tensor"), P("tensor"),
            P("tensor", CELLS),
        ),
        check_vma=False,
    )
```
